32 devices in a mesh: blk: 16 (over z, x, core), red: 2 (over y).
Axes of the slice: x: 2, y: 2, z: 4, core: 2. Of those that a mesh axis runs over, the one named last changes fastest.
Arguments:
- amplitudes: float32 [4096, 1536], P('blk', 'red'), may hold values from -6 to 6
- integrals: float32 [4096, 1536], P('blk', 'red'), may hold values from -0.4375 to 0.4375
- cd_irrep: int32 [2, 768], P('red'), may hold values from 0 to 7, never falling along the last dimension, each value on 1 to 192 neighbouring positions
- ab_irrep: int32 [16, 256], P('blk'), may hold values from 0 to 7, never falling along the last dimension, each value on 1 to 64 neighbouring positions
- ij_irrep: int32 [16, 256], P('blk'), may hold values from 0 to 7, never falling along the last dimension, each value on 1 to 64 neighbouring positions
Outputs:
- ladder: float32 [4, 4096, 256], P(None, ('blk', 'red'))
The draws below stay inside these ranges and needn't reach their ends.
Inputs may be any that keep to these rules, and one draw needn't show every extreme that they name: `cd_irrep`: each row's labels never fall, every irrep 0 to 7 occurs in every row, and each irrep holds at most 192 positions of a row, exactly that many for some irrep. `ab_irrep`: each row's labels never fall, every irrep 0 to 7 occurs in every row, and each irrep holds at most 64 positions of a row, exactly that many for some irrep. `ij_irrep`: each row's labels never fall, every irrep 0 to 7 occurs in every row, and each irrep holds at most 64 positions of a row, exactly that many for some irrep.
All inputs are finite; a program needn't handle non-finite values.
Results may differ from the reference program's by a relative error of at most 0.0003.
Values sent between devices are 32-bit elements; how exact they have to be, the bound alone decides.
No kernel may reach another device: no remote copies, remote signals or barrier semaphores. Data moves between devices by JAX's collectives and lax.ppermute only.
A program may use at most 64 MiB of HBM per device.

```python
import math
import jax
import jax.numpy as jnp
import numpy as np
from jax import lax

AB_ROWS = 256
OCC_PAIRS = 256
CD_DEV = 768
SHIFTS = 4
ROW_BLOCKS = 16
CD_PARTS = 2
CD = 1536


def shard_levels(stream_key, dims, cuts, least, top_value):
    def one(dim, shards_of):
        steps = jax.random.uniform(jax.random.fold_in(jax.random.fold_in(stream_key, 6), dim), (shards_of,), jnp.float32, least / len(cuts), top_value / len(cuts))
        return jnp.repeat(jnp.exp(steps), dims[dim] // shards_of).reshape((-1,) + (1,) * (len(dims) - dim - 1))

    factor_of = one(*cuts[0])
    for cut in cuts[1:]:
        factor_of = factor_of * one(*cut)
    return factor_of


def split_up(number_of, total, bound, lean):
    portions = [(1 << 20) // math.isqrt(rank ** lean) + 1 for rank in range(2, number_of + 1)]
    spare, counts = total - bound - (number_of - 1), [1] * (number_of - 1)
    while spare > 0:
        candidates = [i for i in range(number_of - 1) if counts[i] < bound]
        whole, left = sum([portions[i] for i in candidates]), spare
        for i in candidates:
            addition = min(bound - counts[i], max(1, left * portions[i] // whole), spare)
            counts[i] = counts[i] + addition
            spare = spare - addition
    return np.array([bound] + counts)


def ragged_sizes(key, number_of, total, bound, skew):
    if number_of == 2:
        one = jax.random.randint(key, (), max(1, total - bound), min(bound, total - 1) + 1)
        return jnp.stack([one, total - one])
    sizes = jnp.asarray(split_up(number_of, total, bound, skew), jnp.int32)
    twos = (number_of - 1) // 2
    source_of, taker = sizes[1:1 + 2 * twos:2], sizes[2:2 + 2 * twos:2]
    margin = jnp.minimum(source_of - 1, bound - taker)
    shifted = jax.random.randint(jax.random.fold_in(key, 1), (twos,), 0, 1 << 20) % (margin + 1)
    sizes = sizes.at[1:1 + 2 * twos:2].set(source_of - shifted).at[2:2 + 2 * twos:2].set(taker + shifted)
    return sizes[jax.random.permutation(jax.random.fold_in(key, 2), number_of)]


def normal_values(rng, shape, spread, reach, pieces=(), kind=jnp.bfloat16):
    entries = spread * jax.random.normal(rng, shape, jnp.float32)
    if pieces:
        entries = entries * shard_levels(rng, shape, pieces, -0.22, 0.18)
    return jnp.clip(entries, -reach, reach).astype(kind)


def setup_inputs(seed: int = 0) -> dict:
    seeds = jax.random.split(jax.random.key(seed), 6)
    return {
        "amplitudes": normal_values(seeds[0], (ROW_BLOCKS * OCC_PAIRS, CD), 1.0, 6.0, ((0, 16), (1, 2)), jnp.float32),
        "integrals": normal_values(seeds[1], (ROW_BLOCKS * AB_ROWS, CD), (CD // 8) ** -0.5, 0.4375, ((0, 16), (1, 2)), jnp.float32),
        "cd_irrep": jax.vmap(lambda own: jnp.searchsorted(jnp.cumsum(ragged_sizes(own, 8, CD_DEV, CD_DEV // 4, 1)), jnp.arange(CD_DEV), side="right"))(jax.random.split(seeds[2], CD_PARTS)).reshape((CD_PARTS, CD_DEV)).astype(jnp.int32),
        "ab_irrep": jax.vmap(lambda own: jnp.searchsorted(jnp.cumsum(ragged_sizes(own, 8, AB_ROWS, AB_ROWS // 4, 1)), jnp.arange(AB_ROWS), side="right"))(jax.random.split(seeds[3], ROW_BLOCKS)).reshape((ROW_BLOCKS, AB_ROWS)).astype(jnp.int32),
        "ij_irrep": jax.vmap(lambda own: jnp.searchsorted(jnp.cumsum(ragged_sizes(own, 8, OCC_PAIRS, OCC_PAIRS // 4, 1)), jnp.arange(OCC_PAIRS), side="right"))(jax.random.split(seeds[4], ROW_BLOCKS)).reshape((ROW_BLOCKS, OCC_PAIRS)).astype(jnp.int32),
    }


def reference(amplitudes, integrals, cd_irrep, ab_irrep, ij_irrep):
    cd_labels = cd_irrep.reshape(-1)
    amp_blocks = amplitudes.reshape(ROW_BLOCKS, OCC_PAIRS, CD)
    row_blocks = integrals.reshape(ROW_BLOCKS, AB_ROWS, CD)

    def one_block(index):
        rows = lax.dynamic_index_in_dim(row_blocks, index, 0, keepdims=False)
        row_labels = lax.dynamic_index_in_dim(ab_irrep, index, 0, keepdims=False)
        results = []
        for shift in range(SHIFTS):
            source = ((index - shift) % ROW_BLOCKS).astype(jnp.int32)
            amp_slab = lax.dynamic_index_in_dim(amp_blocks, source, 0, keepdims=False)
            slab_labels = lax.dynamic_index_in_dim(ij_irrep, source, 0, keepdims=False)
            screened = jnp.where(slab_labels[:, None] == cd_labels[None, :], amp_slab, 0.0)
            product = lax.dot_general(rows, screened, (((1,), (1,)), ((), ())), precision=lax.Precision.HIGHEST, preferred_element_type=jnp.float32)
            results.append(jnp.where(row_labels[:, None] == slab_labels[None, :], product, 0.0))
        return jnp.stack(results, 0)

    result = lax.map(one_block, jnp.arange(ROW_BLOCKS, dtype=jnp.int32))
    return jnp.transpose(result, (1, 0, 2, 3)).reshape(SHIFTS, ROW_BLOCKS * AB_ROWS, OCC_PAIRS)
```

```python
import functools
import jax
import jax.numpy as jnp
from jax import lax
from jax.experimental import pallas as pl
from jax.experimental.pallas import tpu as pltpu
from jax.sharding import PartitionSpec as P

IRREPS = 8
LANES = 128
F32 = jnp.float32


def column(labels):
    return jnp.broadcast_to(labels.astype(F32), (LANES, labels.shape[1])).T


def fold(rows_ref, row_labels, cd_labels, width):
    total = None
    for start in range(0, rows_ref.shape[1], width):
        part = slice(start, start + width)
        kept = jnp.where(row_labels[:, :1] == cd_labels[:, part], rows_ref[:, part], 0.0)
        total = kept if total is None else total + kept
    return total


def pack_kernel(amp_ref, ij_ref, cd_ref, out_ref):
    width = out_ref.shape[0] - 8
    folded = fold(amp_ref, column(ij_ref[...]), cd_ref[...].astype(F32), width)
    out_ref[:width, :] = folded.T
    out_ref[width:, :] = jnp.broadcast_to(ij_ref[...].astype(F32), (8, out_ref.shape[1]))


def fold_rows_kernel(rows_ref, ab_ref, cd_ref, out_ref):
    out_ref[...] = fold(rows_ref, column(ab_ref[...]), cd_ref[...].astype(F32), out_ref.shape[1])


def product(rows, slab_ref, row_labels, narrow):
    width = rows.shape[1]
    full = jnp.dot(rows, slab_ref[:width, :], precision=lax.Precision.HIGHEST, preferred_element_type=F32)
    full = jnp.where(row_labels[:, :1] == slab_ref[width:width + 1, :], full, 0.0)
    total = None
    for start in range(0, full.shape[1], narrow):
        part = full[:, start:start + narrow]
        total = part if total is None else total + part
    return total


def terms_kernel(rows_ref, ab_ref, own_ref, two_ref, mix_ref, swap_ref, keep_ref, send_ref, labels_ref, all_ref):
    narrow = keep_ref.shape[1] // 4
    width = rows_ref.shape[1]
    odd = lax.rem(lax.axis_index("blk"), 2) == 1
    row_labels = column(ab_ref[...])
    rows = rows_ref[...]
    own, two, mix, swap = [product(rows, ref, row_labels, narrow) for ref in (own_ref, two_ref, mix_ref, swap_ref)]
    one = jnp.where(odd, mix, swap)
    three = jnp.where(odd, swap, mix)
    all_ref[...] = jnp.concatenate([own, one, two, three], axis=1)
    own, two, mix, swap = [ref[width:width + 1, :] for ref in (own_ref, two_ref, mix_ref, swap_ref)]
    labels_ref[...] = jnp.concatenate([own, jnp.where(odd, mix, swap), two, jnp.where(odd, swap, mix)] * 2, axis=0)
    parts = send_ref.shape[0] + 1
    mine = lax.axis_index("red")
    count = keep_ref.shape[0]
    keep_ref[...] = all_ref[pl.ds(pl.multiple_of(mine * count, count), count), :]
    for step in range(1, parts):
        peer = lax.rem(mine + step, parts)
        send_ref[step - 1] = all_ref[pl.ds(pl.multiple_of(peer * count, count), count), :]


def finish_kernel(parts, keep_ref, *refs):
    taken, (labels_ref, ab_ref, out_ref) = refs[:parts - 1], refs[parts - 1:]
    total = keep_ref[...]
    for ref in taken:
        total = total + ref[...]
    count = total.shape[0]
    narrow = total.shape[1] // 4
    rows = column(ab_ref[...])
    mine = lax.axis_index("red")
    own = rows[:count]
    for part in range(1, parts):
        own = jnp.where(mine == part, rows[part * count:(part + 1) * count], own)
    for m in range(4):
        wide = jnp.concatenate([total[:, m * narrow:(m + 1) * narrow]] * (out_ref.shape[2] // narrow), axis=1)
        out_ref[m] = jnp.where(own[:, :1] == labels_ref[m:m + 1, :], wide, 0.0)


def whole(shape, dtype=F32):
    return jax.ShapeDtypeStruct(shape, dtype)


def vmem(count):
    return [pl.BlockSpec(memory_space=pltpu.VMEM)] * count


def call(kernel, out_shape, args, flops, **more):
    outs = out_shape if isinstance(out_shape, list) else [out_shape]
    moved = sum(a.size * 4 for a in list(args) + outs)
    return pl.pallas_call(
        kernel,
        out_shape=out_shape,
        in_specs=vmem(len(args)),
        out_specs=vmem(len(outs)) if isinstance(out_shape, list) else vmem(1)[0],
        cost_estimate=pl.CostEstimate(flops=flops, bytes_accessed=moved, transcendentals=0),
        compiler_params=pltpu.CompilerParams(vmem_limit_bytes=32 * 1024 * 1024),
        **more,
    )(*args)


def body(amplitudes, integrals, cd_irrep, ab_irrep, ij_irrep):
    blocks, parts = lax.axis_size("blk"), lax.axis_size("red")
    pairs, depth = amplitudes.shape
    row_count = integrals.shape[0]
    width, narrow = depth // 4, pairs // 4
    count = row_count // parts

    two_on = [(i, (i + 2) % blocks) for i in range(blocks)]
    mixed = [(i, (i + 1 if i % 2 == 0 else i + 3) % blocks) for i in range(blocks)]
    cores = [(i, i ^ 1) for i in range(blocks)]

    own = call(pack_kernel, whole((width + 8, pairs)), (amplitudes, ij_irrep, cd_irrep), 4 * amplitudes.size)
    two = lax.ppermute(own, "blk", two_on)
    mix = lax.ppermute(own, "blk", mixed)
    rows = call(fold_rows_kernel, whole((row_count, width)), (integrals, ab_irrep, cd_irrep), 4 * integrals.size)
    swap = lax.ppermute(two, "blk", cores)
    keep, send, labels = call(
        terms_kernel,
        [whole((count, 4 * narrow)), whole((parts - 1, count, 4 * narrow)), whole((8, pairs))],
        (rows, ab_irrep, own, two, mix, swap),
        4 * 2 * row_count * width * pairs,
        scratch_shapes=[pltpu.VMEM((row_count, 4 * narrow), F32)],
    )
    taken = [
        lax.ppermute(send[step - 1], "red", [(i, (i + step) % parts) for i in range(parts)])
        for step in range(1, parts)
    ]
    return call(
        functools.partial(finish_kernel, parts),
        whole((4, count, pairs)),
        (keep, *taken, labels, ab_irrep),
        4 * 2 * count * pairs,
    )


def solution(mesh):
    in_specs = (P("blk", "red"), P("blk", "red"), P("red", None), P("blk", None), P("blk", None))
    out_specs = P(None, ("blk", "red"), None)
    return jax.shard_map(body, mesh=mesh, in_specs=in_specs, out_specs=out_specs, check_vma=False)
```

```python
import functools
import jax
import jax.numpy as jnp
from jax import lax
from jax.experimental import pallas as pl
from jax.experimental.pallas import tpu as pltpu
from jax.sharding import PartitionSpec as P

LANES = 128
F32 = jnp.float32
ONCHIP = pl.BlockSpec(memory_space=pltpu.VMEM)
OFFCHIP = pl.BlockSpec(memory_space=pltpu.HBM)


def column(labels):
    return jnp.broadcast_to(labels.astype(F32), (LANES, labels.shape[1])).T


def fold(rows, row_labels, cd_labels, width):
    total = None
    for start in range(0, rows.shape[1], width):
        part = slice(start, start + width)
        kept = jnp.where(row_labels[:, :1] == cd_labels[:, part], rows[:, part], 0.0)
        total = kept if total is None else total + kept
    return total


def fetch(pairs, sems):
    copies = [pltpu.make_async_copy(src, dst, sems.at[i]) for i, (src, dst) in enumerate(pairs)]
    for copy in copies:
        copy.start()
    return copies


def chunks(count):
    return [pl.ds(start, LANES) for start in range(0, count, LANES)]


def pack_kernel(amp_ref, ij_ref, cd_ref, out_ref, amp, ij, cd, sems):
    pairs, width = amp.shape[0], out_ref.shape[0] - 8
    parts = chunks(pairs)
    copies = fetch([(ij_ref, ij), (cd_ref, cd)] + [(amp_ref.at[c], amp.at[c]) for c in parts], sems)
    copies[0].wait()
    copies[1].wait()
    rows = column(ij[...])
    labels = cd[...].astype(F32)
    out_ref[width:, :] = jnp.broadcast_to(ij[...].astype(F32), (8, pairs))
    for copy, c in zip(copies[2:], parts):
        copy.wait()
        out_ref[:width, c] = fold(amp[c, :], rows[c.start:c.start + LANES], labels, width).T


def narrowed(rows, slab_ref, row_labels):
    width = rows.shape[1]
    full = jnp.dot(rows, slab_ref[:width, :], precision=lax.Precision.HIGHEST, preferred_element_type=F32)
    full = jnp.where(row_labels[:, :1] == slab_ref[width:width + 1, :], full, 0.0)
    narrow = full.shape[1] // 4
    return sum(full[:, k * narrow:(k + 1) * narrow] for k in range(1, 4)) + full[:, :narrow]


def first_kernel(v_ref, ab_ref, cd_ref, own_ref, rows_ref, column_ref, out_ref, v, ab, cd, sems):
    width = rows_ref.shape[1]
    parts = chunks(v.shape[0])
    copies = fetch([(ab_ref, ab), (cd_ref, cd)] + [(v_ref.at[c], v.at[c]) for c in parts], sems)
    copies[0].wait()
    copies[1].wait()
    column_ref[...] = column(ab[...])
    labels = cd[...].astype(F32)
    for copy, c in zip(copies[2:], parts):
        copy.wait()
        rows_ref[c, :] = fold(v[c, :], column_ref[c, :], labels, width)
    out_ref[...] = narrowed(rows_ref[...], own_ref, column_ref[...])


def middle_kernel(rows_ref, column_ref, two_ref, mix_ref, out_ref):
    narrow = out_ref.shape[1] // 2
    out_ref[:, :narrow] = narrowed(rows_ref[...], two_ref, column_ref[...])
    out_ref[:, narrow:] = narrowed(rows_ref[...], mix_ref, column_ref[...])


def last_kernel(rows_ref, column_ref, own_out, mid_out, own_ref, two_ref, mix_ref, late_ref, swap_ref, keep_ref, send_ref, labels_ref, all_ref):
    narrow = own_out.shape[1]
    width = rows_ref.shape[1]
    place = lax.rem(lax.axis_index("blk"), 4)
    odd = lax.rem(place, 2) == 1
    mix_term, mix_labels = mid_out[:, narrow:], mix_ref[width:width + 1, :]
    swap_term = narrowed(rows_ref[...], swap_ref, column_ref[...])
    swap_labels = swap_ref[width:width + 1, :]
    all_ref[...] = jnp.concatenate(
        [own_out[...], jnp.where(odd, mix_term, swap_term), mid_out[:, :narrow], jnp.where(odd, swap_term, mix_term)], axis=1)
    labels_ref[...] = jnp.concatenate(
        [own_ref[width:width + 1, :], jnp.where(odd, mix_labels, swap_labels), two_ref[width:width + 1, :],
         jnp.where(odd, swap_labels, mix_labels)] * 2, axis=0)

    @pl.when(place == 2)
    def _():
        all_ref[:, 3 * narrow:] = narrowed(rows_ref[...], late_ref, column_ref[...])
        labels_ref[3:4, :] = late_ref[width:width + 1, :]

    parts = send_ref.shape[0] + 1
    mine = lax.axis_index("red")
    count = keep_ref.shape[0]
    keep_ref[...] = all_ref[pl.ds(pl.multiple_of(mine * count, count), count), :]
    for step in range(1, parts):
        peer = lax.rem(mine + step, parts)
        send_ref[step - 1] = all_ref[pl.ds(pl.multiple_of(peer * count, count), count), :]


def finish_kernel(parts, keep_ref, *refs):
    taken, (labels_ref, column_ref, out_ref) = refs[:parts - 1], refs[parts - 1:]
    total = keep_ref[...]
    for ref in taken:
        total = total + ref[...]
    count = total.shape[0]
    narrow = total.shape[1] // 4
    mine = lax.axis_index("red")
    own = column_ref[pl.ds(pl.multiple_of(mine * count, count), count), :]
    for m in range(4):
        wide = jnp.concatenate([total[:, m * narrow:(m + 1) * narrow]] * (out_ref.shape[2] // narrow), axis=1)
        out_ref[m] = jnp.where(own[:, :1] == labels_ref[m:m + 1, :], wide, 0.0)


def whole(*shape):
    return jax.ShapeDtypeStruct(shape, F32)


def call(kernel, out_shape, args, flops, off=0, scratch=()):
    moved = sum(a.size * 4 for a in list(args) + out_shape)
    args = [pltpu.with_memory_space_constraint(a, pltpu.HBM) for a in args[:off]] + list(args[off:])
    return pl.pallas_call(
        kernel,
        out_shape=out_shape,
        in_specs=[OFFCHIP] * off + [ONCHIP] * (len(args) - off),
        out_specs=[ONCHIP] * len(out_shape),
        scratch_shapes=list(scratch),
        cost_estimate=pl.CostEstimate(flops=flops, bytes_accessed=moved, transcendentals=0),
        compiler_params=pltpu.CompilerParams(vmem_limit_bytes=32 * 1024 * 1024),
    )(*args)


def body(amplitudes, integrals, cd_irrep, ab_irrep, ij_irrep):
    blocks, parts = lax.axis_size("blk"), lax.axis_size("red")
    pairs, depth = amplitudes.shape
    row_count = integrals.shape[0]
    width, narrow = depth // 4, pairs // 4
    count = row_count // parts
    one_product = 12 * row_count * width * pairs

    def moved(array, steps):
        return lax.ppermute(array, "blk", [(i, (i + steps[i % 4]) % blocks) for i in range(blocks)])

    def staging(array, labels):
        return [
            pltpu.VMEM(array.shape, F32),
            pltpu.VMEM(labels.shape, jnp.int32),
            pltpu.VMEM(cd_irrep.shape, jnp.int32),
            pltpu.SemaphoreType.DMA((2 + array.shape[0] // LANES,)),
        ]

    own, = call(pack_kernel, [whole(width + 8, pairs)], (amplitudes, ij_irrep, cd_irrep),
                4 * amplitudes.size, 3, staging(amplitudes, ij_irrep))
    two = moved(own, (2, 2, 2, 2))
    mix = moved(own, (1, 3, 1, -1))
    rows, column_labels, own_term = call(
        first_kernel, [whole(row_count, width), whole(row_count, LANES), whole(row_count, narrow)],
        (integrals, ab_irrep, cd_irrep, own), 4 * integrals.size + one_product, 3, staging(integrals, ab_irrep))
    own_late, rows = lax.optimization_barrier((own, rows))
    late = moved(own_late, (1, -1, 1, 3))
    swap = moved(two, (1, -1, 1, -1))
    mid_term, = call(middle_kernel, [whole(row_count, 2 * narrow)], (rows, column_labels, two, mix), 2 * one_product)
    keep, send, labels = call(
        last_kernel,
        [whole(count, 4 * narrow), whole(parts - 1, count, 4 * narrow), whole(8, pairs)],
        (rows, column_labels, own_term, mid_term, own, two, mix, late, swap),
        2 * one_product, 0, [pltpu.VMEM((row_count, 4 * narrow), F32)])
    taken = [
        lax.ppermute(send[step - 1], "red", [(i, (i + step) % parts) for i in range(parts)])
        for step in range(1, parts)
    ]
    out, = call(functools.partial(finish_kernel, parts), [whole(4, count, pairs)],
                (keep, *taken, labels, column_labels), 4 * 2 * count * pairs)
    return out


def solution(mesh):
    in_specs = (P("blk", "red"), P("blk", "red"), P("red", None), P("blk", None), P("blk", None))
    out_specs = P(None, ("blk", "red"), None)
    return jax.shard_map(body, mesh=mesh, in_specs=in_specs, out_specs=out_specs, check_vma=False)
```

```python
import functools
import jax
import jax.numpy as jnp
from jax import lax
from jax.experimental import pallas as pl
from jax.experimental.pallas import tpu as pltpu
from jax.sharding import PartitionSpec as P

LANES = 128
F32 = jnp.float32
ONCHIP = pl.BlockSpec(memory_space=pltpu.VMEM)
OFFCHIP = pl.BlockSpec(memory_space=pltpu.HBM)


def column(labels):
    return jnp.broadcast_to(labels.astype(F32), (LANES, labels.shape[1])).T


def fold(rows, row_labels, cd_labels, width):
    total = None
    for start in range(0, rows.shape[1], width):
        part = slice(start, start + width)
        kept = jnp.where(row_labels[:, :1] == cd_labels[:, part], rows[:, part], 0.0)
        total = kept if total is None else total + kept
    return total


def fetch(pairs, sems):
    copies = [pltpu.make_async_copy(src, dst, sems.at[i]) for i, (src, dst) in enumerate(pairs)]
    for copy in copies:
        copy.start()
    return copies


def chunks(count):
    return [pl.ds(start, LANES) for start in range(0, count, LANES)]


def pack_kernel(amp_ref, ij_ref, cd_ref, out_ref, amp, ij, cd, sems):
    pairs, width = amp.shape[0], out_ref.shape[0] - 8
    parts = chunks(pairs)
    copies = fetch([(ij_ref, ij), (cd_ref, cd)] + [(amp_ref.at[c], amp.at[c]) for c in parts], sems)
    copies[0].wait()
    copies[1].wait()
    rows = column(ij[...])
    labels = cd[...].astype(F32)
    out_ref[width:, :] = jnp.broadcast_to(ij[...].astype(F32), (8, pairs))
    for copy, c in zip(copies[2:], parts):
        copy.wait()
        out_ref[:width, c] = fold(amp[c, :], rows[c.start:c.start + LANES], labels, width).T


def narrowed(rows, slab_ref, row_labels):
    width = rows.shape[1]
    full = jnp.dot(rows, slab_ref[:width, :], precision=lax.Precision.HIGHEST, preferred_element_type=F32)
    full = jnp.where(row_labels[:, :1] == slab_ref[width:width + 1, :], full, 0.0)
    narrow = full.shape[1] // 4
    return sum(full[:, k * narrow:(k + 1) * narrow] for k in range(1, 4)) + full[:, :narrow]


def halved(term):
    half = term.shape[0] // 2
    return jnp.concatenate([term[:half], term[half:]], axis=1)


def unhalved(term):
    half = term.shape[1] // 2
    return jnp.concatenate([term[:, :half], term[:, half:]], axis=0)


def first_kernel(v_ref, ab_ref, cd_ref, own_ref, rows_ref, column_ref, keep_ref, send_ref, v, ab, cd, labels, sems):
    width, count = rows_ref.shape[1], keep_ref.shape[0]
    parts = v.shape[0] // count
    mine = lax.axis_index("red")
    places = [pl.ds(pl.multiple_of(lax.rem(mine + k, parts) * count, count), count) for k in range(parts)]
    held = [pl.ds(k * count, count) for k in range(parts)]
    copies = fetch([(ab_ref, ab), (cd_ref, cd)] + [(v_ref.at[p], v.at[h]) for p, h in zip(places, held)], sems)
    copies[0].wait()
    copies[1].wait()
    labels[...] = column(ab[...])
    cd_labels = cd[...].astype(F32)
    for copy, p, h in zip(copies[2:], places, held):
        column_ref[h, :] = labels[p, :]
        copy.wait()
        rows_ref[h, :] = fold(v[h, :], column_ref[h, :], cd_labels, width)
    term = narrowed(rows_ref[...], own_ref, column_ref[...])
    keep_ref[...] = term[:count]
    for k in range(1, parts):
        send_ref[k - 1] = halved(term[k * count:(k + 1) * count])


def mix_kernel(rows_ref, column_ref, mix_ref, out_ref):
    out_ref[...] = narrowed(rows_ref[...], mix_ref, column_ref[...])


def two_kernel(rows_ref, column_ref, mix_term, two_ref, late_ref, keep_ref, send_ref, third):
    count, narrow = keep_ref.shape
    parts = send_ref.shape[0] + 1
    third[...] = mix_term[...]

    @pl.when(lax.rem(lax.axis_index("blk"), 4) == 2)
    def _():
        third[...] = narrowed(rows_ref[...], late_ref, column_ref[...])

    term = narrowed(rows_ref[count:, :], two_ref, column_ref[count:, :])
    keep_ref[...] = third[:count, :]
    for k in range(1, parts):
        send_ref[k - 1] = jnp.concatenate([term[(k - 1) * count:k * count], third[k * count:(k + 1) * count, :]], axis=1)


def swap_kernel(rows_ref, column_ref, swap_ref, send_ref):
    parts, count = send_ref.shape[0] + 1, 2 * send_ref.shape[1]
    term = narrowed(rows_ref[count:, :], swap_ref, column_ref[count:, :])
    for k in range(1, parts):
        send_ref[k - 1] = halved(term[(k - 1) * count:k * count])


def keep_kernel(rows_ref, column_ref, own_ref, two_ref, mix_ref, late_ref, swap_ref, two_out, swap_out, labels_ref):
    count = two_out.shape[0]
    width = rows_ref.shape[1]
    place = lax.rem(lax.axis_index("blk"), 4)
    two_out[...] = narrowed(rows_ref[:count, :], two_ref, column_ref[:count, :])
    swap_out[...] = narrowed(rows_ref[:count, :], swap_ref, column_ref[:count, :])
    own, two, mix, late, swap = [ref[width:width + 1, :] for ref in (own_ref, two_ref, mix_ref, late_ref, swap_ref)]
    third = jnp.where(place == 2, late, mix)
    odd = lax.rem(place, 2) == 1
    labels_ref[...] = jnp.concatenate([own, jnp.where(odd, third, swap), two, jnp.where(odd, swap, third)] * 2, axis=0)


def finish_kernel(parts, *refs):
    (own_keep, third_keep, two_keep, swap_keep), refs = refs[:4], refs[4:]
    own_in, pair_in, swap_in = [refs[i * (parts - 1):(i + 1) * (parts - 1)] for i in range(3)]
    labels_ref, column_ref, out_ref = refs[3 * (parts - 1):]
    count, narrow = own_keep.shape
    own = sum([unhalved(ref[...]) for ref in own_in], own_keep[...])
    two = sum([ref[:, :narrow] for ref in pair_in], two_keep[...])
    third = sum([ref[:, narrow:] for ref in pair_in], third_keep[...])
    swap = sum([unhalved(ref[...]) for ref in swap_in], swap_keep[...])
    odd = lax.rem(lax.axis_index("blk"), 2) == 1
    for m, term in enumerate([own, jnp.where(odd, third, swap), two, jnp.where(odd, swap, third)]):
        wide = jnp.concatenate([term] * (out_ref.shape[2] // narrow), axis=1)
        out_ref[m] = jnp.where(column_ref[:count, :1] == labels_ref[m:m + 1, :], wide, 0.0)


def whole(*shape):
    return jax.ShapeDtypeStruct(shape, F32)


def call(kernel, out_shape, args, flops, off=0, scratch=()):
    moved = sum(a.size * 4 for a in list(args) + out_shape)
    args = [pltpu.with_memory_space_constraint(a, pltpu.HBM) for a in args[:off]] + list(args[off:])
    return pl.pallas_call(
        kernel,
        out_shape=out_shape,
        in_specs=[OFFCHIP] * off + [ONCHIP] * (len(args) - off),
        out_specs=[ONCHIP] * len(out_shape),
        scratch_shapes=list(scratch),
        cost_estimate=pl.CostEstimate(flops=flops, bytes_accessed=moved, transcendentals=0),
        compiler_params=pltpu.CompilerParams(vmem_limit_bytes=32 * 1024 * 1024),
    )(*args)


def body(amplitudes, integrals, cd_irrep, ab_irrep, ij_irrep):
    blocks, parts = lax.axis_size("blk"), lax.axis_size("red")
    pairs, depth = amplitudes.shape
    row_count = integrals.shape[0]
    width, narrow = depth // 4, pairs // 4
    count = row_count // parts
    one_product = 12 * row_count * width * pairs

    def moved(array, steps):
        return lax.ppermute(array, "blk", [(i, (i + steps[i % 4]) % blocks) for i in range(blocks)])

    def exchanged(array):
        return [
            lax.ppermute(array[k - 1], "red", [(i, (i + k) % parts) for i in range(parts)])
            for k in range(1, parts)
        ]

    def after(array, *earlier):
        return lax.optimization_barrier((array, *earlier))[0]

    def staging(array, labels, copies):
        return [
            pltpu.VMEM(array.shape, F32),
            pltpu.VMEM(labels.shape, jnp.int32),
            pltpu.VMEM(cd_irrep.shape, jnp.int32),
        ], pltpu.SemaphoreType.DMA((2 + copies,))

    stage, sems = staging(amplitudes, ij_irrep, pairs // LANES)
    own, = call(pack_kernel, [whole(width + 8, pairs)], (amplitudes, ij_irrep, cd_irrep),
                4 * amplitudes.size, 3, stage + [sems])
    two = moved(own, (2, 2, 2, 2))
    mix = moved(own, (1, 3, 1, -1))
    stage, sems = staging(integrals, ab_irrep, parts)
    rows, labels, own_keep, own_send = call(
        first_kernel,
        [whole(row_count, width), whole(row_count, LANES), whole(count, narrow), whole(parts - 1, count // 2, 2 * narrow)],
        (integrals, ab_irrep, cd_irrep, own), 32 * one_product, 3,
        stage + [pltpu.VMEM((row_count, LANES), F32), sems])
    own_in = exchanged(own_send)
    mix_term, = call(mix_kernel, [whole(row_count, narrow)], (rows, labels, mix), one_product)
    late = moved(after(own, mix_term, *own_in), (1, -1, 1, 3))
    swap = moved(two, (1, -1, 1, -1))
    third_keep, pair_send = call(
        two_kernel, [whole(count, narrow), whole(parts - 1, count, 2 * narrow)],
        (rows, labels, mix_term, two, late), one_product, 0, [pltpu.VMEM((row_count, narrow), F32)])
    pair_in = exchanged(pair_send)
    swap_send, = call(swap_kernel, [whole(parts - 1, count // 2, 2 * narrow)],
                      (rows, labels, after(swap, pair_send)), one_product // 2)
    swap_in = exchanged(swap_send)
    two_keep, swap_keep, slab_labels = call(
        keep_kernel, [whole(count, narrow), whole(count, narrow), whole(8, pairs)],
        (rows, labels, own, two, mix, late, after(swap, swap_send)), one_product)
    out, = call(functools.partial(finish_kernel, parts), [whole(4, count, pairs)],
                (own_keep, third_keep, two_keep, swap_keep, *own_in, *pair_in, *swap_in, slab_labels, labels),
                4 * 2 * count * pairs)
    return out


def solution(mesh):
    in_specs = (P("blk", "red"), P("blk", "red"), P("red", None), P("blk", None), P("blk", None))
    out_specs = P(None, ("blk", "red"), None)
    return jax.shard_map(body, mesh=mesh, in_specs=in_specs, out_specs=out_specs, check_vma=False)
```

```python
import functools
import jax
import jax.numpy as jnp
from jax import lax
from jax.experimental import pallas as pl
from jax.experimental.pallas import tpu as pltpu
from jax.sharding import PartitionSpec as P

LANES = 128
F32 = jnp.float32
ONCHIP = pl.BlockSpec(memory_space=pltpu.VMEM)
OFFCHIP = pl.BlockSpec(memory_space=pltpu.HBM)


def column(labels):
    return jnp.broadcast_to(labels.astype(F32), (LANES, labels.shape[1])).T


def fold(rows, row_labels, cd_labels, width):
    total = None
    for start in range(0, rows.shape[1], width):
        part = slice(start, start + width)
        kept = jnp.where(row_labels[:, :1] == cd_labels[:, part], rows[:, part], 0.0)
        total = kept if total is None else total + kept
    return total


def fetch(pairs, sems):
    copies = [pltpu.make_async_copy(src, dst, sems.at[i]) for i, (src, dst) in enumerate(pairs)]
    for copy in copies:
        copy.start()
    return copies


def chunks(count):
    return [pl.ds(start, LANES) for start in range(0, count, LANES)]


def pack_kernel(amp_ref, ij_ref, cd_ref, out_ref, amp, ij, cd, sems):
    pairs, width = amp.shape[0], out_ref.shape[0] - 8
    parts = chunks(pairs)
    copies = fetch([(ij_ref, ij), (cd_ref, cd)] + [(amp_ref.at[c], amp.at[c]) for c in parts], sems)
    copies[0].wait()
    copies[1].wait()
    rows = column(ij[...])
    labels = cd[...].astype(F32)
    out_ref[width:, :] = jnp.broadcast_to(ij[...].astype(F32), (8, pairs))
    for copy, c in zip(copies[2:], parts):
        copy.wait()
        out_ref[:width, c] = fold(amp[c, :], rows[c.start:c.start + LANES], labels, width).T


def narrowed(rows, slab_ref, row_labels):
    width = rows.shape[1]
    full = jnp.dot(rows, slab_ref[:width, :], precision=lax.Precision.HIGHEST, preferred_element_type=F32)
    full = jnp.where(row_labels[:, :1] == slab_ref[width:width + 1, :], full, 0.0)
    narrow = full.shape[1] // 4
    return sum(full[:, k * narrow:(k + 1) * narrow] for k in range(1, 4)) + full[:, :narrow]


def halved(term):
    half = term.shape[0] // 2
    return jnp.concatenate([term[:half], term[half:]], axis=1)


def unhalved(term):
    half = term.shape[1] // 2
    return jnp.concatenate([term[:, :half], term[:, half:]], axis=0)


def first_kernel(v_ref, ab_ref, cd_ref, own_ref, rows_ref, column_ref, keep_ref, send_ref, v, ab, cd, labels, sems):
    width, count = rows_ref.shape[1], keep_ref.shape[0]
    parts = v.shape[0] // count
    mine = lax.axis_index("red")
    places = [pl.ds(pl.multiple_of(lax.rem(mine + k, parts) * count, count), count) for k in range(parts)]
    held = [pl.ds(k * count, count) for k in range(parts)]
    copies = fetch([(ab_ref, ab), (cd_ref, cd)] + [(v_ref.at[p], v.at[h]) for p, h in zip(places, held)], sems)
    copies[0].wait()
    copies[1].wait()
    labels[...] = column(ab[...])
    cd_labels = cd[...].astype(F32)
    for copy, p, h in zip(copies[2:], places, held):
        column_ref[h, :] = labels[p, :]
        copy.wait()
        rows_ref[h, :] = fold(v[h, :], column_ref[h, :], cd_labels, width)
    term = narrowed(rows_ref[...], own_ref, column_ref[...])
    keep_ref[...] = term[:count]
    for k in range(1, parts):
        send_ref[k - 1] = halved(term[k * count:(k + 1) * count])


def pair_kernel(rows_ref, column_ref, two_ref, mix_ref, send_ref):
    parts, count = send_ref.shape[0] + 1, send_ref.shape[1]
    narrow = send_ref.shape[2] // 2
    for place, ref in enumerate((two_ref, mix_ref)):
        term = narrowed(rows_ref[count:, :], ref, column_ref[count:, :])
        for k in range(1, parts):
            send_ref[k - 1, :, place * narrow:(place + 1) * narrow] = term[(k - 1) * count:k * count]


def swap_kernel(rows_ref, column_ref, swap_ref, send_ref):
    parts, count = send_ref.shape[0] + 1, 2 * send_ref.shape[1]
    term = narrowed(rows_ref[count:, :], swap_ref, column_ref[count:, :])
    for k in range(1, parts):
        send_ref[k - 1] = halved(term[(k - 1) * count:k * count])


def keep_kernel(rows_ref, column_ref, own_ref, two_ref, mix_ref, swap_ref, two_out, mix_out, swap_out, labels_ref):
    count = two_out.shape[0]
    width = rows_ref.shape[1]
    for ref, out_ref in ((two_ref, two_out), (mix_ref, mix_out), (swap_ref, swap_out)):
        out_ref[...] = narrowed(rows_ref[:count, :], ref, column_ref[:count, :])
    own, two, mix, swap = [ref[width:width + 1, :] for ref in (own_ref, two_ref, mix_ref, swap_ref)]
    odd = lax.rem(lax.axis_index("blk"), 2) == 1
    labels_ref[...] = jnp.concatenate([own, jnp.where(odd, mix, swap), two, jnp.where(odd, swap, mix)] * 2, axis=0)


def finish_kernel(parts, *refs):
    (own_keep, mix_keep, two_keep, swap_keep), refs = refs[:4], refs[4:]
    own_in, pair_in, swap_in = [refs[i * (parts - 1):(i + 1) * (parts - 1)] for i in range(3)]
    labels_ref, column_ref, out_ref = refs[3 * (parts - 1):]
    count, narrow = own_keep.shape
    own = sum([unhalved(ref[...]) for ref in own_in], own_keep[...])
    two = sum([ref[:, :narrow] for ref in pair_in], two_keep[...])
    mix = sum([ref[:, narrow:] for ref in pair_in], mix_keep[...])
    swap = sum([unhalved(ref[...]) for ref in swap_in], swap_keep[...])
    odd = lax.rem(lax.axis_index("blk"), 2) == 1
    for m, term in enumerate([own, jnp.where(odd, mix, swap), two, jnp.where(odd, swap, mix)]):
        wide = jnp.concatenate([term] * (out_ref.shape[2] // narrow), axis=1)
        out_ref[m] = jnp.where(column_ref[:count, :1] == labels_ref[m:m + 1, :], wide, 0.0)


def whole(*shape):
    return jax.ShapeDtypeStruct(shape, F32)


def call(kernel, out_shape, args, flops, off=0, scratch=()):
    moved = sum(a.size * 4 for a in list(args) + out_shape)
    args = [pltpu.with_memory_space_constraint(a, pltpu.HBM) for a in args[:off]] + list(args[off:])
    return pl.pallas_call(
        kernel,
        out_shape=out_shape,
        in_specs=[OFFCHIP] * off + [ONCHIP] * (len(args) - off),
        out_specs=[ONCHIP] * len(out_shape),
        scratch_shapes=list(scratch),
        cost_estimate=pl.CostEstimate(flops=flops, bytes_accessed=moved, transcendentals=0),
        compiler_params=pltpu.CompilerParams(vmem_limit_bytes=32 * 1024 * 1024),
    )(*args)


def body(amplitudes, integrals, cd_irrep, ab_irrep, ij_irrep):
    blocks, parts = lax.axis_size("blk"), lax.axis_size("red")
    pairs, depth = amplitudes.shape
    row_count = integrals.shape[0]
    width, narrow = depth // 4, pairs // 4
    count = row_count // parts
    one_product = 12 * row_count * width * pairs

    def moved(array, steps):
        return lax.ppermute(array, "blk", [(i, (i + steps[i % 4]) % blocks) for i in range(blocks)])

    def exchanged(array):
        return [
            lax.ppermute(array[k - 1], "red", [(i, (i + k) % parts) for i in range(parts)])
            for k in range(1, parts)
        ]

    def after(array, *earlier):
        return lax.optimization_barrier((array, *earlier))[0]

    def staging(array, labels, copies):
        return [
            pltpu.VMEM(array.shape, F32),
            pltpu.VMEM(labels.shape, jnp.int32),
            pltpu.VMEM(cd_irrep.shape, jnp.int32),
        ], pltpu.SemaphoreType.DMA((2 + copies,))

    stage, sems = staging(amplitudes, ij_irrep, pairs // LANES)
    own, = call(pack_kernel, [whole(width + 8, pairs)], (amplitudes, ij_irrep, cd_irrep),
                4 * amplitudes.size, 3, stage + [sems])
    two = moved(own, (2, 2, 2, 2))
    stage, sems = staging(integrals, ab_irrep, parts)
    rows, labels, own_keep, own_send = call(
        first_kernel,
        [whole(row_count, width), whole(row_count, LANES), whole(count, narrow), whole(parts - 1, count // 2, 2 * narrow)],
        (integrals, ab_irrep, cd_irrep, own), 32 * one_product, 3,
        stage + [pltpu.VMEM((row_count, LANES), F32), sems])
    own_in = exchanged(own_send)
    mix = moved(after(own, rows), (1, 3, 1, 3))
    swap = moved(after(two, *own_in), (1, -1, 1, -1))
    pair_send, = call(pair_kernel, [whole(parts - 1, count, 2 * narrow)], (rows, labels, two, mix), one_product)
    pair_in = exchanged(pair_send)
    swap_send, = call(swap_kernel, [whole(parts - 1, count // 2, 2 * narrow)],
                      (rows, labels, after(swap, pair_send)), one_product // 2)
    swap_in = exchanged(swap_send)
    two_keep, mix_keep, swap_keep, slab_labels = call(
        keep_kernel, [whole(count, narrow)] * 3 + [whole(8, pairs)],
        (rows, labels, own, two, mix, after(swap, swap_send)), one_product)
    out, = call(functools.partial(finish_kernel, parts), [whole(4, count, pairs)],
                (own_keep, mix_keep, two_keep, swap_keep, *own_in, *pair_in, *swap_in, slab_labels, labels),
                4 * 2 * count * pairs)
    return out


def solution(mesh):
    in_specs = (P("blk", "red"), P("blk", "red"), P("red", None), P("blk", None), P("blk", None))
    out_specs = P(None, ("blk", "red"), None)
    return jax.shard_map(body, mesh=mesh, in_specs=in_specs, out_specs=out_specs, check_vma=False)
```

```python
import functools
import jax
import jax.numpy as jnp
from jax import lax
from jax.experimental import pallas as pl
from jax.experimental.pallas import tpu as pltpu
from jax.sharding import PartitionSpec as P

LANES = 128
F32 = jnp.float32
ONCHIP = pl.BlockSpec(memory_space=pltpu.VMEM)
OFFCHIP = pl.BlockSpec(memory_space=pltpu.HBM)


def column(labels):
    return jnp.broadcast_to(labels.astype(F32), (LANES, labels.shape[1])).T


def fold(rows, row_labels, cd_labels, width):
    total = None
    for start in range(0, rows.shape[1], width):
        part = slice(start, start + width)
        kept = jnp.where(row_labels[:, :1] == cd_labels[:, part], rows[:, part], 0.0)
        total = kept if total is None else total + kept
    return total


def fetch(pairs, sems):
    copies = [pltpu.make_async_copy(src, dst, sems.at[i]) for i, (src, dst) in enumerate(pairs)]
    for copy in copies:
        copy.start()
    return copies


def chunks(count):
    return [pl.ds(start, LANES) for start in range(0, count, LANES)]


def pack_kernel(amp_ref, ij_ref, cd_ref, out_ref, amp, ij, cd, sems):
    pairs, width = amp.shape[0], out_ref.shape[0] - 8
    parts = chunks(pairs)
    copies = fetch([(ij_ref, ij), (cd_ref, cd)] + [(amp_ref.at[c], amp.at[c]) for c in parts], sems)
    copies[0].wait()
    copies[1].wait()
    rows = column(ij[...])
    labels = cd[...].astype(F32)
    out_ref[width:, :] = jnp.broadcast_to(ij[...].astype(F32), (8, pairs))
    for copy, c in zip(copies[2:], parts):
        copy.wait()
        out_ref[:width, c] = fold(amp[c, :], rows[c.start:c.start + LANES], labels, width).T


def narrowed(rows, slab_ref, row_labels):
    width = rows.shape[1]
    full = jnp.dot(rows, slab_ref[:width, :], precision=lax.Precision.HIGHEST, preferred_element_type=F32)
    full = jnp.where(row_labels[:, :1] == slab_ref[width:width + 1, :], full, 0.0)
    narrow = full.shape[1] // 4
    return sum(full[:, k * narrow:(k + 1) * narrow] for k in range(1, 4)) + full[:, :narrow]


def halved(term):
    half = term.shape[0] // 2
    return jnp.concatenate([term[:half], term[half:]], axis=1)


def unhalved(term):
    half = term.shape[1] // 2
    return jnp.concatenate([term[:, :half], term[:, half:]], axis=0)


def first_kernel(v_ref, ab_ref, cd_ref, own_ref, rows_ref, column_ref, keep_ref, send_ref, v, ab, cd, labels, sems):
    width, count = rows_ref.shape[1], keep_ref.shape[0]
    parts = v.shape[0] // count
    mine = lax.axis_index("red")
    places = [pl.ds(pl.multiple_of(lax.rem(mine + k, parts) * count, count), count) for k in range(parts)]
    held = [pl.ds(k * count, count) for k in range(parts)]
    copies = fetch([(ab_ref, ab), (cd_ref, cd)] + [(v_ref.at[p], v.at[h]) for p, h in zip(places, held)], sems)
    copies[0].wait()
    copies[1].wait()
    labels[...] = column(ab[...])
    cd_labels = cd[...].astype(F32)
    for copy, p, h in zip(copies[2:], places, held):
        column_ref[h, :] = labels[p, :]
        copy.wait()
        rows_ref[h, :] = fold(v[h, :], column_ref[h, :], cd_labels, width)
    term = narrowed(rows_ref[...], own_ref, column_ref[...])
    keep_ref[...] = term[:count]
    for k in range(1, parts):
        send_ref[k - 1] = halved(term[k * count:(k + 1) * count])


def pair_kernel(rows_ref, column_ref, two_ref, mix_ref, send_ref):
    parts, count = send_ref.shape[0] + 1, send_ref.shape[1]
    narrow = send_ref.shape[2] // 2
    for place, ref in enumerate((two_ref, mix_ref)):
        term = narrowed(rows_ref[count:, :], ref, column_ref[count:, :])
        for k in range(1, parts):
            send_ref[k - 1, :, place * narrow:(place + 1) * narrow] = term[(k - 1) * count:k * count]


def swap_kernel(rows_ref, column_ref, swap_ref, pair_ref, send_ref):
    parts, count = pair_ref.shape[0] + 1, pair_ref.shape[1]
    term = narrowed(rows_ref[count:, :], swap_ref, column_ref[count:, :])
    for k in range(1, parts):
        send_ref[k - 1, :count, :] = pair_ref[k - 1]
        send_ref[k - 1, count:, :] = halved(term[(k - 1) * count:k * count])


def keep_kernel(rows_ref, column_ref, own_ref, two_ref, mix_ref, swap_ref, two_out, mix_out, swap_out, labels_ref):
    count = two_out.shape[0]
    width = rows_ref.shape[1]
    for ref, out_ref in ((two_ref, two_out), (mix_ref, mix_out), (swap_ref, swap_out)):
        out_ref[...] = narrowed(rows_ref[:count, :], ref, column_ref[:count, :])
    own, two, mix, swap = [ref[width:width + 1, :] for ref in (own_ref, two_ref, mix_ref, swap_ref)]
    odd = lax.rem(lax.axis_index("blk"), 2) == 1
    labels_ref[...] = jnp.concatenate([own, jnp.where(odd, mix, swap), two, jnp.where(odd, swap, mix)] * 2, axis=0)


def finish_kernel(parts, *refs):
    (own_keep, mix_keep, two_keep, swap_keep), refs = refs[:4], refs[4:]
    own_in, late_in = refs[:parts - 1], refs[parts - 1:2 * (parts - 1)]
    labels_ref, column_ref, out_ref = refs[2 * (parts - 1):]
    count, narrow = own_keep.shape
    own = sum([unhalved(ref[...]) for ref in own_in], own_keep[...])
    two = sum([ref[:count, :narrow] for ref in late_in], two_keep[...])
    mix = sum([ref[:count, narrow:] for ref in late_in], mix_keep[...])
    swap = sum([unhalved(ref[count:, :]) for ref in late_in], swap_keep[...])
    odd = lax.rem(lax.axis_index("blk"), 2) == 1
    for m, term in enumerate([own, jnp.where(odd, mix, swap), two, jnp.where(odd, swap, mix)]):
        wide = jnp.concatenate([term] * (out_ref.shape[2] // narrow), axis=1)
        out_ref[m] = jnp.where(column_ref[:count, :1] == labels_ref[m:m + 1, :], wide, 0.0)


def whole(*shape):
    return jax.ShapeDtypeStruct(shape, F32)


def call(kernel, out_shape, args, flops, off=0, scratch=()):
    moved = sum(a.size * 4 for a in list(args) + out_shape)
    args = [pltpu.with_memory_space_constraint(a, pltpu.HBM) for a in args[:off]] + list(args[off:])
    return pl.pallas_call(
        kernel,
        out_shape=out_shape,
        in_specs=[OFFCHIP] * off + [ONCHIP] * (len(args) - off),
        out_specs=[ONCHIP] * len(out_shape),
        scratch_shapes=list(scratch),
        cost_estimate=pl.CostEstimate(flops=flops, bytes_accessed=moved, transcendentals=0),
        compiler_params=pltpu.CompilerParams(vmem_limit_bytes=32 * 1024 * 1024),
    )(*args)


def body(amplitudes, integrals, cd_irrep, ab_irrep, ij_irrep):
    blocks, parts = lax.axis_size("blk"), lax.axis_size("red")
    pairs, depth = amplitudes.shape
    row_count = integrals.shape[0]
    width, narrow = depth // 4, pairs // 4
    count = row_count // parts
    one_product = 12 * row_count * width * pairs

    def moved(array, steps):
        return lax.ppermute(array, "blk", [(i, (i + steps[i % 4]) % blocks) for i in range(blocks)])

    def exchanged(array):
        return [
            lax.ppermute(array[k - 1], "red", [(i, (i + k) % parts) for i in range(parts)])
            for k in range(1, parts)
        ]

    def after(array, *earlier):
        return lax.optimization_barrier((array, *earlier))[0]

    def staging(array, labels, copies):
        return [
            pltpu.VMEM(array.shape, F32),
            pltpu.VMEM(labels.shape, jnp.int32),
            pltpu.VMEM(cd_irrep.shape, jnp.int32),
        ], pltpu.SemaphoreType.DMA((2 + copies,))

    stage, sems = staging(amplitudes, ij_irrep, pairs // LANES)
    own, = call(pack_kernel, [whole(width + 8, pairs)], (amplitudes, ij_irrep, cd_irrep),
                4 * amplitudes.size, 3, stage + [sems])
    two = moved(own, (2, 2, 2, 2))
    stage, sems = staging(integrals, ab_irrep, parts)
    rows, labels, own_keep, own_send = call(
        first_kernel,
        [whole(row_count, width), whole(row_count, LANES), whole(count, narrow), whole(parts - 1, count // 2, 2 * narrow)],
        (integrals, ab_irrep, cd_irrep, own), 32 * one_product, 3,
        stage + [pltpu.VMEM((row_count, LANES), F32), sems])
    own_in = exchanged(own_send)
    mix = moved(after(own, rows), (1, 3, 1, 3))
    swap = moved(after(two, *own_in), (1, -1, 1, -1))
    pair_send, = call(pair_kernel, [whole(parts - 1, count, 2 * narrow)], (rows, labels, two, mix), one_product)
    late_send, = call(swap_kernel, [whole(parts - 1, count + count // 2, 2 * narrow)],
                      (rows, labels, swap, pair_send), one_product // 2)
    late_in = exchanged(late_send)
    two_keep, mix_keep, swap_keep, slab_labels = call(
        keep_kernel, [whole(count, narrow)] * 3 + [whole(8, pairs)],
        (rows, labels, own, two, mix, after(swap, late_send)), one_product)
    out, = call(functools.partial(finish_kernel, parts), [whole(4, count, pairs)],
                (own_keep, mix_keep, two_keep, swap_keep, *own_in, *late_in, slab_labels, labels),
                4 * 2 * count * pairs)
    return out


def solution(mesh):
    in_specs = (P("blk", "red"), P("blk", "red"), P("red", None), P("blk", None), P("blk", None))
    out_specs = P(None, ("blk", "red"), None)
    return jax.shard_map(body, mesh=mesh, in_specs=in_specs, out_specs=out_specs, check_vma=False)
```

```python
import functools
import jax
import jax.numpy as jnp
from jax import lax
from jax.experimental import pallas as pl
from jax.experimental.pallas import tpu as pltpu
from jax.sharding import PartitionSpec as P

LANES = 128
F32 = jnp.float32
ONCHIP = pl.BlockSpec(memory_space=pltpu.VMEM)
OFFCHIP = pl.BlockSpec(memory_space=pltpu.HBM)


def column(labels):
    return jnp.broadcast_to(labels.astype(F32), (LANES, labels.shape[1])).T


def fold(rows, row_labels, cd_labels, width):
    total = None
    for start in range(0, rows.shape[1], width):
        part = slice(start, start + width)
        kept = jnp.where(row_labels[:, :1] == cd_labels[:, part], rows[:, part], 0.0)
        total = kept if total is None else total + kept
    return total


def fetch(pairs, sems):
    copies = [pltpu.make_async_copy(src, dst, sems.at[i]) for i, (src, dst) in enumerate(pairs)]
    for copy in copies:
        copy.start()
    return copies


def chunks(count):
    return [pl.ds(start, LANES) for start in range(0, count, LANES)]


def pack_kernel(amp_ref, ij_ref, cd_ref, out_ref, amp, ij, cd, sems):
    pairs, width = amp.shape[0], out_ref.shape[0] - 8
    parts = chunks(pairs)
    copies = fetch([(ij_ref, ij), (cd_ref, cd)] + [(amp_ref.at[c], amp.at[c]) for c in parts], sems)
    copies[0].wait()
    copies[1].wait()
    rows = column(ij[...])
    labels = cd[...].astype(F32)
    out_ref[width:, :] = jnp.broadcast_to(ij[...].astype(F32), (8, pairs))
    for copy, c in zip(copies[2:], parts):
        copy.wait()
        out_ref[:width, c] = fold(amp[c, :], rows[c.start:c.start + LANES], labels, width).T


def narrowed(rows, slab_ref, row_labels):
    width = rows.shape[1]
    full = jnp.dot(rows, slab_ref[:width, :], precision=lax.Precision.HIGHEST, preferred_element_type=F32)
    full = jnp.where(row_labels[:, :1] == slab_ref[width:width + 1, :], full, 0.0)
    narrow = full.shape[1] // 4
    return sum(full[:, k * narrow:(k + 1) * narrow] for k in range(1, 4)) + full[:, :narrow]


def halved(term):
    half = term.shape[0] // 2
    return jnp.concatenate([term[:half], term[half:]], axis=1)


def unhalved(term):
    half = term.shape[1] // 2
    return jnp.concatenate([term[:, :half], term[:, half:]], axis=0)


def first_kernel(count, v_ref, ab_ref, cd_ref, rows_ref, column_ref, v, ab, cd, labels, sems):
    width, parts = rows_ref.shape[1], v.shape[0] // count
    mine = lax.axis_index("red")
    places = [pl.ds(pl.multiple_of(lax.rem(mine + k, parts) * count, count), count) for k in range(parts)]
    held = [pl.ds(k * count, count) for k in range(parts)]
    copies = fetch([(ab_ref, ab), (cd_ref, cd)] + [(v_ref.at[p], v.at[h]) for p, h in zip(places, held)], sems)
    copies[0].wait()
    copies[1].wait()
    labels[...] = column(ab[...])
    cd_labels = cd[...].astype(F32)
    for copy, p, h in zip(copies[2:], places, held):
        column_ref[h, :] = labels[p, :]
        copy.wait()
        rows_ref[h, :] = fold(v[h, :], column_ref[h, :], cd_labels, width)


def own_kernel(rows_ref, column_ref, own_ref, keep_ref, send_ref):
    count = keep_ref.shape[0]
    term = narrowed(rows_ref[...], own_ref, column_ref[...])
    keep_ref[...] = term[:count]
    for k in range(1, send_ref.shape[0] + 1):
        send_ref[k - 1] = halved(term[k * count:(k + 1) * count])


def pair_kernel(rows_ref, column_ref, two_ref, mix_ref, send_ref):
    parts, count = send_ref.shape[0] + 1, send_ref.shape[1]
    narrow = send_ref.shape[2] // 2
    for place, ref in enumerate((two_ref, mix_ref)):
        term = narrowed(rows_ref[count:, :], ref, column_ref[count:, :])
        for k in range(1, parts):
            send_ref[k - 1, :, place * narrow:(place + 1) * narrow] = term[(k - 1) * count:k * count]


def swap_kernel(rows_ref, column_ref, swap_ref, pair_ref, send_ref):
    parts, count = pair_ref.shape[0] + 1, pair_ref.shape[1]
    term = narrowed(rows_ref[count:, :], swap_ref, column_ref[count:, :])
    for k in range(1, parts):
        send_ref[k - 1, :count, :] = pair_ref[k - 1]
        send_ref[k - 1, count:, :] = halved(term[(k - 1) * count:k * count])


def keep_kernel(rows_ref, column_ref, own_ref, two_ref, mix_ref, swap_ref, two_out, mix_out, swap_out, labels_ref):
    count = two_out.shape[0]
    width = rows_ref.shape[1]
    for ref, out_ref in ((two_ref, two_out), (mix_ref, mix_out), (swap_ref, swap_out)):
        out_ref[...] = narrowed(rows_ref[:count, :], ref, column_ref[:count, :])
    own, two, mix, swap = [ref[width:width + 1, :] for ref in (own_ref, two_ref, mix_ref, swap_ref)]
    odd = lax.rem(lax.axis_index("blk"), 2) == 1
    labels_ref[...] = jnp.concatenate([own, jnp.where(odd, mix, swap), two, jnp.where(odd, swap, mix)] * 2, axis=0)


def finish_kernel(parts, *refs):
    (own_keep, mix_keep, two_keep, swap_keep), refs = refs[:4], refs[4:]
    own_in, late_in = refs[:parts - 1], refs[parts - 1:2 * (parts - 1)]
    labels_ref, column_ref, out_ref = refs[2 * (parts - 1):]
    count, narrow = own_keep.shape
    own = sum([unhalved(ref[...]) for ref in own_in], own_keep[...])
    two = sum([ref[:count, :narrow] for ref in late_in], two_keep[...])
    mix = sum([ref[:count, narrow:] for ref in late_in], mix_keep[...])
    swap = sum([unhalved(ref[count:, :]) for ref in late_in], swap_keep[...])
    odd = lax.rem(lax.axis_index("blk"), 2) == 1
    for m, term in enumerate([own, jnp.where(odd, mix, swap), two, jnp.where(odd, swap, mix)]):
        wide = jnp.concatenate([term] * (out_ref.shape[2] // narrow), axis=1)
        out_ref[m] = jnp.where(column_ref[:count, :1] == labels_ref[m:m + 1, :], wide, 0.0)


def whole(*shape):
    return jax.ShapeDtypeStruct(shape, F32)


def call(kernel, out_shape, args, flops, off=0, scratch=()):
    moved = sum(a.size * 4 for a in list(args) + out_shape)
    args = [pltpu.with_memory_space_constraint(a, pltpu.HBM) for a in args[:off]] + list(args[off:])
    return pl.pallas_call(
        kernel,
        out_shape=out_shape,
        in_specs=[OFFCHIP] * off + [ONCHIP] * (len(args) - off),
        out_specs=[ONCHIP] * len(out_shape),
        scratch_shapes=list(scratch),
        cost_estimate=pl.CostEstimate(flops=flops, bytes_accessed=moved, transcendentals=0),
        compiler_params=pltpu.CompilerParams(vmem_limit_bytes=32 * 1024 * 1024),
    )(*args)


def body(amplitudes, integrals, cd_irrep, ab_irrep, ij_irrep):
    blocks, parts = lax.axis_size("blk"), lax.axis_size("red")
    pairs, depth = amplitudes.shape
    row_count = integrals.shape[0]
    width, narrow = depth // 4, pairs // 4
    count = row_count // parts
    one_product = 12 * row_count * width * pairs

    def moved(array, steps):
        return lax.ppermute(array, "blk", [(i, (i + steps[i % 4]) % blocks) for i in range(blocks)])

    def exchanged(array):
        return [
            lax.ppermute(array[k - 1], "red", [(i, (i + k) % parts) for i in range(parts)])
            for k in range(1, parts)
        ]

    def after(array, *earlier):
        return lax.optimization_barrier((array, *earlier))[0]

    def staging(array, labels, copies):
        return [
            pltpu.VMEM(array.shape, F32),
            pltpu.VMEM(labels.shape, jnp.int32),
            pltpu.VMEM(cd_irrep.shape, jnp.int32),
        ], pltpu.SemaphoreType.DMA((2 + copies,))

    stage, sems = staging(amplitudes, ij_irrep, pairs // LANES)
    own, = call(pack_kernel, [whole(width + 8, pairs)], (amplitudes, ij_irrep, cd_irrep),
                4 * amplitudes.size, 3, stage + [sems])
    two = moved(own, (2, 2, 2, 2))
    stage, sems = staging(integrals, ab_irrep, parts)
    rows, labels = call(
        functools.partial(first_kernel, count), [whole(row_count, width), whole(row_count, LANES)],
        (integrals, ab_irrep, cd_irrep), one_product, 3, stage + [pltpu.VMEM((row_count, LANES), F32), sems])
    own_keep, own_send = call(
        own_kernel, [whole(count, narrow), whole(parts - 1, count // 2, 2 * narrow)],
        (rows, labels, own), one_product)
    own_in = exchanged(own_send)
    mix = moved(after(own, rows), (1, 3, 1, 3))
    swap = moved(after(two, *own_in), (1, -1, 1, -1))
    pair_send, = call(pair_kernel, [whole(parts - 1, count, 2 * narrow)], (rows, labels, two, mix), 40 * one_product)
    late_send, = call(swap_kernel, [whole(parts - 1, count + count // 2, 2 * narrow)],
                      (rows, labels, swap, pair_send), one_product // 2)
    late_in = exchanged(late_send)
    two_keep, mix_keep, swap_keep, slab_labels = call(
        keep_kernel, [whole(count, narrow)] * 3 + [whole(8, pairs)],
        (rows, labels, own, two, mix, after(swap, late_send)), one_product)
    out, = call(functools.partial(finish_kernel, parts), [whole(4, count, pairs)],
                (own_keep, mix_keep, two_keep, swap_keep, *own_in, *late_in, slab_labels, labels),
                4 * 2 * count * pairs)
    return out


def solution(mesh):
    in_specs = (P("blk", "red"), P("blk", "red"), P("red", None), P("blk", None), P("blk", None))
    out_specs = P(None, ("blk", "red"), None)
    return jax.shard_map(body, mesh=mesh, in_specs=in_specs, out_specs=out_specs, check_vma=False)
```

```python
import functools
import jax
import jax.numpy as jnp
from jax import lax
from jax.experimental import pallas as pl
from jax.experimental.pallas import tpu as pltpu
from jax.sharding import PartitionSpec as P

LANES = 128
F32 = jnp.float32
ONCHIP = pl.BlockSpec(memory_space=pltpu.VMEM)
OFFCHIP = pl.BlockSpec(memory_space=pltpu.HBM)


def column(labels):
    return jnp.broadcast_to(labels.astype(F32), (LANES, labels.shape[1])).T


def fold(rows, row_labels, cd_labels, width):
    total = None
    for start in range(0, rows.shape[1], width):
        part = slice(start, start + width)
        kept = jnp.where(row_labels[:, :1] == cd_labels[:, part], rows[:, part], 0.0)
        total = kept if total is None else total + kept
    return total


def fetch(pairs, sems):
    copies = [pltpu.make_async_copy(src, dst, sems.at[i]) for i, (src, dst) in enumerate(pairs)]
    for copy in copies:
        copy.start()
    return copies


def chunks(count):
    return [pl.ds(start, LANES) for start in range(0, count, LANES)]


def pack_kernel(amp_ref, ij_ref, cd_ref, out_ref, amp, ij, cd, sems):
    pairs, width = amp.shape[0], out_ref.shape[0] - 8
    parts = chunks(pairs)
    copies = fetch([(ij_ref, ij), (cd_ref, cd)] + [(amp_ref.at[c], amp.at[c]) for c in parts], sems)
    copies[0].wait()
    copies[1].wait()
    rows = column(ij[...])
    labels = cd[...].astype(F32)
    out_ref[width:, :] = jnp.broadcast_to(ij[...].astype(F32), (8, pairs))
    for copy, c in zip(copies[2:], parts):
        copy.wait()
        out_ref[:width, c] = fold(amp[c, :], rows[c.start:c.start + LANES], labels, width).T


def narrowed(rows, slab_ref, row_labels):
    width = rows.shape[1]
    full = jnp.dot(rows, slab_ref[:width, :], precision=lax.Precision.HIGHEST, preferred_element_type=F32)
    full = jnp.where(row_labels[:, :1] == slab_ref[width:width + 1, :], full, 0.0)
    narrow = full.shape[1] // 4
    return sum(full[:, k * narrow:(k + 1) * narrow] for k in range(1, 4)) + full[:, :narrow]


def halved(term):
    half = term.shape[0] // 2
    return jnp.concatenate([term[:half], term[half:]], axis=1)


def unhalved(term):
    half = term.shape[1] // 2
    return jnp.concatenate([term[:, :half], term[:, half:]], axis=0)


def first_kernel(count, v_ref, ab_ref, cd_ref, rows_ref, column_ref, v, ab, cd, labels, sems):
    width, parts = rows_ref.shape[1], v.shape[0] // count
    mine = lax.axis_index("red")
    places = [pl.ds(pl.multiple_of(lax.rem(mine + k, parts) * count, count), count) for k in range(parts)]
    held = [pl.ds(k * count, count) for k in range(parts)]
    copies = fetch([(ab_ref, ab), (cd_ref, cd)] + [(v_ref.at[p], v.at[h]) for p, h in zip(places, held)], sems)
    copies[0].wait()
    copies[1].wait()
    labels[...] = column(ab[...])
    cd_labels = cd[...].astype(F32)
    for copy, p, h in zip(copies[2:], places, held):
        column_ref[h, :] = labels[p, :]
        copy.wait()
        rows_ref[h, :] = fold(v[h, :], column_ref[h, :], cd_labels, width)


def own_kernel(rows_ref, column_ref, own_ref, keep_ref, send_ref):
    count = keep_ref.shape[0]
    term = narrowed(rows_ref[...], own_ref, column_ref[...])
    keep_ref[...] = term[:count]
    for k in range(1, send_ref.shape[0] + 1):
        send_ref[k - 1] = halved(term[k * count:(k + 1) * count])


def pair_kernel(rows_ref, column_ref, two_ref, mix_ref, send_ref):
    parts, count = send_ref.shape[0] + 1, send_ref.shape[1]
    narrow = send_ref.shape[2] // 2
    for place, ref in enumerate((two_ref, mix_ref)):
        term = narrowed(rows_ref[count:, :], ref, column_ref[count:, :])
        for k in range(1, parts):
            send_ref[k - 1, :, place * narrow:(place + 1) * narrow] = term[(k - 1) * count:k * count]


def swap_kernel(rows_ref, column_ref, swap_ref, pair_ref, send_ref):
    parts, count = pair_ref.shape[0] + 1, pair_ref.shape[1]
    term = narrowed(rows_ref[count:, :], swap_ref, column_ref[count:, :])
    for k in range(1, parts):
        send_ref[k - 1, :count, :] = pair_ref[k - 1]
        send_ref[k - 1, count:, :] = halved(term[(k - 1) * count:k * count])


def keep_kernel(rows_ref, column_ref, own_ref, two_ref, mix_ref, swap_ref, two_out, mix_out, swap_out, labels_ref):
    count = two_out.shape[0]
    width = rows_ref.shape[1]
    for ref, out_ref in ((two_ref, two_out), (mix_ref, mix_out), (swap_ref, swap_out)):
        out_ref[...] = narrowed(rows_ref[:count, :], ref, column_ref[:count, :])
    own, two, mix, swap = [ref[width:width + 1, :] for ref in (own_ref, two_ref, mix_ref, swap_ref)]
    odd = lax.rem(lax.axis_index("blk"), 2) == 1
    labels_ref[...] = jnp.concatenate([own, jnp.where(odd, mix, swap), two, jnp.where(odd, swap, mix)] * 2, axis=0)


def finish_kernel(parts, *refs):
    (own_keep, mix_keep, two_keep, swap_keep), refs = refs[:4], refs[4:]
    own_in, late_in = refs[:parts - 1], refs[parts - 1:2 * (parts - 1)]
    labels_ref, column_ref, out_ref = refs[2 * (parts - 1):]
    count, narrow = own_keep.shape
    own = sum([unhalved(ref[...]) for ref in own_in], own_keep[...])
    two = sum([ref[:count, :narrow] for ref in late_in], two_keep[...])
    mix = sum([ref[:count, narrow:] for ref in late_in], mix_keep[...])
    swap = sum([unhalved(ref[count:, :]) for ref in late_in], swap_keep[...])
    odd = lax.rem(lax.axis_index("blk"), 2) == 1
    for m, term in enumerate([own, jnp.where(odd, mix, swap), two, jnp.where(odd, swap, mix)]):
        wide = jnp.concatenate([term] * (out_ref.shape[2] // narrow), axis=1)
        out_ref[m] = jnp.where(column_ref[:count, :1] == labels_ref[m:m + 1, :], wide, 0.0)


def whole(*shape):
    return jax.ShapeDtypeStruct(shape, F32)


def call(kernel, out_shape, args, flops, off=0, scratch=()):
    moved = sum(a.size * 4 for a in list(args) + out_shape)
    args = [pltpu.with_memory_space_constraint(a, pltpu.HBM) for a in args[:off]] + list(args[off:])
    return pl.pallas_call(
        kernel,
        out_shape=out_shape,
        in_specs=[OFFCHIP] * off + [ONCHIP] * (len(args) - off),
        out_specs=[ONCHIP] * len(out_shape),
        scratch_shapes=list(scratch),
        cost_estimate=pl.CostEstimate(flops=flops, bytes_accessed=moved, transcendentals=0),
        compiler_params=pltpu.CompilerParams(vmem_limit_bytes=32 * 1024 * 1024),
    )(*args)


def body(amplitudes, integrals, cd_irrep, ab_irrep, ij_irrep):
    blocks, parts = lax.axis_size("blk"), lax.axis_size("red")
    pairs, depth = amplitudes.shape
    row_count = integrals.shape[0]
    width, narrow = depth // 4, pairs // 4
    count = row_count // parts
    one_product = 12 * row_count * width * pairs

    def moved(array, steps):
        return lax.ppermute(array, "blk", [(i, (i + steps[i % 4]) % blocks) for i in range(blocks)])

    def exchanged(array):
        return [
            lax.ppermute(array[k - 1], "red", [(i, (i + k) % parts) for i in range(parts)])
            for k in range(1, parts)
        ]

    def after(array, *earlier):
        return lax.optimization_barrier((array, *earlier))[0]

    def staging(array, labels, copies):
        return [
            pltpu.VMEM(array.shape, F32),
            pltpu.VMEM(labels.shape, jnp.int32),
            pltpu.VMEM(cd_irrep.shape, jnp.int32),
        ], pltpu.SemaphoreType.DMA((2 + copies,))

    stage, sems = staging(amplitudes, ij_irrep, pairs // LANES)
    own, = call(pack_kernel, [whole(width + 8, pairs)], (amplitudes, ij_irrep, cd_irrep),
                4 * amplitudes.size, 3, stage + [sems])
    two = moved(own, (2, 2, 2, 2))
    stage, sems = staging(integrals, ab_irrep, parts)
    rows, labels = call(
        functools.partial(first_kernel, count), [whole(row_count, width), whole(row_count, LANES)],
        (integrals, ab_irrep, cd_irrep), one_product, 3, stage + [pltpu.VMEM((row_count, LANES), F32), sems])
    own_keep, own_send = call(
        own_kernel, [whole(count, narrow), whole(parts - 1, count // 2, 2 * narrow)],
        (rows, labels, own), one_product)
    own_in = exchanged(own_send)
    mix = moved(after(own, own_keep), (1, 3, 1, 3))
    swap = moved(after(two, *own_in), (1, -1, 1, -1))
    pair_send, = call(pair_kernel, [whole(parts - 1, count, 2 * narrow)], (rows, labels, two, mix), 40 * one_product)
    late_send, = call(swap_kernel, [whole(parts - 1, count + count // 2, 2 * narrow)],
                      (rows, labels, swap, pair_send), one_product // 2)
    late_in = exchanged(late_send)
    two_keep, mix_keep, swap_keep, slab_labels = call(
        keep_kernel, [whole(count, narrow)] * 3 + [whole(8, pairs)],
        (rows, labels, own, two, mix, after(swap, late_send)), one_product)
    out, = call(functools.partial(finish_kernel, parts), [whole(4, count, pairs)],
                (own_keep, mix_keep, two_keep, swap_keep, *own_in, *late_in, slab_labels, labels),
                4 * 2 * count * pairs)
    return out


def solution(mesh):
    in_specs = (P("blk", "red"), P("blk", "red"), P("red", None), P("blk", None), P("blk", None))
    out_specs = P(None, ("blk", "red"), None)
    return jax.shard_map(body, mesh=mesh, in_specs=in_specs, out_specs=out_specs, check_vma=False)
```

```python
import functools
import jax
import jax.numpy as jnp
from jax import lax
from jax.experimental import pallas as pl
from jax.experimental.pallas import tpu as pltpu
from jax.sharding import PartitionSpec as P

LANES = 128
F32 = jnp.float32
ONCHIP = pl.BlockSpec(memory_space=pltpu.VMEM)
OFFCHIP = pl.BlockSpec(memory_space=pltpu.HBM)


def column(labels):
    return jnp.broadcast_to(labels.astype(F32), (LANES, labels.shape[1])).T


def fold(rows, row_labels, cd_labels):
    tiles = rows.shape[1] // LANES
    kept = [
        jnp.where(row_labels == cd_labels[:, k * LANES:(k + 1) * LANES], rows[:, k * LANES:(k + 1) * LANES], 0.0)
        for k in range(tiles)
    ]
    kept = [kept[k] + kept[k + tiles // 2] for k in range(tiles // 2)]
    low = lower(kept[0].shape)
    first, middle, last = kept
    middle_turned, last_turned = turned(middle), turned(last)
    return first + jnp.where(low, middle_turned, last_turned), middle + last_turned


def lower(shape):
    return lax.broadcasted_iota(jnp.int32, shape, 1) < LANES // 2


def turned(array):
    return pltpu.roll(array, LANES // 2, 1)


def fetch(pairs, sems):
    copies = [pltpu.make_async_copy(src, dst, sems.at[i]) for i, (src, dst) in enumerate(pairs)]
    for copy in copies:
        copy.start()
    return copies


def pack_kernel(amp_ref, ij_ref, cd_ref, out_ref, amp, ij, cd, sems):
    pairs, width = amp.shape[0], out_ref.shape[0] - 8
    copies = fetch([(amp_ref, amp), (ij_ref, ij), (cd_ref, cd)], sems)
    copies[1].wait()
    copies[2].wait()
    rows = column(ij[...])
    labels = cd[...].astype(F32)
    out_ref[width:, :] = jnp.broadcast_to(ij[...].astype(F32), (8, pairs))
    copies[0].wait()
    for start in range(0, pairs, LANES):
        part = slice(start, start + LANES)
        first, second = fold(amp[part, :], rows[part], labels)
        out_ref[:LANES, part] = first.T
        out_ref[LANES:width, part] = second.T[:width - LANES]


def narrowed(rows, slab_ref, row_labels):
    width = rows.shape[1]
    full = jnp.dot(rows, slab_ref[:width, :], precision=lax.Precision.HIGHEST, preferred_element_type=F32)
    labels = slab_ref[width:width + 1, :]
    total = None
    for start in range(0, full.shape[1], LANES):
        part = slice(start, start + LANES)
        kept = jnp.where(row_labels == labels[:, part], full[:, part], 0.0)
        total = kept if total is None else total + kept
    return total + turned(total)


def beside(one, other):
    return jnp.where(lower(one.shape), one, other)


def apart(array):
    low, other = lower(array.shape), turned(array)
    return jnp.where(low, array, other), jnp.where(low, other, array)


def halved(term):
    half = term.shape[0] // 2
    return beside(term[:half], term[half:])


def unhalved(term):
    return jnp.concatenate(apart(term), axis=0)


def first_kernel(count, v_ref, ab_ref, cd_ref, rows_ref, column_ref, v, ab, cd, labels, sems):
    width, parts = rows_ref.shape[1], v.shape[0] // count
    mine = lax.axis_index("red")
    places = [pl.ds(pl.multiple_of(lax.rem(mine + k, parts) * count, count), count) for k in range(parts)]
    held = [pl.ds(k * count, count) for k in range(parts)]
    copies = fetch([(ab_ref, ab), (cd_ref, cd)] + [(v_ref.at[p], v.at[h]) for p, h in zip(places, held)], sems)
    copies[0].wait()
    copies[1].wait()
    labels[...] = column(ab[...])
    cd_labels = cd[...].astype(F32)
    for copy, p, h in zip(copies[2:], places, held):
        column_ref[h, :] = labels[p, :]
        copy.wait()
        first, second = fold(v[h, :], column_ref[h, :], cd_labels)
        rows_ref[h, :LANES] = first
        rows_ref[h, LANES:] = second[:, :width - LANES]


def own_kernel(rows_ref, column_ref, own_ref, keep_ref, send_ref):
    count = keep_ref.shape[0]
    term = narrowed(rows_ref[...], own_ref, column_ref[...])
    keep_ref[...] = term[:count]
    for k in range(1, send_ref.shape[0] + 1):
        send_ref[k - 1] = halved(term[k * count:(k + 1) * count])


def pair_kernel(rows_ref, column_ref, two_ref, mix_ref, send_ref):
    parts, count = send_ref.shape[0] + 1, send_ref.shape[1]
    two, mix = [narrowed(rows_ref[count:, :], ref, column_ref[count:, :]) for ref in (two_ref, mix_ref)]
    both = beside(two, mix)
    for k in range(1, parts):
        send_ref[k - 1] = both[(k - 1) * count:k * count]


def swap_kernel(rows_ref, column_ref, swap_ref, pair_ref, send_ref):
    parts, count = pair_ref.shape[0] + 1, pair_ref.shape[1]
    term = narrowed(rows_ref[count:, :], swap_ref, column_ref[count:, :])
    for k in range(1, parts):
        send_ref[k - 1, :count, :] = pair_ref[k - 1]
        send_ref[k - 1, count:, :] = halved(term[(k - 1) * count:k * count])


def keep_kernel(rows_ref, column_ref, own_ref, two_ref, mix_ref, swap_ref, two_out, mix_out, swap_out, labels_ref):
    count = two_out.shape[0]
    width = rows_ref.shape[1]
    for ref, out_ref in ((two_ref, two_out), (mix_ref, mix_out), (swap_ref, swap_out)):
        out_ref[...] = narrowed(rows_ref[:count, :], ref, column_ref[:count, :])
    own, two, mix, swap = [ref[width:width + 1, :] for ref in (own_ref, two_ref, mix_ref, swap_ref)]
    odd = lax.rem(lax.axis_index("blk"), 2) == 1
    labels_ref[...] = jnp.concatenate([own, jnp.where(odd, mix, swap), two, jnp.where(odd, swap, mix)] * 2, axis=0)


def finish_kernel(parts, own_keep, mix_keep, two_keep, swap_keep, *refs):
    own_in, late_in = refs[:parts - 1], refs[parts - 1:2 * (parts - 1)]
    labels_ref, column_ref, out_ref, out, sems = refs[2 * (parts - 1):]
    count = own_keep.shape[0]
    rows = column_ref[:count, :]
    copies = []

    def store(m, term):
        for start in range(0, out.shape[2], LANES):
            part = slice(start, start + LANES)
            out[m, :, part] = jnp.where(rows == labels_ref[m:m + 1, part], term, 0.0)
        copies.append(pltpu.make_async_copy(out.at[m], out_ref.at[m], sems.at[m]))
        copies[-1].start()

    odd = lax.rem(lax.axis_index("blk"), 2) == 1
    store(0, sum([unhalved(ref[...]) for ref in own_in], own_keep[...]))
    pairs = [apart(ref[:count, :]) for ref in late_in]
    store(2, sum([two for two, _ in pairs], two_keep[...]))
    mix = sum([mix for _, mix in pairs], mix_keep[...])
    swap = sum([unhalved(ref[count:, :]) for ref in late_in], swap_keep[...])
    store(1, jnp.where(odd, mix, swap))
    store(3, jnp.where(odd, swap, mix))
    for copy in copies:
        copy.wait()


def whole(*shape):
    return jax.ShapeDtypeStruct(shape, F32)


def call(kernel, out_shape, args, flops, off=0, scratch=(), out_specs=ONCHIP):
    moved = sum(a.size * 4 for a in list(args) + out_shape)
    args = [pltpu.with_memory_space_constraint(a, pltpu.HBM) for a in args[:off]] + list(args[off:])
    return pl.pallas_call(
        kernel,
        out_shape=out_shape,
        in_specs=[OFFCHIP] * off + [ONCHIP] * (len(args) - off),
        out_specs=[out_specs] * len(out_shape),
        scratch_shapes=list(scratch),
        cost_estimate=pl.CostEstimate(flops=flops, bytes_accessed=moved, transcendentals=0),
        compiler_params=pltpu.CompilerParams(vmem_limit_bytes=32 * 1024 * 1024),
    )(*args)


def body(amplitudes, integrals, cd_irrep, ab_irrep, ij_irrep):
    blocks, parts = lax.axis_size("blk"), lax.axis_size("red")
    pairs, depth = amplitudes.shape
    row_count = integrals.shape[0]
    width = depth // 4
    count = row_count // parts
    one_product = 12 * row_count * width * pairs

    def moved(array, steps):
        return lax.ppermute(array, "blk", [(i, (i + steps[i % 4]) % blocks) for i in range(blocks)])

    def exchanged(array):
        return [
            lax.ppermute(array[k - 1], "red", [(i, (i + k) % parts) for i in range(parts)])
            for k in range(1, parts)
        ]

    def after(array, *earlier):
        return lax.optimization_barrier((array, *earlier))[0]

    def staging(array, labels, copies):
        return [
            pltpu.VMEM(array.shape, F32),
            pltpu.VMEM(labels.shape, jnp.int32),
            pltpu.VMEM(cd_irrep.shape, jnp.int32),
        ], pltpu.SemaphoreType.DMA((2 + copies,))

    stage, sems = staging(amplitudes, ij_irrep, 1)
    own, = call(pack_kernel, [whole(width + 8, pairs)], (amplitudes, ij_irrep, cd_irrep),
                4 * amplitudes.size, 3, stage + [sems])
    two = moved(own, (2, 2, 2, 2))
    stage, sems = staging(integrals, ab_irrep, parts)
    rows, labels = call(
        functools.partial(first_kernel, count), [whole(row_count, width), whole(row_count, LANES)],
        (integrals, ab_irrep, cd_irrep), one_product, 3, stage + [pltpu.VMEM((row_count, LANES), F32), sems])
    own_keep, own_send = call(
        own_kernel, [whole(count, LANES), whole(parts - 1, count // 2, LANES)],
        (rows, labels, own), one_product)
    own_in = exchanged(own_send)
    mix = moved(after(own, own_keep), (1, 3, 1, 3))
    swap = moved(after(two, *own_in), (1, -1, 1, -1))
    pair_send, = call(pair_kernel, [whole(parts - 1, count, LANES)], (rows, labels, two, mix), 40 * one_product)
    late_send, = call(swap_kernel, [whole(parts - 1, count + count // 2, LANES)],
                      (rows, labels, swap, pair_send), one_product // 2)
    late_in = exchanged(late_send)
    two_keep, mix_keep, swap_keep, slab_labels = call(
        keep_kernel, [whole(count, LANES)] * 3 + [whole(8, pairs)],
        (rows, labels, own, two, mix, after(swap, late_send)), one_product)
    out, = call(functools.partial(finish_kernel, parts), [whole(4, count, pairs)],
                (own_keep, mix_keep, two_keep, swap_keep, *own_in, *late_in, slab_labels, labels),
                4 * 2 * count * pairs, 0, [pltpu.VMEM((4, count, pairs), F32), pltpu.SemaphoreType.DMA((4,))], OFFCHIP)
    return out


def solution(mesh):
    in_specs = (P("blk", "red"), P("blk", "red"), P("red", None), P("blk", None), P("blk", None))
    out_specs = P(None, ("blk", "red"), None)
    return jax.shard_map(body, mesh=mesh, in_specs=in_specs, out_specs=out_specs, check_vma=False)
```

```python
import functools
import jax
import jax.numpy as jnp
from jax import lax
from jax.experimental import pallas as pl
from jax.experimental.pallas import tpu as pltpu
from jax.sharding import PartitionSpec as P

LANES = 128
F32 = jnp.float32
ONCHIP = pl.BlockSpec(memory_space=pltpu.VMEM)
OFFCHIP = pl.BlockSpec(memory_space=pltpu.HBM)


def column(labels):
    return jnp.broadcast_to(labels.astype(F32), (LANES, labels.shape[1])).T


def fold(rows, row_labels, cd_labels):
    tiles = rows.shape[1] // LANES
    kept = [
        jnp.where(row_labels == cd_labels[:, k * LANES:(k + 1) * LANES], rows[:, k * LANES:(k + 1) * LANES], 0.0)
        for k in range(tiles)
    ]
    kept = [kept[k] + kept[k + tiles // 2] for k in range(tiles // 2)]
    low = lower(kept[0].shape)
    first, middle, last = kept
    middle_turned, last_turned = turned(middle), turned(last)
    return first + jnp.where(low, middle_turned, last_turned), middle + last_turned


def lower(shape):
    return lax.broadcasted_iota(jnp.int32, shape, 1) < LANES // 2


def turned(array):
    return pltpu.roll(array, LANES // 2, 1)


def fetch(pairs, sems):
    copies = [pltpu.make_async_copy(src, dst, sems.at[i]) for i, (src, dst) in enumerate(pairs)]
    for copy in copies:
        copy.start()
    return copies


def pack_kernel(amp_ref, ij_ref, cd_ref, out_ref, amp, ij, cd, sems):
    pairs, width = amp.shape[0], out_ref.shape[0] - 8
    copies = fetch([(amp_ref, amp), (ij_ref, ij), (cd_ref, cd)], sems)
    copies[1].wait()
    copies[2].wait()
    rows = column(ij[...])
    labels = cd[...].astype(F32)
    out_ref[width:, :] = jnp.broadcast_to(ij[...].astype(F32), (8, pairs))
    copies[0].wait()
    for start in range(0, pairs, LANES):
        part = slice(start, start + LANES)
        first, second = fold(amp[part, :], rows[part], labels)
        out_ref[:LANES, part] = first.T
        out_ref[LANES:width, part] = second.T[:width - LANES]


def narrowed(rows, slab_ref, row_labels):
    width = rows.shape[1]
    full = jnp.dot(rows, slab_ref[:width, :], precision=lax.Precision.HIGHEST, preferred_element_type=F32)
    labels = slab_ref[width:width + 1, :]
    total = None
    for start in range(0, full.shape[1], LANES):
        part = slice(start, start + LANES)
        kept = jnp.where(row_labels == labels[:, part], full[:, part], 0.0)
        total = kept if total is None else total + kept
    return total + turned(total)


def beside(one, other):
    return jnp.where(lower(one.shape), one, other)


def apart(array):
    low, other = lower(array.shape), turned(array)
    return jnp.where(low, array, other), jnp.where(low, other, array)


def halved(term):
    half = term.shape[0] // 2
    return beside(term[:half], term[half:])


def unhalved(term):
    return jnp.concatenate(apart(term), axis=0)


def first_kernel(count, v_ref, ab_ref, cd_ref, rows_ref, column_ref, v, ab, cd, labels, sems):
    width, parts = rows_ref.shape[1], v.shape[0] // count
    mine = lax.axis_index("red")
    places = [pl.ds(pl.multiple_of(lax.rem(mine + k, parts) * count, count), count) for k in range(parts)]
    held = [pl.ds(k * count, count) for k in range(parts)]
    copies = fetch([(ab_ref, ab), (cd_ref, cd)] + [(v_ref.at[p], v.at[h]) for p, h in zip(places, held)], sems)
    copies[0].wait()
    copies[1].wait()
    labels[...] = column(ab[...])
    cd_labels = cd[...].astype(F32)
    for copy, p, h in zip(copies[2:], places, held):
        column_ref[h, :] = labels[p, :]
        copy.wait()
        first, second = fold(v[h, :], column_ref[h, :], cd_labels)
        rows_ref[h, :LANES] = first
        rows_ref[h, LANES:] = second[:, :width - LANES]


def own_kernel(rows_ref, column_ref, own_ref, keep_ref, send_ref):
    count = keep_ref.shape[0]
    term = narrowed(rows_ref[...], own_ref, column_ref[...])
    keep_ref[...] = term[:count]
    for k in range(1, send_ref.shape[0] + 1):
        send_ref[k - 1] = halved(term[k * count:(k + 1) * count])


def late_place():
    return lax.rem(lax.axis_index("blk"), 4) == 2


def third_term(part, rows_ref, column_ref, mix_ref, late_ref, out_ref):
    for ref, here in ((mix_ref, ~late_place()), (late_ref, late_place())):

        @pl.when(here)
        def _():
            out_ref[...] = narrowed(rows_ref[part, :], ref, column_ref[part, :])


def pair_kernel(rows_ref, column_ref, two_ref, mix_ref, late_ref, send_ref, third):
    parts, count = send_ref.shape[0] + 1, send_ref.shape[1]
    third_term(slice(count, None), rows_ref, column_ref, mix_ref, late_ref, third)
    both = beside(narrowed(rows_ref[count:, :], two_ref, column_ref[count:, :]), third[...])
    for k in range(1, parts):
        send_ref[k - 1] = both[(k - 1) * count:k * count]


def swap_kernel(rows_ref, column_ref, swap_ref, pair_ref, send_ref):
    parts, count = pair_ref.shape[0] + 1, pair_ref.shape[1]
    term = narrowed(rows_ref[count:, :], swap_ref, column_ref[count:, :])
    for k in range(1, parts):
        send_ref[k - 1, :count, :] = pair_ref[k - 1]
        send_ref[k - 1, count:, :] = halved(term[(k - 1) * count:k * count])


def keep_kernel(rows_ref, column_ref, own_ref, two_ref, mix_ref, late_ref, swap_ref, two_out, mix_out, swap_out, labels_ref):
    count = two_out.shape[0]
    width = rows_ref.shape[1]
    third_term(slice(0, count), rows_ref, column_ref, mix_ref, late_ref, mix_out)
    for ref, out_ref in ((two_ref, two_out), (swap_ref, swap_out)):
        out_ref[...] = narrowed(rows_ref[:count, :], ref, column_ref[:count, :])
    own, two, mix, late, swap = [ref[width:width + 1, :] for ref in (own_ref, two_ref, mix_ref, late_ref, swap_ref)]
    mix = jnp.where(late_place(), late, mix)
    odd = lax.rem(lax.axis_index("blk"), 2) == 1
    labels_ref[...] = jnp.concatenate([own, jnp.where(odd, mix, swap), two, jnp.where(odd, swap, mix)] * 2, axis=0)


def finish_kernel(parts, own_keep, mix_keep, two_keep, swap_keep, *refs):
    own_in, late_in = refs[:parts - 1], refs[parts - 1:2 * (parts - 1)]
    labels_ref, column_ref, out_ref, out, sems = refs[2 * (parts - 1):]
    count = own_keep.shape[0]
    rows = column_ref[:count, :]
    copies = []

    def store(m, term):
        for start in range(0, out.shape[2], LANES):
            part = slice(start, start + LANES)
            out[m, :, part] = jnp.where(rows == labels_ref[m:m + 1, part], term, 0.0)
        copies.append(pltpu.make_async_copy(out.at[m], out_ref.at[m], sems.at[m]))
        copies[-1].start()

    odd = lax.rem(lax.axis_index("blk"), 2) == 1
    store(0, sum([unhalved(ref[...]) for ref in own_in], own_keep[...]))
    pairs = [apart(ref[:count, :]) for ref in late_in]
    store(2, sum([two for two, _ in pairs], two_keep[...]))
    mix = sum([mix for _, mix in pairs], mix_keep[...])
    swap = sum([unhalved(ref[count:, :]) for ref in late_in], swap_keep[...])
    store(1, jnp.where(odd, mix, swap))
    store(3, jnp.where(odd, swap, mix))
    for copy in copies:
        copy.wait()


def whole(*shape):
    return jax.ShapeDtypeStruct(shape, F32)


def call(kernel, out_shape, args, flops, off=0, scratch=(), out_specs=ONCHIP):
    moved = sum(a.size * 4 for a in list(args) + out_shape)
    args = [pltpu.with_memory_space_constraint(a, pltpu.HBM) for a in args[:off]] + list(args[off:])
    return pl.pallas_call(
        kernel,
        out_shape=out_shape,
        in_specs=[OFFCHIP] * off + [ONCHIP] * (len(args) - off),
        out_specs=[out_specs] * len(out_shape),
        scratch_shapes=list(scratch),
        cost_estimate=pl.CostEstimate(flops=flops, bytes_accessed=moved, transcendentals=0),
        compiler_params=pltpu.CompilerParams(vmem_limit_bytes=32 * 1024 * 1024),
    )(*args)


def body(amplitudes, integrals, cd_irrep, ab_irrep, ij_irrep):
    blocks, parts = lax.axis_size("blk"), lax.axis_size("red")
    pairs, depth = amplitudes.shape
    row_count = integrals.shape[0]
    width = depth // 4
    count = row_count // parts
    one_product = 12 * row_count * width * pairs

    def moved(array, steps):
        return lax.ppermute(array, "blk", [(i, (i + steps[i % 4]) % blocks) for i in range(blocks)])

    def exchanged(array):
        return [
            lax.ppermute(array[k - 1], "red", [(i, (i + k) % parts) for i in range(parts)])
            for k in range(1, parts)
        ]

    def after(array, *earlier):
        return lax.optimization_barrier((array, *earlier))[0]

    def staging(array, labels, copies):
        return [
            pltpu.VMEM(array.shape, F32),
            pltpu.VMEM(labels.shape, jnp.int32),
            pltpu.VMEM(cd_irrep.shape, jnp.int32),
        ], pltpu.SemaphoreType.DMA((2 + copies,))

    stage, sems = staging(amplitudes, ij_irrep, 1)
    own, = call(pack_kernel, [whole(width + 8, pairs)], (amplitudes, ij_irrep, cd_irrep),
                4 * amplitudes.size, 3, stage + [sems])
    two = moved(own, (2, 2, 2, 2))
    mix = moved(own, (1, 3, 1, -1))
    stage, sems = staging(integrals, ab_irrep, parts)
    rows, labels = call(
        functools.partial(first_kernel, count), [whole(row_count, width), whole(row_count, LANES)],
        (integrals, ab_irrep, cd_irrep), one_product, 3, stage + [pltpu.VMEM((row_count, LANES), F32), sems])
    own_keep, own_send = call(
        own_kernel, [whole(count, LANES), whole(parts - 1, count // 2, LANES)],
        (rows, labels, own), one_product)
    own_in = exchanged(own_send)
    late = moved(after(own, own_keep, mix), (1, -1, 1, 3))
    swap = moved(after(two, *own_in), (1, -1, 1, -1))
    pair_send, = call(pair_kernel, [whole(parts - 1, count, LANES)], (rows, labels, two, mix, late), one_product, 0,
                      [pltpu.VMEM((row_count - count, LANES), F32)])
    late_send, = call(swap_kernel, [whole(parts - 1, count + count // 2, LANES)],
                      (rows, labels, swap, pair_send), one_product // 2)
    late_in = exchanged(late_send)
    two_keep, mix_keep, swap_keep, slab_labels = call(
        keep_kernel, [whole(count, LANES)] * 3 + [whole(8, pairs)],
        (rows, labels, own, two, mix, late, after(swap, late_send)), one_product)
    out, = call(functools.partial(finish_kernel, parts), [whole(4, count, pairs)],
                (own_keep, mix_keep, two_keep, swap_keep, *own_in, *late_in, slab_labels, labels),
                4 * 2 * count * pairs, 0, [pltpu.VMEM((4, count, pairs), F32), pltpu.SemaphoreType.DMA((4,))], OFFCHIP)
    return out


def solution(mesh):
    in_specs = (P("blk", "red"), P("blk", "red"), P("red", None), P("blk", None), P("blk", None))
    out_specs = P(None, ("blk", "red"), None)
    return jax.shard_map(body, mesh=mesh, in_specs=in_specs, out_specs=out_specs, check_vma=False)
```

```python
import functools
import jax
import jax.numpy as jnp
from jax import lax
from jax.experimental import pallas as pl
from jax.experimental.pallas import tpu as pltpu
from jax.sharding import PartitionSpec as P

LANES = 128
F32 = jnp.float32
ONCHIP = pl.BlockSpec(memory_space=pltpu.VMEM)
OFFCHIP = pl.BlockSpec(memory_space=pltpu.HBM)


def column(labels):
    return jnp.broadcast_to(labels.astype(F32), (LANES, labels.shape[1])).T


def fold(rows, row_labels, cd_labels):
    tiles = rows.shape[1] // LANES
    kept = [
        jnp.where(row_labels == cd_labels[:, k * LANES:(k + 1) * LANES], rows[:, k * LANES:(k + 1) * LANES], 0.0)
        for k in range(tiles)
    ]
    kept = [kept[k] + kept[k + tiles // 2] for k in range(tiles // 2)]
    low = lower(kept[0].shape)
    first, middle, last = kept
    middle_turned, last_turned = turned(middle), turned(last)
    return first + jnp.where(low, middle_turned, last_turned), middle + last_turned


def lower(shape):
    return lax.broadcasted_iota(jnp.int32, shape, 1) < LANES // 2


def turned(array):
    return pltpu.roll(array, LANES // 2, 1)


def fetch(pairs, sems):
    copies = [pltpu.make_async_copy(src, dst, sems.at[i]) for i, (src, dst) in enumerate(pairs)]
    for copy in copies:
        copy.start()
    return copies


def pack_kernel(amp_ref, ij_ref, cd_ref, out_ref, amp, ij, cd, sems):
    pairs, width = amp.shape[0], out_ref.shape[0] - 8
    copies = fetch([(amp_ref, amp), (ij_ref, ij), (cd_ref, cd)], sems)
    copies[1].wait()
    copies[2].wait()
    rows = column(ij[...])
    labels = cd[...].astype(F32)
    out_ref[width:, :] = jnp.broadcast_to(ij[...].astype(F32), (8, pairs))
    copies[0].wait()
    for start in range(0, pairs, LANES):
        part = slice(start, start + LANES)
        first, second = fold(amp[part, :], rows[part], labels)
        out_ref[:LANES, part] = first.T
        out_ref[LANES:width, part] = second.T[:width - LANES]


def narrowed(rows, slab_ref, row_labels):
    width = rows.shape[1]
    full = jnp.dot(rows, slab_ref[:width, :], precision=lax.Precision.HIGHEST, preferred_element_type=F32)
    labels = slab_ref[width:width + 1, :]
    total = None
    for start in range(0, full.shape[1], LANES):
        part = slice(start, start + LANES)
        kept = jnp.where(row_labels == labels[:, part], full[:, part], 0.0)
        total = kept if total is None else total + kept
    return total + turned(total)


def beside(one, other):
    return jnp.where(lower(one.shape), one, other)


def apart(array):
    low, other = lower(array.shape), turned(array)
    return jnp.where(low, array, other), jnp.where(low, other, array)


def halved(term):
    half = term.shape[0] // 2
    return beside(term[:half], term[half:])


def unhalved(term):
    return jnp.concatenate(apart(term), axis=0)


def first_kernel(count, v_ref, ab_ref, cd_ref, rows_ref, column_ref, v, ab, cd, labels, sems):
    width, parts = rows_ref.shape[1], v.shape[0] // count
    mine = lax.axis_index("red")
    places = [pl.ds(pl.multiple_of(lax.rem(mine + k, parts) * count, count), count) for k in range(parts)]
    held = [pl.ds(k * count, count) for k in range(parts)]
    copies = fetch([(ab_ref, ab), (cd_ref, cd)] + [(v_ref.at[p], v.at[h]) for p, h in zip(places, held)], sems)
    copies[0].wait()
    copies[1].wait()
    labels[...] = column(ab[...])
    cd_labels = cd[...].astype(F32)
    for copy, p, h in zip(copies[2:], places, held):
        column_ref[h, :] = labels[p, :]
        copy.wait()
        first, second = fold(v[h, :], column_ref[h, :], cd_labels)
        rows_ref[h, :LANES] = first
        rows_ref[h, LANES:] = second[:, :width - LANES]


def labels_kernel(slab_ref, out_ref):
    out_ref[...] = slab_ref[slab_ref.shape[0] - 8:, :]


def own_kernel(rows_ref, column_ref, own_ref, keep_ref, send_ref):
    count = keep_ref.shape[0]
    term = narrowed(rows_ref[...], own_ref, column_ref[...])
    keep_ref[...] = term[:count]
    for k in range(1, send_ref.shape[0] + 1):
        send_ref[k - 1] = halved(term[k * count:(k + 1) * count])


def late_place():
    return lax.rem(lax.axis_index("blk"), 4) == 2


def third_term(part, rows_ref, column_ref, mix_ref, late_ref, out_ref):
    for ref, here in ((mix_ref, ~late_place()), (late_ref, late_place())):

        @pl.when(here)
        def _():
            out_ref[...] = narrowed(rows_ref[part, :], ref, column_ref[part, :])


def pair_kernel(rows_ref, column_ref, two_ref, mix_ref, late_ref, send_ref, third):
    parts, count = send_ref.shape[0] + 1, send_ref.shape[1]
    third_term(slice(count, None), rows_ref, column_ref, mix_ref, late_ref, third)
    both = beside(narrowed(rows_ref[count:, :], two_ref, column_ref[count:, :]), third[...])
    for k in range(1, parts):
        send_ref[k - 1] = both[(k - 1) * count:k * count]


def swap_kernel(rows_ref, column_ref, swap_ref, pair_ref, send_ref):
    parts, count = pair_ref.shape[0] + 1, pair_ref.shape[1]
    term = narrowed(rows_ref[count:, :], swap_ref, column_ref[count:, :])
    for k in range(1, parts):
        send_ref[k - 1, :count, :] = pair_ref[k - 1]
        send_ref[k - 1, count:, :] = halved(term[(k - 1) * count:k * count])


def keep_kernel(rows_ref, column_ref, own_labels, two_ref, mix_ref, late_ref, swap_ref, two_out, mix_out, swap_out, labels_ref):
    count = two_out.shape[0]
    width = rows_ref.shape[1]
    third_term(slice(0, count), rows_ref, column_ref, mix_ref, late_ref, mix_out)
    for ref, out_ref in ((two_ref, two_out), (swap_ref, swap_out)):
        out_ref[...] = narrowed(rows_ref[:count, :], ref, column_ref[:count, :])
    two, mix, late, swap = [ref[width:width + 1, :] for ref in (two_ref, mix_ref, late_ref, swap_ref)]
    mix = jnp.where(late_place(), late, mix)
    odd = lax.rem(lax.axis_index("blk"), 2) == 1
    labels_ref[...] = jnp.concatenate([own_labels[:1, :], jnp.where(odd, mix, swap), two, jnp.where(odd, swap, mix)] * 2, axis=0)


def finish_kernel(parts, own_keep, mix_keep, two_keep, swap_keep, *refs):
    own_in, late_in = refs[:parts - 1], refs[parts - 1:2 * (parts - 1)]
    labels_ref, column_ref, out_ref, out, sems = refs[2 * (parts - 1):]
    count = own_keep.shape[0]
    rows = column_ref[:count, :]
    copies = []

    def store(m, term):
        for start in range(0, out.shape[2], LANES):
            part = slice(start, start + LANES)
            out[m, :, part] = jnp.where(rows == labels_ref[m:m + 1, part], term, 0.0)
        copies.append(pltpu.make_async_copy(out.at[m], out_ref.at[m], sems.at[m]))
        copies[-1].start()

    odd = lax.rem(lax.axis_index("blk"), 2) == 1
    store(0, sum([unhalved(ref[...]) for ref in own_in], own_keep[...]))
    pairs = [apart(ref[:count, :]) for ref in late_in]
    store(2, sum([two for two, _ in pairs], two_keep[...]))
    mix = sum([mix for _, mix in pairs], mix_keep[...])
    swap = sum([unhalved(ref[count:, :]) for ref in late_in], swap_keep[...])
    store(1, jnp.where(odd, mix, swap))
    store(3, jnp.where(odd, swap, mix))
    for copy in copies:
        copy.wait()


def whole(*shape):
    return jax.ShapeDtypeStruct(shape, F32)


def call(kernel, out_shape, args, flops, off=0, scratch=(), out_specs=ONCHIP):
    moved = sum(a.size * 4 for a in list(args) + out_shape)
    args = [pltpu.with_memory_space_constraint(a, pltpu.HBM) for a in args[:off]] + list(args[off:])
    return pl.pallas_call(
        kernel,
        out_shape=out_shape,
        in_specs=[OFFCHIP] * off + [ONCHIP] * (len(args) - off),
        out_specs=[out_specs] * len(out_shape),
        scratch_shapes=list(scratch),
        cost_estimate=pl.CostEstimate(flops=flops, bytes_accessed=moved, transcendentals=0),
        compiler_params=pltpu.CompilerParams(vmem_limit_bytes=32 * 1024 * 1024),
    )(*args)


def body(amplitudes, integrals, cd_irrep, ab_irrep, ij_irrep):
    blocks, parts = lax.axis_size("blk"), lax.axis_size("red")
    pairs, depth = amplitudes.shape
    row_count = integrals.shape[0]
    width = depth // 4
    count = row_count // parts
    one_product = 12 * row_count * width * pairs

    def moved(array, steps):
        return lax.ppermute(array, "blk", [(i, (i + steps[i % 4]) % blocks) for i in range(blocks)])

    def exchanged(array):
        return [
            lax.ppermute(array[k - 1], "red", [(i, (i + k) % parts) for i in range(parts)])
            for k in range(1, parts)
        ]

    def after(array, *earlier):
        return lax.optimization_barrier((array, *earlier))[0]

    def staging(array, labels, copies):
        return [
            pltpu.VMEM(array.shape, F32),
            pltpu.VMEM(labels.shape, jnp.int32),
            pltpu.VMEM(cd_irrep.shape, jnp.int32),
        ], pltpu.SemaphoreType.DMA((2 + copies,))

    stage, sems = staging(amplitudes, ij_irrep, 1)
    own, = call(pack_kernel, [whole(width + 8, pairs)], (amplitudes, ij_irrep, cd_irrep),
                4 * amplitudes.size, 3, stage + [sems])
    two = moved(own, (2, 2, 2, 2))
    own_labels, = call(labels_kernel, [whole(8, pairs)], (own,), 8 * pairs)
    mix = moved(after(own, own_labels), (1, 3, 1, -1))
    stage, sems = staging(integrals, ab_irrep, parts)
    rows, labels = call(
        functools.partial(first_kernel, count), [whole(row_count, width), whole(row_count, LANES)],
        (integrals, ab_irrep, cd_irrep), 64 * one_product, 3, stage + [pltpu.VMEM((row_count, LANES), F32), sems])
    own_keep, own_send = call(
        own_kernel, [whole(count, LANES), whole(parts - 1, count // 2, LANES)],
        (rows, labels, own), one_product)
    own_in = exchanged(own_send)
    late = moved(after(own, own_keep, mix), (1, -1, 1, 3))
    swap = moved(after(two, *own_in), (1, -1, 1, -1))
    pair_send, = call(pair_kernel, [whole(parts - 1, count, LANES)], (rows, labels, two, mix, late), one_product, 0,
                      [pltpu.VMEM((row_count - count, LANES), F32)])
    late_send, = call(swap_kernel, [whole(parts - 1, count + count // 2, LANES)],
                      (rows, labels, swap, pair_send), one_product // 2)
    late_in = exchanged(late_send)
    two_keep, mix_keep, swap_keep, slab_labels = call(
        keep_kernel, [whole(count, LANES)] * 3 + [whole(8, pairs)],
        (rows, labels, own_labels, two, mix, late, after(swap, late_send)), one_product)
    out, = call(functools.partial(finish_kernel, parts), [whole(4, count, pairs)],
                (own_keep, mix_keep, two_keep, swap_keep, *own_in, *late_in, slab_labels, labels),
                4 * 2 * count * pairs, 0, [pltpu.VMEM((4, count, pairs), F32), pltpu.SemaphoreType.DMA((4,))], OFFCHIP)
    return out


def solution(mesh):
    in_specs = (P("blk", "red"), P("blk", "red"), P("red", None), P("blk", None), P("blk", None))
    out_specs = P(None, ("blk", "red"), None)
    return jax.shard_map(body, mesh=mesh, in_specs=in_specs, out_specs=out_specs, check_vma=False)
```

```python
import functools
import jax
import jax.numpy as jnp
from jax import lax
from jax.experimental import pallas as pl
from jax.experimental.pallas import tpu as pltpu
from jax.sharding import PartitionSpec as P

LANES = 128
F32 = jnp.float32
ONCHIP = pl.BlockSpec(memory_space=pltpu.VMEM)
OFFCHIP = pl.BlockSpec(memory_space=pltpu.HBM)


def column(labels):
    return jnp.broadcast_to(labels.astype(F32), (LANES, labels.shape[1])).T


def fold(rows, row_labels, cd_labels):
    tiles = rows.shape[1] // LANES
    kept = [
        jnp.where(row_labels == cd_labels[:, k * LANES:(k + 1) * LANES], rows[:, k * LANES:(k + 1) * LANES], 0.0)
        for k in range(tiles)
    ]
    kept = [kept[k] + kept[k + tiles // 2] for k in range(tiles // 2)]
    low = lower(kept[0].shape)
    first, middle, last = kept
    middle_turned, last_turned = turned(middle), turned(last)
    return first + jnp.where(low, middle_turned, last_turned), middle + last_turned


def lower(shape):
    return lax.broadcasted_iota(jnp.int32, shape, 1) < LANES // 2


def turned(array):
    return pltpu.roll(array, LANES // 2, 1)


def fetch(pairs, sems):
    copies = [pltpu.make_async_copy(src, dst, sems.at[i]) for i, (src, dst) in enumerate(pairs)]
    for copy in copies:
        copy.start()
    return copies


def pack_kernel(amp_ref, ij_ref, cd_ref, out_ref, amp, ij, cd, sems):
    pairs, width = amp.shape[0], out_ref.shape[0] - 8
    copies = fetch([(amp_ref, amp), (ij_ref, ij), (cd_ref, cd)], sems)
    copies[1].wait()
    copies[2].wait()
    rows = column(ij[...])
    labels = cd[...].astype(F32)
    out_ref[width:, :] = jnp.broadcast_to(ij[...].astype(F32), (8, pairs))
    copies[0].wait()
    for start in range(0, pairs, LANES):
        part = slice(start, start + LANES)
        first, second = fold(amp[part, :], rows[part], labels)
        out_ref[:LANES, part] = first.T
        out_ref[LANES:width, part] = second.T[:width - LANES]


def narrowed(rows, slab_ref, row_labels):
    width = rows.shape[1]
    full = jnp.dot(rows, slab_ref[:width, :], precision=lax.Precision.HIGHEST, preferred_element_type=F32)
    labels = slab_ref[width:width + 1, :]
    total = None
    for start in range(0, full.shape[1], LANES):
        part = slice(start, start + LANES)
        kept = jnp.where(row_labels == labels[:, part], full[:, part], 0.0)
        total = kept if total is None else total + kept
    return total + turned(total)


def beside(one, other):
    return jnp.where(lower(one.shape), one, other)


def apart(array):
    low, other = lower(array.shape), turned(array)
    return jnp.where(low, array, other), jnp.where(low, other, array)


def halved(term):
    half = term.shape[0] // 2
    return beside(term[:half], term[half:])


def unhalved(term):
    return jnp.concatenate(apart(term), axis=0)


def first_kernel(count, v_ref, ab_ref, cd_ref, rows_ref, column_ref, v, ab, cd, labels, sems):
    width, parts = rows_ref.shape[1], v.shape[0] // count
    mine = lax.axis_index("red")
    places = [pl.ds(pl.multiple_of(lax.rem(mine + k, parts) * count, count), count) for k in range(parts)]
    held = [pl.ds(k * count, count) for k in range(parts)]
    copies = fetch([(ab_ref, ab), (cd_ref, cd)] + [(v_ref.at[p], v.at[h]) for p, h in zip(places, held)], sems)
    copies[0].wait()
    copies[1].wait()
    labels[...] = column(ab[...])
    cd_labels = cd[...].astype(F32)
    for copy, p, h in zip(copies[2:], places, held):
        column_ref[h, :] = labels[p, :]
        copy.wait()
        first, second = fold(v[h, :], column_ref[h, :], cd_labels)
        rows_ref[h, :LANES] = first
        rows_ref[h, LANES:] = second[:, :width - LANES]


def labels_kernel(slab_ref, out_ref):
    out_ref[...] = slab_ref[slab_ref.shape[0] - 8:, :]


def own_kernel(rows_ref, column_ref, own_ref, keep_ref, send_ref):
    count = keep_ref.shape[0]
    term = narrowed(rows_ref[...], own_ref, column_ref[...])
    keep_ref[...] = term[:count]
    for k in range(1, send_ref.shape[0] + 1):
        send_ref[k - 1] = halved(term[k * count:(k + 1) * count])


def late_place():
    return lax.rem(lax.axis_index("blk"), 4) == 2


def near_kernel(rows_ref, column_ref, near_ref, out_ref):
    count = rows_ref.shape[0] - out_ref.shape[0]
    out_ref[...] = narrowed(rows_ref[count:, :], near_ref, column_ref[count:, :])


def pair_kernel(rows_ref, column_ref, near_ref, mix_ref, late_ref, send_ref):
    parts, count = send_ref.shape[0] + 1, send_ref.shape[1]
    for ref, here in ((mix_ref, ~late_place()), (late_ref, late_place())):

        @pl.when(here)
        def _():
            both = beside(near_ref[...], narrowed(rows_ref[count:, :], ref, column_ref[count:, :]))
            for k in range(1, parts):
                send_ref[k - 1] = both[(k - 1) * count:k * count]


def swap_kernel(rows_ref, column_ref, swap_ref, pair_ref, send_ref):
    parts, count = pair_ref.shape[0] + 1, pair_ref.shape[1]
    term = narrowed(rows_ref[count:, :], swap_ref, column_ref[count:, :])
    for k in range(1, parts):
        send_ref[k - 1, :count, :] = pair_ref[k - 1]
        send_ref[k - 1, count:, :] = halved(term[(k - 1) * count:k * count])


def keep_kernel(rows_ref, column_ref, own_labels, near_ref, mix_ref, late_ref, swap_ref, near_out, mix_out, swap_out, labels_ref):
    count = near_out.shape[0]
    width = rows_ref.shape[1]
    rows, labels = rows_ref[:count, :], column_ref[:count, :]
    for ref, out_ref in ((near_ref, near_out), (mix_ref, mix_out), (swap_ref, swap_out)):
        out_ref[...] = narrowed(rows, ref, labels)

    @pl.when(late_place())
    def _():
        mix_out[...] = narrowed(rows, late_ref, labels)

    near, mix, late, swap = [ref[width:width + 1, :] for ref in (near_ref, mix_ref, late_ref, swap_ref)]
    mix = jnp.where(late_place(), late, mix)
    odd = lax.rem(lax.axis_index("blk"), 2) == 1
    labels_ref[...] = jnp.concatenate([own_labels[:1, :], jnp.where(odd, mix, near), swap, jnp.where(odd, near, mix)] * 2, axis=0)


def finish_kernel(parts, own_keep, near_keep, mix_keep, swap_keep, *refs):
    own_in, late_in = refs[:parts - 1], refs[parts - 1:2 * (parts - 1)]
    labels_ref, column_ref, out_ref, out, sems = refs[2 * (parts - 1):]
    count = own_keep.shape[0]
    rows = column_ref[:count, :]
    copies = []

    def store(m, term):
        for start in range(0, out.shape[2], LANES):
            part = slice(start, start + LANES)
            out[m, :, part] = jnp.where(rows == labels_ref[m:m + 1, part], term, 0.0)
        copies.append(pltpu.make_async_copy(out.at[m], out_ref.at[m], sems.at[m]))
        copies[-1].start()

    odd = lax.rem(lax.axis_index("blk"), 2) == 1
    store(0, sum([unhalved(ref[...]) for ref in own_in], own_keep[...]))
    store(2, sum([unhalved(ref[count:, :]) for ref in late_in], swap_keep[...]))
    pairs = [apart(ref[:count, :]) for ref in late_in]
    near = sum([near for near, _ in pairs], near_keep[...])
    mix = sum([mix for _, mix in pairs], mix_keep[...])
    store(1, jnp.where(odd, mix, near))
    store(3, jnp.where(odd, near, mix))
    for copy in copies:
        copy.wait()


def whole(*shape):
    return jax.ShapeDtypeStruct(shape, F32)


def call(kernel, out_shape, args, flops, off=0, scratch=(), out_specs=ONCHIP):
    moved = sum(a.size * 4 for a in list(args) + out_shape)
    args = [pltpu.with_memory_space_constraint(a, pltpu.HBM) for a in args[:off]] + list(args[off:])
    return pl.pallas_call(
        kernel,
        out_shape=out_shape,
        in_specs=[OFFCHIP] * off + [ONCHIP] * (len(args) - off),
        out_specs=[out_specs] * len(out_shape),
        scratch_shapes=list(scratch),
        cost_estimate=pl.CostEstimate(flops=flops, bytes_accessed=moved, transcendentals=0),
        compiler_params=pltpu.CompilerParams(vmem_limit_bytes=32 * 1024 * 1024),
    )(*args)


def body(amplitudes, integrals, cd_irrep, ab_irrep, ij_irrep):
    blocks, parts = lax.axis_size("blk"), lax.axis_size("red")
    pairs, depth = amplitudes.shape
    row_count = integrals.shape[0]
    width = depth // 4
    count = row_count // parts
    one_product = 12 * row_count * width * pairs

    def moved(array, steps):
        return lax.ppermute(array, "blk", [(i, (i + steps[i % 4]) % blocks) for i in range(blocks)])

    def exchanged(array):
        return [
            lax.ppermute(array[k - 1], "red", [(i, (i + k) % parts) for i in range(parts)])
            for k in range(1, parts)
        ]

    def after(array, *earlier):
        return lax.optimization_barrier((array, *earlier))[0]

    def staging(array, labels, copies):
        return [
            pltpu.VMEM(array.shape, F32),
            pltpu.VMEM(labels.shape, jnp.int32),
            pltpu.VMEM(cd_irrep.shape, jnp.int32),
        ], pltpu.SemaphoreType.DMA((2 + copies,))

    stage, sems = staging(amplitudes, ij_irrep, 1)
    own, = call(pack_kernel, [whole(width + 8, pairs)], (amplitudes, ij_irrep, cd_irrep),
                4 * amplitudes.size, 3, stage + [sems])
    near = moved(own, (3, 1, 3, 1))
    own_labels, = call(labels_kernel, [whole(8, pairs)], (own,), 8 * pairs)
    mix = moved(after(own, own_labels), (1, 3, 1, -1))
    stage, sems = staging(integrals, ab_irrep, parts)
    rows, labels = call(
        functools.partial(first_kernel, count), [whole(row_count, width), whole(row_count, LANES)],
        (integrals, ab_irrep, cd_irrep), 64 * one_product, 3, stage + [pltpu.VMEM((row_count, LANES), F32), sems])
    own_keep, own_send = call(
        own_kernel, [whole(count, LANES), whole(parts - 1, count // 2, LANES)],
        (rows, labels, own), one_product)
    own_in = exchanged(own_send)
    late = moved(after(own, own_keep, mix), (1, -1, 1, 3))
    swap = moved(after(near, *own_in), (1, -1, 1, -1))
    near_term, = call(near_kernel, [whole(row_count - count, LANES)], (rows, labels, near), one_product)
    pair_send, = call(pair_kernel, [whole(parts - 1, count, LANES)], (rows, labels, near_term, mix, late), one_product)
    late_send, = call(swap_kernel, [whole(parts - 1, count + count // 2, LANES)],
                      (rows, labels, swap, pair_send), one_product)
    late_in = exchanged(late_send)
    near_keep, mix_keep, swap_keep, slab_labels = call(
        keep_kernel, [whole(count, LANES)] * 3 + [whole(8, pairs)],
        (rows, labels, own_labels, near, mix, late, after(swap, late_send)), one_product)
    out, = call(functools.partial(finish_kernel, parts), [whole(4, count, pairs)],
                (own_keep, near_keep, mix_keep, swap_keep, *own_in, *late_in, slab_labels, labels),
                4 * 2 * count * pairs, 0, [pltpu.VMEM((4, count, pairs), F32), pltpu.SemaphoreType.DMA((4,))], OFFCHIP)
    return out


def solution(mesh):
    in_specs = (P("blk", "red"), P("blk", "red"), P("red", None), P("blk", None), P("blk", None))
    out_specs = P(None, ("blk", "red"), None)
    return jax.shard_map(body, mesh=mesh, in_specs=in_specs, out_specs=out_specs, check_vma=False)
```

```python
import functools
import jax
import jax.numpy as jnp
from jax import lax
from jax.experimental import pallas as pl
from jax.experimental.pallas import tpu as pltpu
from jax.sharding import PartitionSpec as P

LANES = 128
F32 = jnp.float32
ONCHIP = pl.BlockSpec(memory_space=pltpu.VMEM)
OFFCHIP = pl.BlockSpec(memory_space=pltpu.HBM)


def column(labels):
    return jnp.broadcast_to(labels.astype(F32), (LANES, labels.shape[1])).T


def fold(rows, row_labels, cd_labels):
    tiles = rows.shape[1] // LANES
    kept = [
        jnp.where(row_labels == cd_labels[:, k * LANES:(k + 1) * LANES], rows[:, k * LANES:(k + 1) * LANES], 0.0)
        for k in range(tiles)
    ]
    kept = [kept[k] + kept[k + tiles // 2] for k in range(tiles // 2)]
    low = lower(kept[0].shape)
    first, middle, last = kept
    middle_turned, last_turned = turned(middle), turned(last)
    return first + jnp.where(low, middle_turned, last_turned), middle + last_turned


def lower(shape):
    return lax.broadcasted_iota(jnp.int32, shape, 1) < LANES // 2


def turned(array):
    return pltpu.roll(array, LANES // 2, 1)


def fetch(pairs, sems):
    copies = [pltpu.make_async_copy(src, dst, sems.at[i]) for i, (src, dst) in enumerate(pairs)]
    for copy in copies:
        copy.start()
    return copies


def pack_kernel(amp_ref, ij_ref, cd_ref, out_ref, amp, ij, cd, sems):
    pairs, width = amp.shape[0], out_ref.shape[0] - 8
    parts = [slice(start, start + LANES) for start in range(0, pairs, LANES)]
    copies = fetch([(ij_ref, ij), (cd_ref, cd)] + [(amp_ref.at[part], amp.at[part]) for part in parts], sems)
    copies[0].wait()
    copies[1].wait()
    rows = column(ij[...])
    labels = cd[...].astype(F32)
    out_ref[width:, :] = jnp.broadcast_to(ij[...].astype(F32), (8, pairs))
    for copy, part in zip(copies[2:], parts):
        copy.wait()
        first, second = fold(amp[part, :], rows[part], labels)
        out_ref[:LANES, part] = first.T
        out_ref[LANES:width, part] = second.T[:width - LANES]


def narrowed(rows, slab_ref, row_labels):
    width = rows.shape[1]
    full = jnp.dot(rows, slab_ref[:width, :], precision=lax.Precision.HIGHEST, preferred_element_type=F32)
    labels = slab_ref[width:width + 1, :]
    total = None
    for start in range(0, full.shape[1], LANES):
        part = slice(start, start + LANES)
        kept = jnp.where(row_labels == labels[:, part], full[:, part], 0.0)
        total = kept if total is None else total + kept
    return total + turned(total)


def beside(one, other):
    return jnp.where(lower(one.shape), one, other)


def apart(array):
    low, other = lower(array.shape), turned(array)
    return jnp.where(low, array, other), jnp.where(low, other, array)


def halved(term):
    half = term.shape[0] // 2
    return beside(term[:half], term[half:])


def unhalved(term):
    return jnp.concatenate(apart(term), axis=0)


def first_kernel(count, v_ref, ab_ref, cd_ref, rows_ref, column_ref, v, ab, cd, labels, sems):
    width, parts = rows_ref.shape[1], v.shape[0] // count
    mine = lax.axis_index("red")
    places = [pl.ds(pl.multiple_of(lax.rem(mine + k, parts) * count, count), count) for k in range(parts)]
    held = [pl.ds(k * count, count) for k in range(parts)]
    copies = fetch([(ab_ref, ab), (cd_ref, cd)] + [(v_ref.at[p], v.at[h]) for p, h in zip(places, held)], sems)
    copies[0].wait()
    copies[1].wait()
    labels[...] = column(ab[...])
    cd_labels = cd[...].astype(F32)
    for copy, p, h in zip(copies[2:], places, held):
        column_ref[h, :] = labels[p, :]
        copy.wait()
        first, second = fold(v[h, :], column_ref[h, :], cd_labels)
        rows_ref[h, :LANES] = first
        rows_ref[h, LANES:] = second[:, :width - LANES]


def labels_kernel(slab_ref, out_ref):
    out_ref[...] = slab_ref[slab_ref.shape[0] - 8:, :]


def own_kernel(rows_ref, column_ref, own_ref, keep_ref, send_ref):
    count = keep_ref.shape[0]
    term = narrowed(rows_ref[...], own_ref, column_ref[...])
    keep_ref[...] = term[:count]
    for k in range(1, send_ref.shape[0] + 1):
        send_ref[k - 1] = halved(term[k * count:(k + 1) * count])


def place():
    return lax.rem(lax.axis_index("blk"), 4)


def chosen(second, one, other, out_ref, rows, labels):
    for ref, here in ((one, ~second), (other, second)):

        @pl.when(here)
        def _():
            out_ref[...] = narrowed(rows, ref, labels)


def one_kernel(rows_ref, column_ref, one_ref, out_ref):
    count = rows_ref.shape[0] - out_ref.shape[0]
    out_ref[...] = narrowed(rows_ref[count:, :], one_ref, column_ref[count:, :])


def pair_kernel(rows_ref, column_ref, one_term, three_ref, late_ref, send_ref, third):
    parts, count = send_ref.shape[0] + 1, send_ref.shape[1]
    chosen(place() == 2, three_ref, late_ref, third, rows_ref[count:, :], column_ref[count:, :])
    both = beside(one_term[...], third[...])
    for k in range(1, parts):
        send_ref[k - 1] = both[(k - 1) * count:k * count]


def last_kernel(rows_ref, column_ref, from_one, from_three, pair_ref, send_ref, two):
    parts, count = pair_ref.shape[0] + 1, pair_ref.shape[1]
    chosen(lax.rem(place(), 2) == 1, from_three, from_one, two, rows_ref[count:, :], column_ref[count:, :])
    for k in range(1, parts):
        send_ref[k - 1, :count, :] = pair_ref[k - 1]
        send_ref[k - 1, count:, :] = halved(two[(k - 1) * count:k * count, :])


def keep_kernel(rows_ref, column_ref, own_labels, one_ref, three_ref, late_ref, from_one, from_three, *out_refs):
    one_out, two_out, three_out, labels_ref = out_refs
    count = one_out.shape[0]
    width = rows_ref.shape[1]
    rows, labels = rows_ref[:count, :], column_ref[:count, :]
    odd, second = lax.rem(place(), 2) == 1, place() == 2
    one_out[...] = narrowed(rows, one_ref, labels)
    chosen(odd, from_three, from_one, two_out, rows, labels)
    chosen(second, three_ref, late_ref, three_out, rows, labels)
    one, three, late, even_two, odd_two = [
        ref[width:width + 1, :] for ref in (one_ref, three_ref, late_ref, from_three, from_one)
    ]
    two, three = jnp.where(odd, odd_two, even_two), jnp.where(second, late, three)
    labels_ref[...] = jnp.concatenate([own_labels[:1, :], one, two, three] * 2, axis=0)


def finish_kernel(parts, own_keep, one_keep, two_keep, three_keep, *refs):
    own_in, late_in = refs[:parts - 1], refs[parts - 1:2 * (parts - 1)]
    labels_ref, column_ref, out_ref, out, sems = refs[2 * (parts - 1):]
    count = own_keep.shape[0]
    rows = column_ref[:count, :]
    copies = []

    def store(m, term):
        for start in range(0, out.shape[2], LANES):
            part = slice(start, start + LANES)
            out[m, :, part] = jnp.where(rows == labels_ref[m:m + 1, part], term, 0.0)
        copies.append(pltpu.make_async_copy(out.at[m], out_ref.at[m], sems.at[m]))
        copies[-1].start()

    store(0, sum([unhalved(ref[...]) for ref in own_in], own_keep[...]))
    store(2, sum([unhalved(ref[count:, :]) for ref in late_in], two_keep[...]))
    pairs = [apart(ref[:count, :]) for ref in late_in]
    store(1, sum([one for one, _ in pairs], one_keep[...]))
    store(3, sum([three for _, three in pairs], three_keep[...]))
    for copy in copies:
        copy.wait()


def whole(*shape):
    return jax.ShapeDtypeStruct(shape, F32)


def call(kernel, out_shape, args, flops, off=0, scratch=(), out_specs=ONCHIP):
    moved = sum(a.size * 4 for a in list(args) + out_shape)
    args = [pltpu.with_memory_space_constraint(a, pltpu.HBM) for a in args[:off]] + list(args[off:])
    return pl.pallas_call(
        kernel,
        out_shape=out_shape,
        in_specs=[OFFCHIP] * off + [ONCHIP] * (len(args) - off),
        out_specs=[out_specs] * len(out_shape),
        scratch_shapes=list(scratch),
        cost_estimate=pl.CostEstimate(flops=flops, bytes_accessed=moved, transcendentals=0),
        compiler_params=pltpu.CompilerParams(vmem_limit_bytes=32 * 1024 * 1024),
    )(*args)


def body(amplitudes, integrals, cd_irrep, ab_irrep, ij_irrep):
    blocks, parts = lax.axis_size("blk"), lax.axis_size("red")
    pairs, depth = amplitudes.shape
    row_count = integrals.shape[0]
    width = depth // 4
    count = row_count // parts
    one_product = 12 * row_count * width * pairs

    def moved(array, steps):
        return lax.ppermute(array, "blk", [(i, (i + steps[i % 4]) % blocks) for i in range(blocks)])

    def exchanged(array):
        return [
            lax.ppermute(array[k - 1], "red", [(i, (i + k) % parts) for i in range(parts)])
            for k in range(1, parts)
        ]

    def after(array, *earlier):
        return lax.optimization_barrier((array, *earlier))[0]

    def staging(array, labels, copies):
        return [
            pltpu.VMEM(array.shape, F32),
            pltpu.VMEM(labels.shape, jnp.int32),
            pltpu.VMEM(cd_irrep.shape, jnp.int32),
        ], pltpu.SemaphoreType.DMA((2 + copies,))

    stage, sems = staging(amplitudes, ij_irrep, pairs // LANES)
    own, = call(pack_kernel, [whole(width + 8, pairs)], (amplitudes, ij_irrep, cd_irrep),
                4 * amplitudes.size, 3, stage + [sems])
    one = moved(own, (1, 1, 1, 1))
    own_labels, = call(labels_kernel, [whole(8, pairs)], (own,), 8 * pairs)
    three = moved(after(own, own_labels), (3, 3, 3, -1))
    stage, sems = staging(integrals, ab_irrep, parts)
    rows, labels = call(
        functools.partial(first_kernel, count), [whole(row_count, width), whole(row_count, LANES)],
        (integrals, ab_irrep, cd_irrep), 64 * one_product, 3, stage + [pltpu.VMEM((row_count, LANES), F32), sems])
    own_keep, own_send = call(
        own_kernel, [whole(count, LANES), whole(parts - 1, count // 2, LANES)],
        (rows, labels, own), one_product)
    own_in = exchanged(own_send)
    late = moved(after(own, own_keep), (1, -1, 1, 3))
    from_one = moved(one, (1, -1, 1, -1))
    from_three = moved(after(three, *own_in), (1, -1, 1, -1))
    rest = whole(row_count - count, LANES)
    one_term, = call(one_kernel, [rest], (rows, labels, one), one_product)
    pair_send, = call(pair_kernel, [whole(parts - 1, count, LANES)], (rows, labels, one_term, three, late),
                      one_product, 0, [pltpu.VMEM(rest.shape, F32)])
    late_send, = call(last_kernel, [whole(parts - 1, count + count // 2, LANES)],
                      (rows, labels, from_one, from_three, pair_send), one_product, 0, [pltpu.VMEM(rest.shape, F32)])
    late_in = exchanged(late_send)
    one_keep, two_keep, three_keep, slab_labels = call(
        keep_kernel, [whole(count, LANES)] * 3 + [whole(8, pairs)],
        (rows, labels, own_labels, one, three, late, from_one, after(from_three, late_send)), one_product)
    out, = call(functools.partial(finish_kernel, parts), [whole(4, count, pairs)],
                (own_keep, one_keep, two_keep, three_keep, *own_in, *late_in, slab_labels, labels),
                4 * 2 * count * pairs, 0, [pltpu.VMEM((4, count, pairs), F32), pltpu.SemaphoreType.DMA((4,))], OFFCHIP)
    return out


def solution(mesh):
    in_specs = (P("blk", "red"), P("blk", "red"), P("red", None), P("blk", None), P("blk", None))
    out_specs = P(None, ("blk", "red"), None)
    return jax.shard_map(body, mesh=mesh, in_specs=in_specs, out_specs=out_specs, check_vma=False)
```

```python
import functools
import jax
import jax.numpy as jnp
from jax import lax
from jax.experimental import pallas as pl
from jax.experimental.pallas import tpu as pltpu
from jax.sharding import PartitionSpec as P

LANES = 128
F32 = jnp.float32
ONCHIP = pl.BlockSpec(memory_space=pltpu.VMEM)
OFFCHIP = pl.BlockSpec(memory_space=pltpu.HBM)


def column(labels):
    return jnp.broadcast_to(labels.astype(F32), (LANES, labels.shape[1])).T


def fold(rows, row_labels, cd_labels):
    tiles = rows.shape[1] // LANES
    kept = [
        jnp.where(row_labels == cd_labels[:, k * LANES:(k + 1) * LANES], rows[:, k * LANES:(k + 1) * LANES], 0.0)
        for k in range(tiles)
    ]
    kept = [kept[k] + kept[k + tiles // 2] for k in range(tiles // 2)]
    low = lower(kept[0].shape)
    first, middle, last = kept
    middle_turned, last_turned = turned(middle), turned(last)
    return first + jnp.where(low, middle_turned, last_turned), middle + last_turned


def lower(shape):
    return lax.broadcasted_iota(jnp.int32, shape, 1) < LANES // 2


def turned(array):
    return pltpu.roll(array, LANES // 2, 1)


def fetch(pairs, sems):
    copies = [pltpu.make_async_copy(src, dst, sems.at[i]) for i, (src, dst) in enumerate(pairs)]
    for copy in copies:
        copy.start()
    return copies


def pack_kernel(amp_ref, ij_ref, cd_ref, out_ref, amp, ij, cd, sems):
    pairs, width = amp.shape[0], out_ref.shape[0] - 8
    copies = fetch([(amp_ref, amp), (ij_ref, ij), (cd_ref, cd)], sems)
    copies[1].wait()
    copies[2].wait()
    rows = column(ij[...])
    labels = cd[...].astype(F32)
    out_ref[width:, :] = jnp.broadcast_to(ij[...].astype(F32), (8, pairs))
    copies[0].wait()
    for start in range(0, pairs, LANES):
        part = slice(start, start + LANES)
        first, second = fold(amp[part, :], rows[part], labels)
        out_ref[:LANES, part] = first.T
        out_ref[LANES:width, part] = second.T[:width - LANES]


def narrowed(rows, slab_ref, row_labels):
    width = rows.shape[1]
    full = jnp.dot(rows, slab_ref[:width, :], precision=lax.Precision.HIGHEST, preferred_element_type=F32)
    labels = slab_ref[width:width + 1, :]
    total = None
    for start in range(0, full.shape[1], LANES):
        part = slice(start, start + LANES)
        kept = jnp.where(row_labels == labels[:, part], full[:, part], 0.0)
        total = kept if total is None else total + kept
    return total + turned(total)


def beside(one, other):
    return jnp.where(lower(one.shape), one, other)


def apart(array):
    low, other = lower(array.shape), turned(array)
    return jnp.where(low, array, other), jnp.where(low, other, array)


def halved(term):
    half = term.shape[0] // 2
    return beside(term[:half], term[half:])


def unhalved(term):
    return jnp.concatenate(apart(term), axis=0)


def first_kernel(count, v_ref, ab_ref, cd_ref, rows_ref, column_ref, v, ab, cd, labels, sems):
    width, parts = rows_ref.shape[1], v.shape[0] // count
    mine = lax.axis_index("red")
    places = [pl.ds(pl.multiple_of(lax.rem(mine + k, parts) * count, count), count) for k in range(parts)]
    held = [pl.ds(k * count, count) for k in range(parts)]
    copies = fetch([(ab_ref, ab), (cd_ref, cd)] + [(v_ref.at[p], v.at[h]) for p, h in zip(places, held)], sems)
    copies[0].wait()
    copies[1].wait()
    labels[...] = column(ab[...])
    cd_labels = cd[...].astype(F32)
    for copy, p, h in zip(copies[2:], places, held):
        column_ref[h, :] = labels[p, :]
        copy.wait()
        first, second = fold(v[h, :], column_ref[h, :], cd_labels)
        rows_ref[h, :LANES] = first
        rows_ref[h, LANES:] = second[:, :width - LANES]


def labels_kernel(slab_ref, out_ref):
    out_ref[...] = slab_ref[slab_ref.shape[0] - 8:, :]


def own_kernel(rows_ref, column_ref, own_ref, keep_ref, send_ref):
    count = keep_ref.shape[0]
    term = narrowed(rows_ref[...], own_ref, column_ref[...])
    keep_ref[...] = term[:count]
    for k in range(1, send_ref.shape[0] + 1):
        send_ref[k - 1] = halved(term[k * count:(k + 1) * count])


def second():
    return lax.rem(lax.axis_index("blk"), 4) == 2


def either(here, one, other, out_ref, rows, labels):
    for ref, holds in ((one, here), (other, ~here)):

        @pl.when(holds)
        def _():
            out_ref[...] = narrowed(rows, ref, labels)


def mix_kernel(rows_ref, column_ref, mix_ref, out_ref):
    count = rows_ref.shape[0] - out_ref.shape[0]
    out_ref[...] = narrowed(rows_ref[count:, :], mix_ref, column_ref[count:, :])


def early_kernel(rows_ref, column_ref, mix_term, two_ref, send_ref, term):
    parts, count = send_ref.shape[0] + 1, 2 * send_ref.shape[1]
    term[...] = mix_term[...]

    @pl.when(second())
    def _():
        term[...] = narrowed(rows_ref[count:, :], two_ref, column_ref[count:, :])

    for k in range(1, parts):
        send_ref[k - 1] = halved(term[(k - 1) * count:k * count, :])


def other_kernel(rows_ref, column_ref, two_ref, late_ref, out_ref):
    count = rows_ref.shape[0] - out_ref.shape[0]
    either(second(), late_ref, two_ref, out_ref, rows_ref[count:, :], column_ref[count:, :])


def swap_kernel(rows_ref, column_ref, swap_ref, other_ref, send_ref):
    parts, count = send_ref.shape[0] + 1, send_ref.shape[1]
    both = beside(other_ref[...], narrowed(rows_ref[count:, :], swap_ref, column_ref[count:, :]))
    for k in range(1, parts):
        send_ref[k - 1] = both[(k - 1) * count:k * count]


def keep_kernel(parts, *refs):
    early_in, refs = refs[:parts - 1], refs[parts - 1:]
    rows_ref, column_ref, own_labels, two_ref, mix_ref, late_ref, swap_ref = refs[:7]
    two_out, three_out, swap_out, labels_ref = refs[7:]
    count = two_out.shape[0]
    width = rows_ref.shape[1]
    rows, labels = rows_ref[:count, :], column_ref[:count, :]
    two_out[...] = narrowed(rows, two_ref, labels)
    swap_out[...] = narrowed(rows, swap_ref, labels)
    either(second(), late_ref, mix_ref, three_out, rows, labels)
    early = sum([unhalved(ref[...]) for ref in early_in[1:]], unhalved(early_in[0][...])) if early_in else 0.0
    two_out[...] = jnp.where(second(), two_out[...] + early, two_out[...])
    three_out[...] = jnp.where(second(), three_out[...], three_out[...] + early)
    two, mix, late, swap = [ref[width:width + 1, :] for ref in (two_ref, mix_ref, late_ref, swap_ref)]
    mix = jnp.where(second(), late, mix)
    odd = lax.rem(lax.axis_index("blk"), 2) == 1
    labels_ref[...] = jnp.concatenate([own_labels[:1, :], jnp.where(odd, mix, swap), two, jnp.where(odd, swap, mix)] * 2, axis=0)


def finish_kernel(parts, own_keep, two_keep, three_keep, swap_keep, *refs):
    own_in, late_in = refs[:parts - 1], refs[parts - 1:2 * (parts - 1)]
    labels_ref, column_ref, out_ref, out, sems = refs[2 * (parts - 1):]
    count = own_keep.shape[0]
    rows = column_ref[:count, :]
    copies = []

    def store(m, term):
        for start in range(0, out.shape[2], LANES):
            part = slice(start, start + LANES)
            out[m, :, part] = jnp.where(rows == labels_ref[m:m + 1, part], term, 0.0)
        copies.append(pltpu.make_async_copy(out.at[m], out_ref.at[m], sems.at[m]))
        copies[-1].start()

    odd = lax.rem(lax.axis_index("blk"), 2) == 1
    store(0, sum([unhalved(ref[...]) for ref in own_in], own_keep[...]))
    pairs = [apart(ref[...]) for ref in late_in]
    two, three = two_keep[...], three_keep[...]
    store(2, jnp.where(second(), two, sum([other for other, _ in pairs], two)))
    mix = jnp.where(second(), sum([other for other, _ in pairs], three), three)
    swap = sum([swap for _, swap in pairs], swap_keep[...])
    store(1, jnp.where(odd, mix, swap))
    store(3, jnp.where(odd, swap, mix))
    for copy in copies:
        copy.wait()


def whole(*shape):
    return jax.ShapeDtypeStruct(shape, F32)


def call(kernel, out_shape, args, flops, off=0, scratch=(), out_specs=ONCHIP):
    moved = sum(a.size * 4 for a in list(args) + out_shape)
    args = [pltpu.with_memory_space_constraint(a, pltpu.HBM) for a in args[:off]] + list(args[off:])
    return pl.pallas_call(
        kernel,
        out_shape=out_shape,
        in_specs=[OFFCHIP] * off + [ONCHIP] * (len(args) - off),
        out_specs=[out_specs] * len(out_shape),
        scratch_shapes=list(scratch),
        cost_estimate=pl.CostEstimate(flops=flops, bytes_accessed=moved, transcendentals=0),
        compiler_params=pltpu.CompilerParams(vmem_limit_bytes=32 * 1024 * 1024),
    )(*args)


def body(amplitudes, integrals, cd_irrep, ab_irrep, ij_irrep):
    blocks, parts = lax.axis_size("blk"), lax.axis_size("red")
    pairs, depth = amplitudes.shape
    row_count = integrals.shape[0]
    width = depth // 4
    count = row_count // parts
    one_product = 12 * row_count * width * pairs

    def moved(array, steps):
        return lax.ppermute(array, "blk", [(i, (i + steps[i % 4]) % blocks) for i in range(blocks)])

    def exchanged(array):
        return [
            lax.ppermute(array[k - 1], "red", [(i, (i + k) % parts) for i in range(parts)])
            for k in range(1, parts)
        ]

    def after(array, *earlier):
        return lax.optimization_barrier((array, *earlier))[0]

    def staging(array, labels, copies):
        return [
            pltpu.VMEM(array.shape, F32),
            pltpu.VMEM(labels.shape, jnp.int32),
            pltpu.VMEM(cd_irrep.shape, jnp.int32),
        ], pltpu.SemaphoreType.DMA((2 + copies,))

    stage, sems = staging(amplitudes, ij_irrep, 1)
    own, = call(pack_kernel, [whole(width + 8, pairs)], (amplitudes, ij_irrep, cd_irrep),
                4 * amplitudes.size, 3, stage + [sems])
    two = moved(own, (2, 2, 2, 2))
    own_labels, = call(labels_kernel, [whole(8, pairs)], (own,), 8 * pairs)
    mix = moved(after(own, own_labels), (1, 3, 1, -1))
    stage, sems = staging(integrals, ab_irrep, parts)
    rows, labels = call(
        functools.partial(first_kernel, count), [whole(row_count, width), whole(row_count, LANES)],
        (integrals, ab_irrep, cd_irrep), 64 * one_product, 3, stage + [pltpu.VMEM((row_count, LANES), F32), sems])
    own_keep, own_send = call(
        own_kernel, [whole(count, LANES), whole(parts - 1, count // 2, LANES)],
        (rows, labels, own), one_product)
    own_in = exchanged(own_send)
    late = moved(after(own, own_keep, mix), (1, -1, 1, 3))
    rest = whole(row_count - count, LANES)
    mix_term, = call(mix_kernel, [rest], (rows, labels, mix), one_product)
    early_send, = call(early_kernel, [whole(parts - 1, count // 2, LANES)], (rows, labels, mix_term, two),
                       one_product, 0, [pltpu.VMEM(rest.shape, F32)])
    early_in = exchanged(early_send)
    swap = moved(after(two, mix_term, *own_in), (1, -1, 1, -1))
    other_term, = call(other_kernel, [rest], (rows, labels, two, late), one_product)
    late_send, = call(swap_kernel, [whole(parts - 1, count, LANES)], (rows, labels, swap, other_term), one_product)
    late_in = exchanged(late_send)
    two_keep, three_keep, swap_keep, slab_labels = call(
        functools.partial(keep_kernel, parts), [whole(count, LANES)] * 3 + [whole(8, pairs)],
        (*early_in, rows, labels, own_labels, two, mix, late, after(swap, late_send)), 16 * one_product)
    out, = call(functools.partial(finish_kernel, parts), [whole(4, count, pairs)],
                (own_keep, two_keep, three_keep, swap_keep, *own_in, *late_in, slab_labels, labels),
                4 * 2 * count * pairs, 0, [pltpu.VMEM((4, count, pairs), F32), pltpu.SemaphoreType.DMA((4,))], OFFCHIP)
    return out


def solution(mesh):
    in_specs = (P("blk", "red"), P("blk", "red"), P("red", None), P("blk", None), P("blk", None))
    out_specs = P(None, ("blk", "red"), None)
    return jax.shard_map(body, mesh=mesh, in_specs=in_specs, out_specs=out_specs, check_vma=False)
```

```python
import functools
import jax
import jax.numpy as jnp
from jax import lax
from jax.experimental import pallas as pl
from jax.experimental.pallas import tpu as pltpu
from jax.sharding import PartitionSpec as P

LANES = 128
F32 = jnp.float32
ONCHIP = pl.BlockSpec(memory_space=pltpu.VMEM)
OFFCHIP = pl.BlockSpec(memory_space=pltpu.HBM)


def column(labels):
    return jnp.broadcast_to(labels.astype(F32), (LANES, labels.shape[1])).T


def fold(rows, row_labels, cd_labels):
    tiles = rows.shape[1] // LANES
    kept = [
        jnp.where(row_labels == cd_labels[:, k * LANES:(k + 1) * LANES], rows[:, k * LANES:(k + 1) * LANES], 0.0)
        for k in range(tiles)
    ]
    kept = [kept[k] + kept[k + tiles // 2] for k in range(tiles // 2)]
    low = lower(kept[0].shape)
    first, middle, last = kept
    middle_turned, last_turned = turned(middle), turned(last)
    return first + jnp.where(low, middle_turned, last_turned), middle + last_turned


def lower(shape):
    return lax.broadcasted_iota(jnp.int32, shape, 1) < LANES // 2


def turned(array):
    return pltpu.roll(array, LANES // 2, 1)


def fetch(pairs, sems):
    copies = [pltpu.make_async_copy(src, dst, sems.at[i]) for i, (src, dst) in enumerate(pairs)]
    for copy in copies:
        copy.start()
    return copies


def pack_kernel(amp_ref, ij_ref, cd_ref, out_ref, amp, ij, cd, sems):
    pairs, width = amp.shape[0], out_ref.shape[0] - 8
    copies = fetch([(amp_ref, amp), (ij_ref, ij), (cd_ref, cd)], sems)
    copies[1].wait()
    copies[2].wait()
    rows = column(ij[...])
    labels = cd[...].astype(F32)
    out_ref[width:, :] = jnp.broadcast_to(ij[...].astype(F32), (8, pairs))
    copies[0].wait()
    for start in range(0, pairs, LANES):
        part = slice(start, start + LANES)
        first, second = fold(amp[part, :], rows[part], labels)
        out_ref[:LANES, part] = first.T
        out_ref[LANES:width, part] = second.T[:width - LANES]


def row_labels(rows):
    tile = rows[:, -LANES:]
    return jnp.where(lower(tile.shape), turned(tile), tile)


def narrowed(rows, slab_ref):
    width = slab_ref.shape[0] - 8
    full = jnp.dot(rows[:, :width], slab_ref[:width, :], precision=lax.Precision.HIGHEST, preferred_element_type=F32)
    slab_labels, own_labels = slab_ref[width:width + 1, :], row_labels(rows)
    total = None
    for start in range(0, full.shape[1], LANES):
        part = slice(start, start + LANES)
        kept = jnp.where(own_labels == slab_labels[:, part], full[:, part], 0.0)
        total = kept if total is None else total + kept
    return total + turned(total)


def beside(one, other):
    return jnp.where(lower(one.shape), one, other)


def apart(array):
    low, other = lower(array.shape), turned(array)
    return jnp.where(low, array, other), jnp.where(low, other, array)


def halved(term):
    half = term.shape[0] // 2
    return beside(term[:half], term[half:])


def unhalved(term):
    return jnp.concatenate(apart(term), axis=0)


def odd():
    return lax.rem(lax.axis_index("blk"), 2) == 1


def first_kernel(count, v_ref, ab_ref, cd_ref, rows_ref, v, ab, cd, labels, sems):
    parts = v.shape[0] // count
    mine = lax.axis_index("red")
    places = [pl.ds(pl.multiple_of(lax.rem(mine + k, parts) * count, count), count) for k in range(parts)]
    held = [pl.ds(k * count, count) for k in range(parts)]
    copies = fetch([(ab_ref, ab), (cd_ref, cd)] + [(v_ref.at[p], v.at[h]) for p, h in zip(places, held)], sems)
    copies[0].wait()
    copies[1].wait()
    labels[...] = column(ab[...])
    cd_labels = cd[...].astype(F32)
    for copy, p, h in zip(copies[2:], places, held):
        own_labels = labels[p, :]
        copy.wait()
        leading, last = fold(v[h, :], own_labels, cd_labels)
        rows_ref[h, :LANES] = leading
        rows_ref[h, LANES:] = beside(last, own_labels)


def labels_kernel(slab_ref, out_ref):
    out_ref[...] = slab_ref[slab_ref.shape[0] - 8:, :]


def own_kernel(rows_ref, own_ref, out_ref):
    out_ref[...] = narrowed(rows_ref[...], own_ref)


def near_kernel(rows_ref, twin_ref, below_ref, own_ref, mine_out, twin_out):
    @pl.when(odd())
    def _():
        mine_out[...] = narrowed(rows_ref[...], below_ref)
        twin_out[...] = narrowed(twin_ref[...], below_ref)

    @pl.when(~odd())
    def _():
        mine_out[...] = jnp.zeros_like(mine_out)
        twin_out[...] = narrowed(twin_ref[...], own_ref)


def far_terms(part, rows_ref, twin_ref, far_ref, third_ref):
    count = rows_ref[part, :].shape[0]
    both = narrowed(jnp.concatenate([rows_ref[part, :], twin_ref[part, :]], axis=0), far_ref)
    return both[:count], both[count:], narrowed(twin_ref[part, :], third_ref)


def send_kernel(rows_ref, twin_ref, far_ref, third_ref, own_term, mine_term, twin_term, send_ref):
    parts, count = send_ref.shape[0] + 1, send_ref.shape[1] // 3
    tail = slice(count, None)
    held = [slice(k * count, (k + 1) * count) for k in range(parts - 1)]

    @pl.when(odd())
    def _():
        mine, twin, third = far_terms(tail, rows_ref, twin_ref, far_ref, third_ref)
        second, last = beside(twin_term[tail, :], twin), beside(mine, third)
        for k, h in enumerate(held):
            send_ref[k, count:2 * count, :] = second[h]
            send_ref[k, 2 * count:, :] = last[h]

    @pl.when(~odd())
    def _():
        for k in range(parts - 1):
            send_ref[k, count:2 * count, :] = twin_term[(k + 1) * count:(k + 2) * count, :]
            send_ref[k, 2 * count:, :] = jnp.zeros((count, LANES), F32)

    first = beside(own_term[tail, :], mine_term[tail, :])
    for k, h in enumerate(held):
        send_ref[k, :count, :] = first[h]


def keep_kernel(rows_ref, twin_ref, below_ref, far_ref, third_ref, own_ref, twin_term, second_out, last_out, labels_out):
    count = second_out.shape[0]
    width = own_ref.shape[0] - 8
    head = slice(0, count)

    @pl.when(odd())
    def _():
        mine, twin, third = far_terms(head, rows_ref, twin_ref, far_ref, third_ref)
        second_out[...] = beside(twin_term[head, :], twin)
        last_out[...] = beside(mine, third)

    @pl.when(~odd())
    def _():
        second_out[...] = twin_term[head, :]
        last_out[...] = jnp.zeros_like(last_out)

    own = own_ref[width:width + 1, :]
    sent = [jnp.where(odd(), ref[width:width + 1, :], own) for ref in (below_ref, far_ref, third_ref)]
    tiles = [label[:, start:start + LANES] for label in sent for start in range(0, own.shape[1], LANES)]
    labels_out[...] = jnp.concatenate((tiles * 8)[:8], axis=0)


def sum_kernel(second_keep, last_keep, labels_ref, *refs):
    taken, (cross_ref, last_out) = refs[:-2], refs[-2:]
    count = second_keep.shape[0]
    last = sum([ref[2 * count:, :] for ref in taken], last_keep[...])
    cross_ref[:count, :] = sum([ref[count:2 * count, :] for ref in taken], second_keep[...])
    cross_ref[count:count + count // 2, :] = halved(apart(last)[1])
    cross_ref[count + count // 2:, :] = labels_ref[...]
    last_out[...] = last


def finish_kernel(parts, rows_ref, own_term, mine_term, last_ref, own_labels, below_ref, far_ref, cross_ref, *refs):
    taken, (out_ref, out, sems) = refs[:parts - 1], refs[parts - 1:]
    count = last_ref.shape[0]
    width = below_ref.shape[0] - 8
    tiles = out.shape[2] // LANES
    rows = row_labels(rows_ref[:count, :])
    copies = []

    def store(m, term, labels):
        for k in range(tiles):
            out[m, :, k * LANES:(k + 1) * LANES] = jnp.where(rows == labels[k], term, 0.0)
        copies.append(pltpu.make_async_copy(out.at[m], out_ref.at[m], sems.at[m]))
        copies[-1].start()

    def of(ref, row=width):
        return [ref[row:row + 1, k * LANES:(k + 1) * LANES] for k in range(tiles)]

    def pick(one, other):
        return [jnp.where(odd(), x, y) for x, y in zip(one, other)]

    start = count + count // 2
    labels = [[cross_ref[start + i * tiles + k:start + i * tiles + k + 1, :] for k in range(tiles)] for i in range(3)]
    pairs = [apart(ref[:count, :]) for ref in taken]
    store(0, sum([own for own, _ in pairs], own_term[:count, :]), of(own_labels, 0))
    mine = sum([mine for _, mine in pairs], mine_term[:count, :])
    one, two = apart(cross_ref[:count, :])
    store(1, one, labels[0])
    store(2, jnp.where(odd(), mine, two), pick(of(below_ref), labels[1]))
    far, three = apart(last_ref[...])[0], unhalved(cross_ref[count:start, :])
    store(3, jnp.where(odd(), far, three), pick(of(far_ref), labels[2]))
    for copy in copies:
        copy.wait()


def whole(*shape):
    return jax.ShapeDtypeStruct(shape, F32)


def call(kernel, out_shape, args, flops, off=0, scratch=(), out_specs=ONCHIP):
    moved = sum(a.size * 4 for a in list(args) + out_shape)
    args = [pltpu.with_memory_space_constraint(a, pltpu.HBM) for a in args[:off]] + list(args[off:])
    return pl.pallas_call(
        kernel,
        out_shape=out_shape,
        in_specs=[OFFCHIP] * off + [ONCHIP] * (len(args) - off),
        out_specs=[out_specs] * len(out_shape),
        scratch_shapes=list(scratch),
        cost_estimate=pl.CostEstimate(flops=flops, bytes_accessed=0, transcendentals=0),
        compiler_params=pltpu.CompilerParams(vmem_limit_bytes=32 * 1024 * 1024),
    )(*args)


def body(amplitudes, integrals, cd_irrep, ab_irrep, ij_irrep):
    blocks, parts = lax.axis_size("blk"), lax.axis_size("red")
    pairs, depth = amplitudes.shape
    row_count = integrals.shape[0]
    width = depth // 4
    count = row_count // parts
    one_product = 12 * row_count * width * pairs

    def moved(array, steps):
        return lax.ppermute(array, "blk", [(i, (i + steps[i % 4]) % blocks) for i in range(blocks)])

    def exchanged(array):
        return [
            lax.ppermute(array[k - 1], "red", [(i, (i + k) % parts) for i in range(parts)])
            for k in range(1, parts)
        ]

    def after(array, *earlier):
        return lax.optimization_barrier((array, *earlier))[0]

    def staging(array, labels, copies):
        return [
            pltpu.VMEM(array.shape, F32),
            pltpu.VMEM(labels.shape, jnp.int32),
            pltpu.VMEM(cd_irrep.shape, jnp.int32),
        ], pltpu.SemaphoreType.DMA((2 + copies,))

    stage, sems = staging(amplitudes, ij_irrep, 1)
    own, = call(pack_kernel, [whole(width + 8, pairs)], (amplitudes, ij_irrep, cd_irrep),
                4 * amplitudes.size, 3, stage + [sems])
    def up(array, step):
        pairs_of = [
            ((b, r), ((b + step) % blocks, r) if b % 2 else (b, (r + 1) % parts))
            for b in range(blocks) for r in range(parts)
        ]
        return lax.ppermute(array, ("blk", "red"), [(b * parts + r, c * parts + t) for (b, r), (c, t) in pairs_of])

    below = up(own, 2)
    own_labels, = call(labels_kernel, [whole(8, pairs)], (own,), 8 * pairs)
    stage, sems = staging(integrals, ab_irrep, parts)
    rows, = call(
        functools.partial(first_kernel, count), [whole(row_count, 2 * LANES)],
        (after(integrals, own_labels), ab_irrep, cd_irrep), 0, 3,
        stage + [pltpu.VMEM((row_count, LANES), F32), sems])
    far = moved(after(own, own_labels), (3, -1, 3, -1))
    twin = moved(rows, (1, -1, 1, -1))
    term = whole(row_count, LANES)
    own_term, = call(own_kernel, [term], (rows, own), 64 * one_product)
    third = up(after(own, own_term), 4)
    mine_term, twin_term = call(near_kernel, [term, term], (rows, twin, below, own), 0)
    send, = call(send_kernel, [whole(parts - 1, 3 * count, LANES)],
                 (rows, twin, far, third, own_term, mine_term, twin_term), 0)
    taken = exchanged(send)
    second_keep, last_keep, cross_labels = call(
        keep_kernel, [whole(count, LANES), whole(count, LANES), whole(8, LANES)],
        (rows, twin, below, far, after(third, send), own, twin_term), 0)
    summed, last = call(sum_kernel, [whole(count + count // 2 + 8, LANES), whole(count, LANES)],
                        (second_keep, last_keep, cross_labels, *taken), 0)
    cross = moved(summed, (1, -1, 1, -1))
    out, = call(functools.partial(finish_kernel, parts), [whole(4, count, pairs)],
                (rows, own_term, mine_term, last, own_labels, below, far, cross, *taken),
                4 * 2 * count * pairs, 0, [pltpu.VMEM((4, count, pairs), F32), pltpu.SemaphoreType.DMA((4,))], OFFCHIP)
    return out


def solution(mesh):
    in_specs = (P("blk", "red"), P("blk", "red"), P("red", None), P("blk", None), P("blk", None))
    out_specs = P(None, ("blk", "red"), None)
    return jax.shard_map(body, mesh=mesh, in_specs=in_specs, out_specs=out_specs, check_vma=False)
```

```python
import functools
import jax
import jax.numpy as jnp
from jax import lax
from jax.experimental import pallas as pl
from jax.experimental.pallas import tpu as pltpu
from jax.sharding import PartitionSpec as P

LANES = 128
F32 = jnp.float32
ONCHIP = pl.BlockSpec(memory_space=pltpu.VMEM)
OFFCHIP = pl.BlockSpec(memory_space=pltpu.HBM)


def column(labels):
    return jnp.broadcast_to(labels.astype(F32), (LANES, labels.shape[1])).T


def fold(rows, row_labels, cd_labels):
    tiles = rows.shape[1] // LANES
    kept = [
        jnp.where(row_labels == cd_labels[:, k * LANES:(k + 1) * LANES], rows[:, k * LANES:(k + 1) * LANES], 0.0)
        for k in range(tiles)
    ]
    kept = [kept[k] + kept[k + tiles // 2] for k in range(tiles // 2)]
    low = lower(kept[0].shape)
    first, middle, last = kept
    middle_turned, last_turned = turned(middle), turned(last)
    return first + jnp.where(low, middle_turned, last_turned), middle + last_turned


def lower(shape):
    return lax.broadcasted_iota(jnp.int32, shape, 1) < LANES // 2


def turned(array):
    return pltpu.roll(array, LANES // 2, 1)


def fetch(pairs, sems):
    copies = [pltpu.make_async_copy(src, dst, sems.at[i]) for i, (src, dst) in enumerate(pairs)]
    for copy in copies:
        copy.start()
    return copies


def pack_kernel(amp_ref, ij_ref, cd_ref, out_ref, amp, ij, cd, sems):
    pairs, width = amp.shape[0], out_ref.shape[0] - 8
    copies = fetch([(amp_ref, amp), (ij_ref, ij), (cd_ref, cd)], sems)
    copies[1].wait()
    copies[2].wait()
    rows = column(ij[...])
    labels = cd[...].astype(F32)
    out_ref[width:, :] = jnp.broadcast_to(ij[...].astype(F32), (8, pairs))
    copies[0].wait()
    for start in range(0, pairs, LANES):
        part = slice(start, start + LANES)
        first, second = fold(amp[part, :], rows[part], labels)
        out_ref[:LANES, part] = first.T
        out_ref[LANES:width, part] = second.T[:width - LANES]


def row_labels(rows):
    tile = rows[:, -LANES:]
    return jnp.where(lower(tile.shape), turned(tile), tile)


def narrowed(rows, slab_ref):
    width = slab_ref.shape[0] - 8
    full = jnp.dot(rows[:, :width], slab_ref[:width, :], precision=lax.Precision.HIGHEST, preferred_element_type=F32)
    slab_labels, own_labels = slab_ref[width:width + 1, :], row_labels(rows)
    total = None
    for start in range(0, full.shape[1], LANES):
        part = slice(start, start + LANES)
        kept = jnp.where(own_labels == slab_labels[:, part], full[:, part], 0.0)
        total = kept if total is None else total + kept
    return total + turned(total)


def beside(one, other):
    return jnp.where(lower(one.shape), one, other)


def apart(array):
    low, other = lower(array.shape), turned(array)
    return jnp.where(low, array, other), jnp.where(low, other, array)


def halved(term):
    half = term.shape[0] // 2
    return beside(term[:half], term[half:])


def unhalved(term):
    return jnp.concatenate(apart(term), axis=0)


def odd():
    return lax.rem(lax.axis_index("blk"), 2) == 1


def first_kernel(count, v_ref, ab_ref, cd_ref, rows_ref, v, ab, cd, labels, sems):
    parts = v.shape[0] // count
    mine = lax.axis_index("red")
    places = [pl.ds(pl.multiple_of(lax.rem(mine + k, parts) * count, count), count) for k in range(parts)]
    held = [pl.ds(k * count, count) for k in range(parts)]
    copies = fetch([(ab_ref, ab), (cd_ref, cd)] + [(v_ref.at[p], v.at[h]) for p, h in zip(places, held)], sems)
    copies[0].wait()
    copies[1].wait()
    labels[...] = column(ab[...])
    cd_labels = cd[...].astype(F32)
    for copy, p, h in zip(copies[2:], places, held):
        own_labels = labels[p, :]
        copy.wait()
        leading, last = fold(v[h, :], own_labels, cd_labels)
        rows_ref[h, :LANES] = leading
        rows_ref[h, LANES:] = beside(last, own_labels)


def labels_kernel(slab_ref, out_ref):
    out_ref[...] = slab_ref[slab_ref.shape[0] - 8:, :]


def own_kernel(rows_ref, own_ref, out_ref):
    out_ref[...] = narrowed(rows_ref[...], own_ref)


def early_kernel(twin_ref, own_ref, own_term, twin_out, send_ref):
    parts, count = send_ref.shape[0] + 1, send_ref.shape[1]

    @pl.when(~odd())
    def _():
        twin_out[...] = narrowed(twin_ref[...], own_ref)

    @pl.when(odd())
    def _():
        twin_out[...] = jnp.zeros_like(twin_out)

    both = beside(own_term[count:, :], twin_out[count:, :])
    for k in range(parts - 1):
        send_ref[k] = both[k * count:(k + 1) * count]


def near_kernel(rows_ref, twin_ref, below_ref, mine_out, twin_out):
    @pl.when(odd())
    def _():
        mine_out[...] = narrowed(rows_ref[...], below_ref)
        twin_out[...] = narrowed(twin_ref[...], below_ref)

    @pl.when(~odd())
    def _():
        mine_out[...] = jnp.zeros_like(mine_out)
        twin_out[...] = jnp.zeros_like(twin_out)


def far_terms(part, rows_ref, twin_ref, far_ref, third_ref):
    count = rows_ref[part, :].shape[0]
    both = narrowed(jnp.concatenate([rows_ref[part, :], twin_ref[part, :]], axis=0), far_ref)
    return both[:count], both[count:], narrowed(twin_ref[part, :], third_ref)


def send_kernel(rows_ref, twin_ref, far_ref, third_ref, mine_term, twin_term, send_ref):
    parts, count = send_ref.shape[0] + 1, 2 * send_ref.shape[1] // 5
    tail = slice(count, None)

    @pl.when(odd())
    def _():
        mine, twin, third = far_terms(tail, rows_ref, twin_ref, far_ref, third_ref)
        pair, last = beside(twin_term[tail, :], twin), beside(mine, third)
        for k in range(parts - 1):
            held = slice(k * count, (k + 1) * count)
            send_ref[k, :count, :] = pair[held]
            send_ref[k, count:2 * count, :] = last[held]
            send_ref[k, 2 * count:, :] = halved(mine_term[(k + 1) * count:(k + 2) * count, :])

    @pl.when(~odd())
    def _():
        send_ref[...] = jnp.zeros_like(send_ref)


def keep_kernel(rows_ref, twin_ref, below_ref, far_ref, third_ref, own_ref, twin_term, early_term, pair_out, last_out, labels_out):
    count = pair_out.shape[0]
    width = own_ref.shape[0] - 8
    head = slice(0, count)

    @pl.when(odd())
    def _():
        mine, twin, third = far_terms(head, rows_ref, twin_ref, far_ref, third_ref)
        pair_out[...] = beside(twin_term[head, :], twin)
        last_out[...] = beside(mine, third)

    @pl.when(~odd())
    def _():
        pair_out[...] = early_term[head, :]
        last_out[...] = jnp.zeros_like(last_out)

    own = own_ref[width:width + 1, :]
    sent = [jnp.where(odd(), ref[width:width + 1, :], own) for ref in (below_ref, far_ref, third_ref)]
    tiles = [label[:, start:start + LANES] for label in sent for start in range(0, own.shape[1], LANES)]
    labels_out[...] = jnp.concatenate((tiles * 8)[:8], axis=0)


def sum_kernel(parts, pair_keep, last_keep, labels_ref, *refs):
    early_in, late_in, (cross_ref, last_out) = refs[:parts - 1], refs[parts - 1:-2], refs[-2:]
    count = pair_keep.shape[0]
    pair, last = pair_keep[...], last_keep[...]
    for early, late in zip(early_in, late_in):
        pair = pair + jnp.where(odd(), late[:count, :], apart(early[...])[1])
        last = last + late[count:2 * count, :]
    cross_ref[:count, :] = pair
    cross_ref[count:count + count // 2, :] = halved(apart(last)[1])
    cross_ref[count + count // 2:, :] = labels_ref[...]
    last_out[...] = last


def finish_kernel(parts, rows_ref, own_term, mine_term, last_ref, own_labels, below_ref, far_ref, cross_ref, *refs):
    early_in, late_in, (out_ref, out, sems) = refs[:parts - 1], refs[parts - 1:-3], refs[-3:]
    count = last_ref.shape[0]
    width = below_ref.shape[0] - 8
    tiles = out.shape[2] // LANES
    rows = row_labels(rows_ref[:count, :])
    copies = []

    def store(m, term, labels):
        for k in range(tiles):
            out[m, :, k * LANES:(k + 1) * LANES] = jnp.where(rows == labels[k], term, 0.0)
        copies.append(pltpu.make_async_copy(out.at[m], out_ref.at[m], sems.at[m]))
        copies[-1].start()

    def of(ref, row=width):
        return [ref[row:row + 1, k * LANES:(k + 1) * LANES] for k in range(tiles)]

    def pick(one, other):
        return [jnp.where(odd(), x, y) for x, y in zip(one, other)]

    start = count + count // 2
    labels = [[cross_ref[start + i * tiles + k:start + i * tiles + k + 1, :] for k in range(tiles)] for i in range(3)]
    store(0, sum([apart(ref[...])[0] for ref in early_in], own_term[:count, :]), of(own_labels, 0))
    mine = sum([unhalved(ref[2 * count:, :]) for ref in late_in], mine_term[:count, :])
    one, two = apart(cross_ref[:count, :])
    store(1, one, labels[0])
    store(2, jnp.where(odd(), mine, two), pick(of(below_ref), labels[1]))
    far, three = apart(last_ref[...])[0], unhalved(cross_ref[count:start, :])
    store(3, jnp.where(odd(), far, three), pick(of(far_ref), labels[2]))
    for copy in copies:
        copy.wait()


def whole(*shape):
    return jax.ShapeDtypeStruct(shape, F32)


def call(kernel, out_shape, args, flops, off=0, scratch=(), out_specs=ONCHIP):
    moved = sum(a.size * 4 for a in list(args) + out_shape)
    args = [pltpu.with_memory_space_constraint(a, pltpu.HBM) for a in args[:off]] + list(args[off:])
    return pl.pallas_call(
        kernel,
        out_shape=out_shape,
        in_specs=[OFFCHIP] * off + [ONCHIP] * (len(args) - off),
        out_specs=[out_specs] * len(out_shape),
        scratch_shapes=list(scratch),
        cost_estimate=pl.CostEstimate(flops=flops, bytes_accessed=0, transcendentals=0),
        compiler_params=pltpu.CompilerParams(vmem_limit_bytes=32 * 1024 * 1024),
    )(*args)


def body(amplitudes, integrals, cd_irrep, ab_irrep, ij_irrep):
    blocks, parts = lax.axis_size("blk"), lax.axis_size("red")
    pairs, depth = amplitudes.shape
    row_count = integrals.shape[0]
    width = depth // 4
    count = row_count // parts
    one_product = 12 * row_count * width * pairs

    def moved(array, steps):
        return lax.ppermute(array, "blk", [(i, (i + steps[i % 4]) % blocks) for i in range(blocks)])

    def exchanged(array):
        return [
            lax.ppermute(array[k - 1], "red", [(i, (i + k) % parts) for i in range(parts)])
            for k in range(1, parts)
        ]

    def after(array, *earlier):
        return lax.optimization_barrier((array, *earlier))[0]

    def staging(array, labels, copies):
        return [
            pltpu.VMEM(array.shape, F32),
            pltpu.VMEM(labels.shape, jnp.int32),
            pltpu.VMEM(cd_irrep.shape, jnp.int32),
        ], pltpu.SemaphoreType.DMA((2 + copies,))

    stage, sems = staging(amplitudes, ij_irrep, 1)
    own, = call(pack_kernel, [whole(width + 8, pairs)], (amplitudes, ij_irrep, cd_irrep),
                4 * amplitudes.size, 3, stage + [sems])
    def routed(array, of_odd, of_even):
        routes = [((b, r), (of_odd if b % 2 else of_even)(b, r)) for b in range(blocks) for r in range(parts)]
        return lax.ppermute(array, ("blk", "red"),
                            [(b * parts + r, c % blocks * parts + t % parts) for (b, r), (c, t) in routes])

    below = routed(own, lambda b, r: (b + 2, r), lambda b, r: (b ^ 2, r))
    own_labels, = call(labels_kernel, [whole(8, pairs)], (own,), 8 * pairs)
    stage, sems = staging(integrals, ab_irrep, parts)
    rows, = call(
        functools.partial(first_kernel, count), [whole(row_count, 2 * LANES)],
        (after(integrals, own_labels), ab_irrep, cd_irrep), 0 * one_product, 3,
        stage + [pltpu.VMEM((row_count, LANES), F32), sems])
    far = moved(after(own, own_labels), (3, -1, 3, -1))
    twin = moved(rows, (1, -1, 1, -1))
    term = whole(row_count, LANES)
    own_term, = call(own_kernel, [term], (rows, own), 64 * one_product)
    third = routed(after(own, rows), lambda b, r: (b + 4, r), lambda b, r: (b, r + 1))
    early_term, early_send = call(early_kernel, [term, whole(parts - 1, count, LANES)], (twin, own, own_term), 0)
    early_in = exchanged(early_send)
    mine_term, twin_term = call(near_kernel, [term, term], (rows, twin, after(below, *early_in)), 0)
    send, = call(send_kernel, [whole(parts - 1, 5 * count // 2, LANES)],
                 (rows, twin, far, third, mine_term, twin_term), 0)
    late_in = [
        routed(send[k - 1], lambda b, r: (b, r + k), lambda b, r: (b ^ 2, r)) for k in range(1, parts)
    ]
    pair_keep, last_keep, cross_labels = call(
        keep_kernel, [whole(count, LANES), whole(count, LANES), whole(8, LANES)],
        (rows, twin, below, far, after(third, send), own, twin_term, early_term), 0)
    summed, last = call(functools.partial(sum_kernel, parts), [whole(count + count // 2 + 8, LANES), whole(count, LANES)],
                        (pair_keep, last_keep, cross_labels, *early_in, *late_in), 0)
    cross = moved(summed, (1, -1, 1, -1))
    out, = call(functools.partial(finish_kernel, parts), [whole(4, count, pairs)],
                (rows, own_term, mine_term, last, own_labels, below, far, cross, *early_in, *late_in),
                4 * 2 * count * pairs, 0, [pltpu.VMEM((4, count, pairs), F32), pltpu.SemaphoreType.DMA((4,))], OFFCHIP)
    return out


def solution(mesh):
    in_specs = (P("blk", "red"), P("blk", "red"), P("red", None), P("blk", None), P("blk", None))
    out_specs = P(None, ("blk", "red"), None)
    return jax.shard_map(body, mesh=mesh, in_specs=in_specs, out_specs=out_specs, check_vma=False)
```

```python
import functools
import jax
import jax.numpy as jnp
from jax import lax
from jax.experimental import pallas as pl
from jax.experimental.pallas import tpu as pltpu
from jax.sharding import PartitionSpec as P

LANES = 128
F32 = jnp.float32
ONCHIP = pl.BlockSpec(memory_space=pltpu.VMEM)
OFFCHIP = pl.BlockSpec(memory_space=pltpu.HBM)


def column(labels):
    return jnp.broadcast_to(labels.astype(F32), (LANES, labels.shape[1])).T


def fold(rows, row_labels, cd_labels):
    tiles = rows.shape[1] // LANES
    kept = [
        jnp.where(row_labels == cd_labels[:, k * LANES:(k + 1) * LANES], rows[:, k * LANES:(k + 1) * LANES], 0.0)
        for k in range(tiles)
    ]
    kept = [kept[k] + kept[k + tiles // 2] for k in range(tiles // 2)]
    low = lower(kept[0].shape)
    first, middle, last = kept
    middle_turned, last_turned = turned(middle), turned(last)
    return first + jnp.where(low, middle_turned, last_turned), middle + last_turned


def lower(shape):
    return lax.broadcasted_iota(jnp.int32, shape, 1) < LANES // 2


def turned(array):
    return pltpu.roll(array, LANES // 2, 1)


def fetch(pairs, sems):
    copies = [pltpu.make_async_copy(src, dst, sems.at[i]) for i, (src, dst) in enumerate(pairs)]
    for copy in copies:
        copy.start()
    return copies


def pack_kernel(amp_ref, ij_ref, cd_ref, out_ref, amp, ij, cd, sems):
    pairs, width = amp.shape[0], out_ref.shape[0] - 8
    copies = fetch([(amp_ref, amp), (ij_ref, ij), (cd_ref, cd)], sems)
    copies[1].wait()
    copies[2].wait()
    rows = column(ij[...])
    labels = cd[...].astype(F32)
    out_ref[width:, :] = jnp.broadcast_to(ij[...].astype(F32), (8, pairs))
    copies[0].wait()
    for start in range(0, pairs, LANES):
        part = slice(start, start + LANES)
        first, second = fold(amp[part, :], rows[part], labels)
        out_ref[:LANES, part] = first.T
        out_ref[LANES:width, part] = second.T[:width - LANES]


def row_labels(rows):
    tile = rows[:, -LANES:]
    return jnp.where(lower(tile.shape), turned(tile), tile)


def narrowed(rows, slab_ref):
    width = slab_ref.shape[0] - 8
    full = jnp.dot(rows[:, :width], slab_ref[:width, :], precision=lax.Precision.HIGHEST, preferred_element_type=F32)
    slab_labels, own_labels = slab_ref[width:width + 1, :], row_labels(rows)
    total = None
    for start in range(0, full.shape[1], LANES):
        part = slice(start, start + LANES)
        kept = jnp.where(own_labels == slab_labels[:, part], full[:, part], 0.0)
        total = kept if total is None else total + kept
    return total + turned(total)


def beside(one, other):
    return jnp.where(lower(one.shape), one, other)


def apart(array):
    low, other = lower(array.shape), turned(array)
    return jnp.where(low, array, other), jnp.where(low, other, array)


def halved(term):
    half = term.shape[0] // 2
    return beside(term[:half], term[half:])


def unhalved(term):
    return jnp.concatenate(apart(term), axis=0)


def odd():
    return lax.rem(lax.axis_index("blk"), 2) == 1


def first_kernel(count, v_ref, ab_ref, cd_ref, rows_ref, v, ab, cd, labels, sems):
    parts = v.shape[0] // count
    mine = lax.axis_index("red")
    places = [pl.ds(pl.multiple_of(lax.rem(mine + k, parts) * count, count), count) for k in range(parts)]
    held = [pl.ds(k * count, count) for k in range(parts)]
    copies = fetch([(ab_ref, ab), (cd_ref, cd)] + [(v_ref.at[p], v.at[h]) for p, h in zip(places, held)], sems)
    copies[0].wait()
    copies[1].wait()
    labels[...] = column(ab[...])
    cd_labels = cd[...].astype(F32)
    for copy, p, h in zip(copies[2:], places, held):
        own_labels = labels[p, :]
        copy.wait()
        leading, last = fold(v[h, :], own_labels, cd_labels)
        rows_ref[h, :LANES] = leading
        rows_ref[h, LANES:] = beside(last, own_labels)


def labels_kernel(slab_ref, out_ref):
    out_ref[...] = slab_ref[slab_ref.shape[0] - 8:, :]


def own_kernel(rows_ref, own_ref, out_ref):
    out_ref[...] = narrowed(rows_ref[...], own_ref)


def far_kernel(rows_ref, twin_ref, far_ref, own_ref, mine_out, twin_out):
    @pl.when(odd())
    def _():
        mine_out[...] = narrowed(rows_ref[...], far_ref)
        twin_out[...] = narrowed(twin_ref[...], far_ref)

    @pl.when(~odd())
    def _():
        mine_out[...] = jnp.zeros_like(mine_out)
        twin_out[...] = narrowed(twin_ref[...], own_ref)


def near_terms(part, rows_ref, twin_ref, near_ref, third_ref):
    count = rows_ref[part, :].shape[0]
    both = narrowed(jnp.concatenate([rows_ref[part, :], twin_ref[part, :]], axis=0), near_ref)
    return both[:count], both[count:], narrowed(twin_ref[part, :], third_ref)


def send_kernel(rows_ref, twin_ref, near_ref, third_ref, own_term, mine_term, twin_term, send_ref):
    parts, count = send_ref.shape[0] + 1, send_ref.shape[1] // 3
    tail = slice(count, None)
    held = [slice(k * count, (k + 1) * count) for k in range(parts - 1)]

    @pl.when(odd())
    def _():
        mine, twin, third = near_terms(tail, rows_ref, twin_ref, near_ref, third_ref)
        second, last = beside(twin_term[tail, :], twin), beside(mine, third)
        for k, h in enumerate(held):
            send_ref[k, count:2 * count, :] = second[h]
            send_ref[k, 2 * count:, :] = last[h]

    @pl.when(~odd())
    def _():
        for k in range(parts - 1):
            send_ref[k, count:2 * count, :] = twin_term[(k + 1) * count:(k + 2) * count, :]
            send_ref[k, 2 * count:, :] = jnp.zeros((count, LANES), F32)

    first = beside(own_term[tail, :], mine_term[tail, :])
    for k, h in enumerate(held):
        send_ref[k, :count, :] = first[h]


def keep_kernel(rows_ref, twin_ref, far_ref, near_ref, third_ref, own_ref, twin_term, second_out, last_out, labels_out):
    count = second_out.shape[0]
    width = own_ref.shape[0] - 8
    head = slice(0, count)

    @pl.when(odd())
    def _():
        mine, twin, third = near_terms(head, rows_ref, twin_ref, near_ref, third_ref)
        second_out[...] = beside(twin_term[head, :], twin)
        last_out[...] = beside(mine, third)

    @pl.when(~odd())
    def _():
        second_out[...] = twin_term[head, :]
        last_out[...] = jnp.zeros_like(last_out)

    own = own_ref[width:width + 1, :]
    sent = [jnp.where(odd(), ref[width:width + 1, :], own) for ref in (far_ref, near_ref, third_ref)]
    tiles = [label[:, start:start + LANES] for label in sent for start in range(0, own.shape[1], LANES)]
    labels_out[...] = jnp.concatenate((tiles * 8)[:8], axis=0)


def sum_kernel(second_keep, last_keep, labels_ref, *refs):
    taken, (cross_ref, last_out) = refs[:-2], refs[-2:]
    count = second_keep.shape[0]
    last = sum([ref[2 * count:, :] for ref in taken], last_keep[...])
    cross_ref[:count, :] = sum([ref[count:2 * count, :] for ref in taken], second_keep[...])
    cross_ref[count:count + count // 2, :] = halved(apart(last)[1])
    cross_ref[count + count // 2:, :] = labels_ref[...]
    last_out[...] = last


def finish_kernel(parts, rows_ref, own_term, mine_term, last_ref, own_labels, far_ref, near_ref, cross_ref, *refs):
    taken, (out_ref, out, sems) = refs[:parts - 1], refs[parts - 1:]
    count = last_ref.shape[0]
    width = far_ref.shape[0] - 8
    tiles = out.shape[2] // LANES
    rows = row_labels(rows_ref[:count, :])
    copies = []

    def store(m, term, labels):
        for k in range(tiles):
            out[m, :, k * LANES:(k + 1) * LANES] = jnp.where(rows == labels[k], term, 0.0)
        copies.append(pltpu.make_async_copy(out.at[m], out_ref.at[m], sems.at[m]))
        copies[-1].start()

    def of(ref, row=width):
        return [ref[row:row + 1, k * LANES:(k + 1) * LANES] for k in range(tiles)]

    def pick(one, other):
        return [jnp.where(odd(), x, y) for x, y in zip(one, other)]

    start = count + count // 2
    labels = [[cross_ref[start + i * tiles + k:start + i * tiles + k + 1, :] for k in range(tiles)] for i in range(3)]
    pairs = [apart(ref[:count, :]) for ref in taken]
    store(0, sum([own for own, _ in pairs], own_term[:count, :]), of(own_labels, 0))
    mine = sum([mine for _, mine in pairs], mine_term[:count, :])
    two, one = apart(cross_ref[:count, :])
    store(1, one, labels[1])
    store(2, jnp.where(odd(), apart(last_ref[...])[0], two), pick(of(near_ref), labels[0]))
    store(3, jnp.where(odd(), mine, unhalved(cross_ref[count:start, :])), pick(of(far_ref), labels[2]))
    for copy in copies:
        copy.wait()


def whole(*shape):
    return jax.ShapeDtypeStruct(shape, F32)


def call(kernel, out_shape, args, flops, off=0, scratch=(), out_specs=ONCHIP):
    moved = sum(a.size * 4 for a in list(args) + out_shape)
    args = [pltpu.with_memory_space_constraint(a, pltpu.HBM) for a in args[:off]] + list(args[off:])
    return pl.pallas_call(
        kernel,
        out_shape=out_shape,
        in_specs=[OFFCHIP] * off + [ONCHIP] * (len(args) - off),
        out_specs=[out_specs] * len(out_shape),
        scratch_shapes=list(scratch),
        cost_estimate=pl.CostEstimate(flops=flops, bytes_accessed=0, transcendentals=0),
        compiler_params=pltpu.CompilerParams(vmem_limit_bytes=32 * 1024 * 1024),
    )(*args)


def body(amplitudes, integrals, cd_irrep, ab_irrep, ij_irrep):
    blocks, parts = lax.axis_size("blk"), lax.axis_size("red")
    pairs, depth = amplitudes.shape
    row_count = integrals.shape[0]
    width = depth // 4
    count = row_count // parts
    one_product = 12 * row_count * width * pairs

    def moved(array, steps):
        return lax.ppermute(array, "blk", [(i, (i + steps[i % 4]) % blocks) for i in range(blocks)])

    def exchanged(array):
        return [
            lax.ppermute(array[k - 1], "red", [(i, (i + k) % parts) for i in range(parts)])
            for k in range(1, parts)
        ]

    def after(array, *earlier):
        return lax.optimization_barrier((array, *earlier))[0]

    def staging(array, labels, copies):
        return [
            pltpu.VMEM(array.shape, F32),
            pltpu.VMEM(labels.shape, jnp.int32),
            pltpu.VMEM(cd_irrep.shape, jnp.int32),
        ], pltpu.SemaphoreType.DMA((2 + copies,))

    stage, sems = staging(amplitudes, ij_irrep, 1)
    own, = call(pack_kernel, [whole(width + 8, pairs)], (amplitudes, ij_irrep, cd_irrep),
                4 * amplitudes.size, 3, stage + [sems])
    far = moved(own, (3, -1, 3, -1))
    own_labels, = call(labels_kernel, [whole(8, pairs)], (own,), 0)
    other = moved(after(own, own_labels), (1, -1, 1, -1))
    stage, sems = staging(integrals, ab_irrep, parts)
    rows, = call(
        functools.partial(first_kernel, count), [whole(row_count, 2 * LANES)],
        (after(integrals, own_labels), ab_irrep, cd_irrep), 0, 3,
        stage + [pltpu.VMEM((row_count, LANES), F32), sems])
    near = moved(other, (3, -1, 3, -1))
    twin = moved(rows, (1, -1, 1, -1))
    term = whole(row_count, LANES)
    own_term, = call(own_kernel, [term], (rows, own), 64 * one_product)
    third = moved(after(other, own_term), (5, -1, 5, -1))
    mine_term, twin_term = call(far_kernel, [term, term], (rows, twin, far, own), 0)
    send, = call(send_kernel, [whole(parts - 1, 3 * count, LANES)],
                 (rows, twin, near, third, own_term, mine_term, twin_term), 0)
    taken = exchanged(send)
    pair_keep, last_keep, cross_labels = call(
        keep_kernel, [whole(count, LANES), whole(count, LANES), whole(8, LANES)],
        (rows, twin, far, near, after(third, send), own, twin_term), 0)
    summed, last = call(sum_kernel, [whole(count + count // 2 + 8, LANES), whole(count, LANES)],
                        (pair_keep, last_keep, cross_labels, *taken), 0)
    cross = moved(summed, (1, -1, 1, -1))
    out, = call(functools.partial(finish_kernel, parts), [whole(4, count, pairs)],
                (rows, own_term, mine_term, last, own_labels, far, near, cross, *taken),
                0, 0, [pltpu.VMEM((4, count, pairs), F32), pltpu.SemaphoreType.DMA((4,))], OFFCHIP)
    return out


def solution(mesh):
    in_specs = (P("blk", "red"), P("blk", "red"), P("red", None), P("blk", None), P("blk", None))
    out_specs = P(None, ("blk", "red"), None)
    return jax.shard_map(body, mesh=mesh, in_specs=in_specs, out_specs=out_specs, check_vma=False)
```

```python
import functools
import jax
import jax.numpy as jnp
from jax import lax
from jax.experimental import pallas as pl
from jax.experimental.pallas import tpu as pltpu
from jax.sharding import PartitionSpec as P

LANES = 128
F32 = jnp.float32
ONCHIP = pl.BlockSpec(memory_space=pltpu.VMEM)
OFFCHIP = pl.BlockSpec(memory_space=pltpu.HBM)


def column(labels):
    return jnp.broadcast_to(labels.astype(F32), (LANES, labels.shape[1])).T


def fold(rows, row_labels, cd_labels):
    tiles = rows.shape[1] // LANES
    kept = [
        jnp.where(row_labels == cd_labels[:, k * LANES:(k + 1) * LANES], rows[:, k * LANES:(k + 1) * LANES], 0.0)
        for k in range(tiles)
    ]
    kept = [kept[k] + kept[k + tiles // 2] for k in range(tiles // 2)]
    low = lower(kept[0].shape)
    first, middle, last = kept
    middle_turned, last_turned = turned(middle), turned(last)
    return first + jnp.where(low, middle_turned, last_turned), middle + last_turned


def lower(shape):
    return lax.broadcasted_iota(jnp.int32, shape, 1) < LANES // 2


def turned(array):
    return pltpu.roll(array, LANES // 2, 1)


def fetch(pairs, sems):
    copies = [pltpu.make_async_copy(src, dst, sems.at[i]) for i, (src, dst) in enumerate(pairs)]
    for copy in copies:
        copy.start()
    return copies


def pack_kernel(amp_ref, ij_ref, cd_ref, out_ref, amp, ij, cd, sems):
    pairs, width = amp.shape[0], out_ref.shape[0] - 8
    copies = fetch([(amp_ref, amp), (ij_ref, ij), (cd_ref, cd)], sems)
    copies[1].wait()
    copies[2].wait()
    rows = column(ij[...])
    labels = cd[...].astype(F32)
    out_ref[width:, :] = jnp.broadcast_to(ij[...].astype(F32), (8, pairs))
    copies[0].wait()
    for start in range(0, pairs, LANES):
        part = slice(start, start + LANES)
        first, second = fold(amp[part, :], rows[part], labels)
        out_ref[:LANES, part] = first.T
        out_ref[LANES:width, part] = second.T[:width - LANES]


def narrowed(rows, slab_ref, row_labels):
    width = rows.shape[1]
    full = jnp.dot(rows, slab_ref[:width, :], precision=lax.Precision.HIGHEST, preferred_element_type=F32)
    labels = slab_ref[width:width + 1, :]
    total = None
    for start in range(0, full.shape[1], LANES):
        part = slice(start, start + LANES)
        kept = jnp.where(row_labels == labels[:, part], full[:, part], 0.0)
        total = kept if total is None else total + kept
    return total + turned(total)


def beside(one, other):
    return jnp.where(lower(one.shape), one, other)


def apart(array):
    low, other = lower(array.shape), turned(array)
    return jnp.where(low, array, other), jnp.where(low, other, array)


def halved(term):
    half = term.shape[0] // 2
    return beside(term[:half], term[half:])


def unhalved(term):
    return jnp.concatenate(apart(term), axis=0)


def first_kernel(count, v_ref, ab_ref, cd_ref, rows_ref, column_ref, v, ab, cd, labels, sems):
    width, parts = rows_ref.shape[1], v.shape[0] // count
    mine = lax.axis_index("red")
    places = [pl.ds(pl.multiple_of(lax.rem(mine + k, parts) * count, count), count) for k in range(parts)]
    held = [pl.ds(k * count, count) for k in range(parts)]
    copies = fetch([(ab_ref, ab), (cd_ref, cd)] + [(v_ref.at[p], v.at[h]) for p, h in zip(places, held)], sems)
    copies[0].wait()
    copies[1].wait()
    labels[...] = column(ab[...])
    cd_labels = cd[...].astype(F32)
    for copy, p, h in zip(copies[2:], places, held):
        column_ref[h, :] = labels[p, :]
        copy.wait()
        first, second = fold(v[h, :], column_ref[h, :], cd_labels)
        rows_ref[h, :LANES] = first
        rows_ref[h, LANES:] = second[:, :width - LANES]


def labels_kernel(slab_ref, out_ref):
    out_ref[...] = slab_ref[slab_ref.shape[0] - 8:, :]


def own_kernel(rows_ref, column_ref, own_ref, keep_ref, send_ref):
    count = keep_ref.shape[0]
    term = narrowed(rows_ref[...], own_ref, column_ref[...])
    keep_ref[...] = term[:count]
    for k in range(1, send_ref.shape[0] + 1):
        send_ref[k - 1] = halved(term[k * count:(k + 1) * count])


def second():
    return lax.rem(lax.axis_index("blk"), 4) == 2


def either(here, one, other, out_ref, rows, labels):
    for ref, holds in ((one, here), (other, ~here)):

        @pl.when(holds)
        def _():
            out_ref[...] = narrowed(rows, ref, labels)


def sent_kernel(rows_ref, column_ref, slab_ref, out_ref):
    count = rows_ref.shape[0] - out_ref.shape[0]
    out_ref[...] = narrowed(rows_ref[count:, :], slab_ref, column_ref[count:, :])


def early_kernel(mix_term, two_term, send_ref):
    parts, count = send_ref.shape[0] + 1, 2 * send_ref.shape[1]
    term = jnp.where(second(), two_term[...], mix_term[...])
    for k in range(1, parts):
        send_ref[k - 1] = halved(term[(k - 1) * count:k * count, :])


def other_kernel(rows_ref, column_ref, two_term, late_ref, out_ref):
    count = rows_ref.shape[0] - out_ref.shape[0]
    out_ref[...] = two_term[...]

    @pl.when(second())
    def _():
        out_ref[...] = narrowed(rows_ref[count:, :], late_ref, column_ref[count:, :])


def swap_kernel(rows_ref, column_ref, swap_ref, other_ref, send_ref):
    parts, count = send_ref.shape[0] + 1, send_ref.shape[1]
    both = beside(other_ref[...], narrowed(rows_ref[count:, :], swap_ref, column_ref[count:, :]))
    for k in range(1, parts):
        send_ref[k - 1] = both[(k - 1) * count:k * count]


def keep_kernel(parts, *refs):
    early_in, refs = refs[:parts - 1], refs[parts - 1:]
    rows_ref, column_ref, own_labels, two_ref, mix_ref, late_ref, swap_ref = refs[:7]
    two_out, three_out, swap_out, labels_ref = refs[7:]
    count = two_out.shape[0]
    width = rows_ref.shape[1]
    rows, labels = rows_ref[:count, :], column_ref[:count, :]
    two_out[...] = narrowed(rows, two_ref, labels)
    swap_out[...] = narrowed(rows, swap_ref, labels)
    either(second(), late_ref, mix_ref, three_out, rows, labels)
    early = sum([unhalved(ref[...]) for ref in early_in[1:]], unhalved(early_in[0][...])) if early_in else 0.0
    two_out[...] = jnp.where(second(), two_out[...] + early, two_out[...])
    three_out[...] = jnp.where(second(), three_out[...], three_out[...] + early)
    two, mix, late, swap = [ref[width:width + 1, :] for ref in (two_ref, mix_ref, late_ref, swap_ref)]
    mix = jnp.where(second(), late, mix)
    odd = lax.rem(lax.axis_index("blk"), 2) == 1
    labels_ref[...] = jnp.concatenate([own_labels[:1, :], jnp.where(odd, mix, swap), two, jnp.where(odd, swap, mix)] * 2, axis=0)


def finish_kernel(parts, own_keep, two_keep, three_keep, swap_keep, *refs):
    own_in, late_in = refs[:parts - 1], refs[parts - 1:2 * (parts - 1)]
    labels_ref, column_ref, out_ref, out, sems = refs[2 * (parts - 1):]
    count = own_keep.shape[0]
    rows = column_ref[:count, :]
    copies = []

    def store(m, term):
        for start in range(0, out.shape[2], LANES):
            part = slice(start, start + LANES)
            out[m, :, part] = jnp.where(rows == labels_ref[m:m + 1, part], term, 0.0)
        copies.append(pltpu.make_async_copy(out.at[m], out_ref.at[m], sems.at[m]))
        copies[-1].start()

    odd = lax.rem(lax.axis_index("blk"), 2) == 1
    store(0, sum([unhalved(ref[...]) for ref in own_in], own_keep[...]))
    pairs = [apart(ref[...]) for ref in late_in]
    two, three = two_keep[...], three_keep[...]
    store(2, jnp.where(second(), two, sum([other for other, _ in pairs], two)))
    mix = jnp.where(second(), sum([other for other, _ in pairs], three), three)
    swap = sum([swap for _, swap in pairs], swap_keep[...])
    store(1, jnp.where(odd, mix, swap))
    store(3, jnp.where(odd, swap, mix))
    for copy in copies:
        copy.wait()


def whole(*shape):
    return jax.ShapeDtypeStruct(shape, F32)


def call(kernel, out_shape, args, flops, off=0, scratch=(), out_specs=ONCHIP):
    moved = sum(a.size * 4 for a in list(args) + out_shape)
    args = [pltpu.with_memory_space_constraint(a, pltpu.HBM) for a in args[:off]] + list(args[off:])
    return pl.pallas_call(
        kernel,
        out_shape=out_shape,
        in_specs=[OFFCHIP] * off + [ONCHIP] * (len(args) - off),
        out_specs=[out_specs] * len(out_shape),
        scratch_shapes=list(scratch),
        cost_estimate=pl.CostEstimate(flops=flops, bytes_accessed=moved, transcendentals=0),
        compiler_params=pltpu.CompilerParams(vmem_limit_bytes=32 * 1024 * 1024),
    )(*args)


def body(amplitudes, integrals, cd_irrep, ab_irrep, ij_irrep):
    blocks, parts = lax.axis_size("blk"), lax.axis_size("red")
    pairs, depth = amplitudes.shape
    row_count = integrals.shape[0]
    width = depth // 4
    count = row_count // parts
    one_product = 12 * row_count * width * pairs

    def moved(array, steps):
        return lax.ppermute(array, "blk", [(i, (i + steps[i % 4]) % blocks) for i in range(blocks)])

    def exchanged(array):
        return [
            lax.ppermute(array[k - 1], "red", [(i, (i + k) % parts) for i in range(parts)])
            for k in range(1, parts)
        ]

    def after(array, *earlier):
        return lax.optimization_barrier((array, *earlier))[0]

    def staging(array, labels, copies):
        return [
            pltpu.VMEM(array.shape, F32),
            pltpu.VMEM(labels.shape, jnp.int32),
            pltpu.VMEM(cd_irrep.shape, jnp.int32),
        ], pltpu.SemaphoreType.DMA((2 + copies,))

    stage, sems = staging(amplitudes, ij_irrep, 1)
    own, = call(pack_kernel, [whole(width + 8, pairs)], (amplitudes, ij_irrep, cd_irrep),
                4 * amplitudes.size, 3, stage + [sems])
    two = moved(own, (2, 2, 2, 2))
    own_labels, = call(labels_kernel, [whole(8, pairs)], (own,), 8 * pairs)
    mix = moved(after(own, own_labels), (1, 3, 1, -1))
    stage, sems = staging(integrals, ab_irrep, parts)
    rows, labels = call(
        functools.partial(first_kernel, count), [whole(row_count, width), whole(row_count, LANES)],
        (integrals, ab_irrep, cd_irrep), 64 * one_product, 3, stage + [pltpu.VMEM((row_count, LANES), F32), sems])
    own_keep, own_send = call(
        own_kernel, [whole(count, LANES), whole(parts - 1, count // 2, LANES)],
        (rows, labels, own), one_product)
    own_in = exchanged(own_send)
    late = moved(after(own, own_keep, mix), (1, -1, 1, 3))
    rest = whole(row_count - count, LANES)
    mix_term, = call(sent_kernel, [rest], (rows, labels, mix), one_product)
    swap = moved(after(two, mix_term, *own_in), (1, -1, 1, -1))
    two_term, = call(sent_kernel, [rest], (rows, labels, two), one_product)
    early_send, = call(early_kernel, [whole(parts - 1, count // 2, LANES)], (mix_term, two_term), 0)
    early_in = exchanged(early_send)
    other_term, = call(other_kernel, [rest], (rows, labels, two_term, late), one_product)
    late_send, = call(swap_kernel, [whole(parts - 1, count, LANES)], (rows, labels, swap, other_term), one_product)
    late_in = exchanged(late_send)
    two_keep, three_keep, swap_keep, slab_labels = call(
        functools.partial(keep_kernel, parts), [whole(count, LANES)] * 3 + [whole(8, pairs)],
        (*early_in, rows, labels, own_labels, two, mix, late, after(swap, late_send)), 16 * one_product)
    out, = call(functools.partial(finish_kernel, parts), [whole(4, count, pairs)],
                (own_keep, two_keep, three_keep, swap_keep, *own_in, *late_in, slab_labels, labels),
                4 * 2 * count * pairs, 0, [pltpu.VMEM((4, count, pairs), F32), pltpu.SemaphoreType.DMA((4,))], OFFCHIP)
    return out


def solution(mesh):
    in_specs = (P("blk", "red"), P("blk", "red"), P("red", None), P("blk", None), P("blk", None))
    out_specs = P(None, ("blk", "red"), None)
    return jax.shard_map(body, mesh=mesh, in_specs=in_specs, out_specs=out_specs, check_vma=False)
```

```python
import functools
import jax
import jax.numpy as jnp
from jax import lax
from jax.experimental import pallas as pl
from jax.experimental.pallas import tpu as pltpu
from jax.sharding import PartitionSpec as P

LANES = 128
F32 = jnp.float32
ONCHIP = pl.BlockSpec(memory_space=pltpu.VMEM)
OFFCHIP = pl.BlockSpec(memory_space=pltpu.HBM)


def column(labels):
    return jnp.broadcast_to(labels.astype(F32), (LANES, labels.shape[1])).T


def fold(rows, row_labels, cd_labels):
    tiles = rows.shape[1] // LANES
    kept = [
        jnp.where(row_labels == cd_labels[:, k * LANES:(k + 1) * LANES], rows[:, k * LANES:(k + 1) * LANES], 0.0)
        for k in range(tiles)
    ]
    kept = [kept[k] + kept[k + tiles // 2] for k in range(tiles // 2)]
    low = lower(kept[0].shape)
    first, middle, last = kept
    middle_turned, last_turned = turned(middle), turned(last)
    return first + jnp.where(low, middle_turned, last_turned), middle + last_turned


def lower(shape):
    return lax.broadcasted_iota(jnp.int32, shape, 1) < LANES // 2


def turned(array):
    return pltpu.roll(array, LANES // 2, 1)


def fetch(pairs, sems):
    copies = [pltpu.make_async_copy(src, dst, sems.at[i]) for i, (src, dst) in enumerate(pairs)]
    for copy in copies:
        copy.start()
    return copies


def pack_kernel(amp_ref, ij_ref, cd_ref, out_ref, amp, ij, cd, sems):
    pairs, width = amp.shape[0], out_ref.shape[0] - 8
    copies = fetch([(amp_ref, amp), (ij_ref, ij), (cd_ref, cd)], sems)
    copies[1].wait()
    copies[2].wait()
    rows = column(ij[...])
    labels = cd[...].astype(F32)
    out_ref[width:, :] = jnp.broadcast_to(ij[...].astype(F32), (8, pairs))
    copies[0].wait()
    for start in range(0, pairs, LANES):
        part = slice(start, start + LANES)
        first, second = fold(amp[part, :], rows[part], labels)
        out_ref[:LANES, part] = first.T
        out_ref[LANES:width, part] = second.T[:width - LANES]


def row_labels(rows):
    tile = rows[:, -LANES:]
    return jnp.where(lower(tile.shape), turned(tile), tile)


def narrowed(rows, slab_ref):
    width = slab_ref.shape[0] - 8
    full = jnp.dot(rows[:, :width], slab_ref[:width, :], precision=lax.Precision.HIGHEST, preferred_element_type=F32)
    slab_labels, own_labels = slab_ref[width:width + 1, :], row_labels(rows)
    total = None
    for start in range(0, full.shape[1], LANES):
        part = slice(start, start + LANES)
        kept = jnp.where(own_labels == slab_labels[:, part], full[:, part], 0.0)
        total = kept if total is None else total + kept
    return total + turned(total)


def beside(one, other):
    return jnp.where(lower(one.shape), one, other)


def apart(array):
    low, other = lower(array.shape), turned(array)
    return jnp.where(low, array, other), jnp.where(low, other, array)


def halved(term):
    half = term.shape[0] // 2
    return beside(term[:half], term[half:])


def unhalved(term):
    return jnp.concatenate(apart(term), axis=0)


def odd():
    return lax.rem(lax.axis_index("blk"), 2) == 1


def first_kernel(count, v_ref, ab_ref, cd_ref, rows_ref, v, ab, cd, labels, sems):
    parts = v.shape[0] // count
    mine = lax.axis_index("red")
    places = [pl.ds(pl.multiple_of(lax.rem(mine + k, parts) * count, count), count) for k in range(parts)]
    held = [pl.ds(k * count, count) for k in range(parts)]
    copies = fetch([(ab_ref, ab), (cd_ref, cd)] + [(v_ref.at[p], v.at[h]) for p, h in zip(places, held)], sems)
    copies[0].wait()
    copies[1].wait()
    labels[...] = column(ab[...])
    cd_labels = cd[...].astype(F32)
    for copy, p, h in zip(copies[2:], places, held):
        own_labels = labels[p, :]
        copy.wait()
        leading, last = fold(v[h, :], own_labels, cd_labels)
        rows_ref[h, :LANES] = leading
        rows_ref[h, LANES:] = beside(last, own_labels)


def labels_kernel(slab_ref, out_ref):
    out_ref[...] = slab_ref[slab_ref.shape[0] - 8:, :]


def second():
    return lax.rem(lax.axis_index("blk"), 4) == 2


def own_kernel(rows_ref, own_ref, keep_ref, send_ref):
    count = keep_ref.shape[0]
    term = narrowed(rows_ref[...], own_ref)
    keep_ref[...] = term[:count]
    for k in range(1, send_ref.shape[0] + 1):
        send_ref[k - 1] = halved(term[k * count:(k + 1) * count])


def sent_kernel(rows_ref, slab_ref, out_ref):
    count = rows_ref.shape[0] - out_ref.shape[0]
    out_ref[...] = narrowed(rows_ref[count:, :], slab_ref)


def pair_kernel(rows_ref, two_ref, late_ref, mix_term, send_ref, third):
    parts, count = send_ref.shape[0] + 1, send_ref.shape[1]
    third[...] = mix_term[...]

    @pl.when(second())
    def _():
        third[...] = narrowed(rows_ref[count:, :], late_ref)

    both = beside(narrowed(rows_ref[count:, :], two_ref), third[...])
    for k in range(1, parts):
        send_ref[k - 1] = both[(k - 1) * count:k * count]


def cross_kernel(twin_ref, two_ref, core_ref, diagonal_ref):
    parts, half = diagonal_ref.shape[0] + 1, diagonal_ref.shape[1]
    term = narrowed(twin_ref[...], two_ref)
    width = two_ref.shape[0] - 8
    labels = two_ref[width:width + 1, :]
    tiles = [labels[:, start:start + LANES] for start in range(0, labels.shape[1], LANES)]
    core_ref[:half, :] = halved(term[:2 * half])
    core_ref[half:, :] = jnp.concatenate((tiles * 8)[:8], axis=0)
    for k in range(1, parts):
        diagonal_ref[k - 1] = halved(term[2 * k * half:2 * (k + 1) * half])


def keep_kernel(rows_ref, two_ref, mix_ref, late_ref, two_out, third_out):
    count = two_out.shape[0]
    two_out[...] = narrowed(rows_ref[:count, :], two_ref)

    @pl.when(second())
    def _():
        third_out[...] = narrowed(rows_ref[:count, :], late_ref)

    @pl.when(~second())
    def _():
        third_out[...] = narrowed(rows_ref[:count, :], mix_ref)


def finish_kernel(parts, rows_ref, own_keep, two_keep, third_keep, own_labels, two_ref, mix_ref, late_ref, core_ref, *refs):
    own_in, pair_in, diagonal_in = [refs[i * (parts - 1):(i + 1) * (parts - 1)] for i in range(3)]
    out_ref, out, sems = refs[-3:]
    count = own_keep.shape[0]
    width = two_ref.shape[0] - 8
    tiles = out.shape[2] // LANES
    rows = row_labels(rows_ref[:count, :])
    copies = []

    def store(m, term, labels):
        for k in range(tiles):
            out[m, :, k * LANES:(k + 1) * LANES] = jnp.where(rows == labels[k], term, 0.0)
        copies.append(pltpu.make_async_copy(out.at[m], out_ref.at[m], sems.at[m]))
        copies[-1].start()

    def of(ref, row=width):
        return [ref[row:row + 1, k * LANES:(k + 1) * LANES] for k in range(tiles)]

    def pick(here, one, other):
        return [jnp.where(here, x, y) for x, y in zip(one, other)]

    pairs = [apart(ref[...]) for ref in pair_in]
    store(0, sum([unhalved(ref[...]) for ref in own_in], own_keep[...]), of(own_labels, 0))
    store(2, sum([two for two, _ in pairs], two_keep[...]), of(two_ref))
    third = sum([third for _, third in pairs], third_keep[...])
    crossed = sum([unhalved(ref[...]) for ref in diagonal_in], unhalved(core_ref[:count // 2, :]))
    crossed_labels = [core_ref[count // 2 + k:count // 2 + k + 1, :] for k in range(tiles)]
    third_labels = pick(second(), of(late_ref), of(mix_ref))
    store(1, jnp.where(odd(), third, crossed), pick(odd(), third_labels, crossed_labels))
    store(3, jnp.where(odd(), crossed, third), pick(odd(), crossed_labels, third_labels))
    for copy in copies:
        copy.wait()


def whole(*shape):
    return jax.ShapeDtypeStruct(shape, F32)


def call(kernel, out_shape, args, flops, off=0, scratch=(), out_specs=ONCHIP):
    moved = sum(a.size * 4 for a in list(args) + out_shape)
    args = [pltpu.with_memory_space_constraint(a, pltpu.HBM) for a in args[:off]] + list(args[off:])
    return pl.pallas_call(
        kernel,
        out_shape=out_shape,
        in_specs=[OFFCHIP] * off + [ONCHIP] * (len(args) - off),
        out_specs=[out_specs] * len(out_shape),
        scratch_shapes=list(scratch),
        cost_estimate=pl.CostEstimate(flops=flops, bytes_accessed=0, transcendentals=0),
        compiler_params=pltpu.CompilerParams(vmem_limit_bytes=32 * 1024 * 1024),
    )(*args)


def body(amplitudes, integrals, cd_irrep, ab_irrep, ij_irrep):
    blocks, parts = lax.axis_size("blk"), lax.axis_size("red")
    pairs, depth = amplitudes.shape
    row_count = integrals.shape[0]
    width = depth // 4
    count = row_count // parts
    one_product = 12 * row_count * width * pairs

    def moved(array, steps):
        return lax.ppermute(array, "blk", [(i, (i + steps[i % 4]) % blocks) for i in range(blocks)])

    def exchanged(array):
        return [
            lax.ppermute(array[k - 1], "red", [(i, (i + k) % parts) for i in range(parts)])
            for k in range(1, parts)
        ]

    def after(array, *earlier):
        return lax.optimization_barrier((array, *earlier))[0]

    def staging(array, labels, copies):
        return [
            pltpu.VMEM(array.shape, F32),
            pltpu.VMEM(labels.shape, jnp.int32),
            pltpu.VMEM(cd_irrep.shape, jnp.int32),
        ], pltpu.SemaphoreType.DMA((2 + copies,))

    stage, sems = staging(amplitudes, ij_irrep, 1)
    own, = call(pack_kernel, [whole(width + 8, pairs)], (amplitudes, ij_irrep, cd_irrep),
                4 * amplitudes.size, 3, stage + [sems])
    def crossed(array, step):
        routes = [((b, r), (b ^ 1, (r + step) % parts)) for b in range(blocks) for r in range(parts)]
        return lax.ppermute(array, ("blk", "red"), [(b * parts + r, c * parts + t) for (b, r), (c, t) in routes])

    two = moved(own, (2, 2, 2, 2))
    own_labels, = call(labels_kernel, [whole(8, pairs)], (own,), 0)
    mix = moved(after(own, own_labels), (1, 3, 1, -1))
    stage, sems = staging(integrals, ab_irrep, parts)
    rows, = call(
        functools.partial(first_kernel, count), [whole(row_count, 2 * LANES)],
        (after(integrals, own_labels), ab_irrep, cd_irrep), 0, 3,
        stage + [pltpu.VMEM((row_count, LANES), F32), sems])
    twin = moved(rows, (1, -1, 1, -1))
    own_keep, own_send = call(
        own_kernel, [whole(count, LANES), whole(parts - 1, count // 2, LANES)], (rows, own), 64 * one_product)
    own_in = exchanged(own_send)
    late = moved(after(own, own_keep), (1, -1, 1, 3))
    rest = whole(row_count - count, LANES)
    mix_term, = call(sent_kernel, [rest], (rows, mix), 64 * one_product)
    pair_send, = call(pair_kernel, [whole(parts - 1, count, LANES)], (rows, after(two, mix_term, *own_in), late, mix_term),
                      0, 0, [pltpu.VMEM(rest.shape, F32)])
    pair_in = exchanged(pair_send)
    core_send, diagonal_send = call(
        cross_kernel, [whole(count // 2 + 8, LANES), whole(parts - 1, count // 2, LANES)],
        (twin, after(two, pair_send)), 0)
    diagonal_in = [crossed(diagonal_send[k - 1], k) for k in range(1, parts)]
    core_in = moved(core_send, (1, -1, 1, -1))
    two_keep, third_keep = call(keep_kernel, [whole(count, LANES)] * 2,
                                (rows, after(two, diagonal_send), mix, late), 64 * one_product)
    out, = call(functools.partial(finish_kernel, parts), [whole(4, count, pairs)],
                (rows, own_keep, two_keep, third_keep, own_labels, two, mix, late, core_in, *own_in, *pair_in, *diagonal_in),
                0, 0, [pltpu.VMEM((4, count, pairs), F32), pltpu.SemaphoreType.DMA((4,))], OFFCHIP)
    return out


def solution(mesh):
    in_specs = (P("blk", "red"), P("blk", "red"), P("red", None), P("blk", None), P("blk", None))
    out_specs = P(None, ("blk", "red"), None)
    return jax.shard_map(body, mesh=mesh, in_specs=in_specs, out_specs=out_specs, check_vma=False)
```

```python
import functools
import jax
import jax.numpy as jnp
from jax import lax
from jax.experimental import pallas as pl
from jax.experimental.pallas import tpu as pltpu
from jax.sharding import PartitionSpec as P

LANES = 128
F32 = jnp.float32
ONCHIP = pl.BlockSpec(memory_space=pltpu.VMEM)
OFFCHIP = pl.BlockSpec(memory_space=pltpu.HBM)


def column(labels):
    return jnp.broadcast_to(labels.astype(F32), (LANES, labels.shape[1])).T


def fold(rows, row_labels, cd_labels):
    tiles = rows.shape[1] // LANES
    kept = [
        jnp.where(row_labels == cd_labels[:, k * LANES:(k + 1) * LANES], rows[:, k * LANES:(k + 1) * LANES], 0.0)
        for k in range(tiles)
    ]
    kept = [kept[k] + kept[k + tiles // 2] for k in range(tiles // 2)]
    low = lower(kept[0].shape)
    first, middle, last = kept
    middle_turned, last_turned = turned(middle), turned(last)
    return first + jnp.where(low, middle_turned, last_turned), middle + last_turned


def lower(shape):
    return lax.broadcasted_iota(jnp.int32, shape, 1) < LANES // 2


def turned(array):
    return pltpu.roll(array, LANES // 2, 1)


def fetch(pairs, sems):
    copies = [pltpu.make_async_copy(src, dst, sems.at[i]) for i, (src, dst) in enumerate(pairs)]
    for copy in copies:
        copy.start()
    return copies


def pack_kernel(amp_ref, ij_ref, cd_ref, out_ref, amp, ij, cd, sems):
    pairs, width = amp.shape[0], out_ref.shape[0] - 8
    copies = fetch([(amp_ref, amp), (ij_ref, ij), (cd_ref, cd)], sems)
    copies[1].wait()
    copies[2].wait()
    rows = column(ij[...])
    labels = cd[...].astype(F32)
    out_ref[width:, :] = jnp.broadcast_to(ij[...].astype(F32), (8, pairs))
    copies[0].wait()
    for start in range(0, pairs, LANES):
        part = slice(start, start + LANES)
        first, second = fold(amp[part, :], rows[part], labels)
        out_ref[:LANES, part] = first.T
        out_ref[LANES:width, part] = second.T[:width - LANES]


def row_labels(rows):
    tile = rows[:, -LANES:]
    return jnp.where(lower(tile.shape), turned(tile), tile)


def narrowed(rows, slab_ref):
    width = slab_ref.shape[0] - 8
    full = jnp.dot(rows[:, :width], slab_ref[:width, :], precision=lax.Precision.HIGHEST, preferred_element_type=F32)
    slab_labels, own_labels = slab_ref[width:width + 1, :], row_labels(rows)
    total = None
    for start in range(0, full.shape[1], LANES):
        part = slice(start, start + LANES)
        kept = jnp.where(own_labels == slab_labels[:, part], full[:, part], 0.0)
        total = kept if total is None else total + kept
    return total + turned(total)


def beside(one, other):
    return jnp.where(lower(one.shape), one, other)


def apart(array):
    low, other = lower(array.shape), turned(array)
    return jnp.where(low, array, other), jnp.where(low, other, array)


def halved(term):
    half = term.shape[0] // 2
    return beside(term[:half], term[half:])


def unhalved(term):
    return jnp.concatenate(apart(term), axis=0)


def odd():
    return lax.rem(lax.axis_index("blk"), 2) == 1


def first_kernel(count, v_ref, ab_ref, cd_ref, rows_ref, v, ab, cd, labels, sems):
    parts = v.shape[0] // count
    mine = lax.axis_index("red")
    places = [pl.ds(pl.multiple_of(lax.rem(mine + k, parts) * count, count), count) for k in range(parts)]
    held = [pl.ds(k * count, count) for k in range(parts)]
    copies = fetch([(ab_ref, ab), (cd_ref, cd)] + [(v_ref.at[p], v.at[h]) for p, h in zip(places, held)], sems)
    copies[0].wait()
    copies[1].wait()
    labels[...] = column(ab[...])
    cd_labels = cd[...].astype(F32)
    for copy, p, h in zip(copies[2:], places, held):
        own_labels = labels[p, :]
        copy.wait()
        leading, last = fold(v[h, :], own_labels, cd_labels)
        rows_ref[h, :LANES] = leading
        rows_ref[h, LANES:] = beside(last, own_labels)


def labels_kernel(slab_ref, out_ref):
    out_ref[...] = slab_ref[slab_ref.shape[0] - 8:, :]


def second():
    return lax.rem(lax.axis_index("blk"), 4) == 2


def own_kernel(rows_ref, own_ref, keep_ref, send_ref):
    count = keep_ref.shape[0]
    term = narrowed(rows_ref[...], own_ref)
    keep_ref[...] = term[:count]
    for k in range(1, send_ref.shape[0] + 1):
        send_ref[k - 1] = halved(term[k * count:(k + 1) * count])


def sent_kernel(rows_ref, slab_ref, out_ref):
    count = rows_ref.shape[0] - out_ref.shape[0]
    out_ref[...] = narrowed(rows_ref[count:, :], slab_ref)


def pair_kernel(rows_ref, two_ref, late_ref, mix_term, send_ref, third):
    parts, count = send_ref.shape[0] + 1, send_ref.shape[1]
    third[...] = mix_term[...]

    @pl.when(second())
    def _():
        third[...] = narrowed(rows_ref[count:, :], late_ref)

    both = beside(narrowed(rows_ref[count:, :], two_ref), third[...])
    for k in range(1, parts):
        send_ref[k - 1] = both[(k - 1) * count:k * count]


def cross_kernel(twin_ref, two_ref, core_ref, diagonal_ref):
    parts, half = diagonal_ref.shape[0] + 1, diagonal_ref.shape[1]
    term = narrowed(twin_ref[...], two_ref)
    width = two_ref.shape[0] - 8
    labels = two_ref[width:width + 1, :]
    tiles = [labels[:, start:start + LANES] for start in range(0, labels.shape[1], LANES)]
    core_ref[:half, :] = halved(term[:2 * half])
    core_ref[half:, :] = jnp.concatenate((tiles * 8)[:8], axis=0)
    for k in range(1, parts):
        diagonal_ref[k - 1] = halved(term[2 * k * half:2 * (k + 1) * half])


def keep_kernel(rows_ref, two_ref, mix_ref, late_ref, two_out, third_out):
    count = two_out.shape[0]
    two_out[...] = narrowed(rows_ref[:count, :], two_ref)

    @pl.when(second())
    def _():
        third_out[...] = narrowed(rows_ref[:count, :], late_ref)

    @pl.when(~second())
    def _():
        third_out[...] = narrowed(rows_ref[:count, :], mix_ref)


def finish_kernel(parts, rows_ref, own_keep, two_keep, third_keep, own_labels, two_ref, mix_ref, late_ref, core_ref, *refs):
    own_in, pair_in, diagonal_in = [refs[i * (parts - 1):(i + 1) * (parts - 1)] for i in range(3)]
    out_ref, out, sems = refs[-3:]
    count = own_keep.shape[0]
    width = two_ref.shape[0] - 8
    tiles = out.shape[2] // LANES
    rows = row_labels(rows_ref[:count, :])
    copies = []

    def store(m, term, labels):
        for k in range(tiles):
            out[m, :, k * LANES:(k + 1) * LANES] = jnp.where(rows == labels[k], term, 0.0)
        copies.append(pltpu.make_async_copy(out.at[m], out_ref.at[m], sems.at[m]))
        copies[-1].start()

    def of(ref, row=width):
        return [ref[row:row + 1, k * LANES:(k + 1) * LANES] for k in range(tiles)]

    def pick(here, one, other):
        return [jnp.where(here, x, y) for x, y in zip(one, other)]

    pairs = [apart(ref[...]) for ref in pair_in]
    store(0, sum([unhalved(ref[...]) for ref in own_in], own_keep[...]), of(own_labels, 0))
    store(2, sum([two for two, _ in pairs], two_keep[...]), of(two_ref))
    third = sum([third for _, third in pairs], third_keep[...])
    crossed = sum([unhalved(ref[...]) for ref in diagonal_in], unhalved(core_ref[:count // 2, :]))
    crossed_labels = [core_ref[count // 2 + k:count // 2 + k + 1, :] for k in range(tiles)]
    third_labels = pick(second(), of(late_ref), of(mix_ref))
    store(1, jnp.where(odd(), third, crossed), pick(odd(), third_labels, crossed_labels))
    store(3, jnp.where(odd(), crossed, third), pick(odd(), crossed_labels, third_labels))
    for copy in copies:
        copy.wait()


def whole(*shape):
    return jax.ShapeDtypeStruct(shape, F32)


def call(kernel, out_shape, args, flops, off=0, scratch=(), out_specs=ONCHIP):
    moved = sum(a.size * 4 for a in list(args) + out_shape)
    args = [pltpu.with_memory_space_constraint(a, pltpu.HBM) for a in args[:off]] + list(args[off:])
    return pl.pallas_call(
        kernel,
        out_shape=out_shape,
        in_specs=[OFFCHIP] * off + [ONCHIP] * (len(args) - off),
        out_specs=[out_specs] * len(out_shape),
        scratch_shapes=list(scratch),
        cost_estimate=pl.CostEstimate(flops=flops, bytes_accessed=0, transcendentals=0),
        compiler_params=pltpu.CompilerParams(vmem_limit_bytes=32 * 1024 * 1024),
    )(*args)


def body(amplitudes, integrals, cd_irrep, ab_irrep, ij_irrep):
    blocks, parts = lax.axis_size("blk"), lax.axis_size("red")
    pairs, depth = amplitudes.shape
    row_count = integrals.shape[0]
    width = depth // 4
    count = row_count // parts
    one_product = 12 * row_count * width * pairs

    def moved(array, steps):
        return lax.ppermute(array, "blk", [(i, (i + steps[i % 4]) % blocks) for i in range(blocks)])

    def exchanged(array):
        return [
            lax.ppermute(array[k - 1], "red", [(i, (i + k) % parts) for i in range(parts)])
            for k in range(1, parts)
        ]

    def after(array, *earlier):
        return lax.optimization_barrier((array, *earlier))[0]

    def staging(array, labels, copies):
        return [
            pltpu.VMEM(array.shape, F32),
            pltpu.VMEM(labels.shape, jnp.int32),
            pltpu.VMEM(cd_irrep.shape, jnp.int32),
        ], pltpu.SemaphoreType.DMA((2 + copies,))

    stage, sems = staging(amplitudes, ij_irrep, 1)
    own, = call(pack_kernel, [whole(width + 8, pairs)], (amplitudes, ij_irrep, cd_irrep),
                4 * amplitudes.size, 3, stage + [sems])
    def crossed(array, step):
        routes = [((b, r), (b ^ 1, (r + step) % parts)) for b in range(blocks) for r in range(parts)]
        return lax.ppermute(array, ("blk", "red"), [(b * parts + r, c * parts + t) for (b, r), (c, t) in routes])

    two = moved(own, (2, 2, 2, 2))
    own_labels, = call(labels_kernel, [whole(8, pairs)], (own,), 0)
    mix = moved(after(own, own_labels), (1, 3, 1, -1))
    stage, sems = staging(integrals, ab_irrep, parts)
    rows, = call(
        functools.partial(first_kernel, count), [whole(row_count, 2 * LANES)],
        (after(integrals, own_labels), ab_irrep, cd_irrep), 0, 3,
        stage + [pltpu.VMEM((row_count, LANES), F32), sems])
    twin = moved(rows, (1, -1, 1, -1))
    own_keep, own_send = call(
        own_kernel, [whole(count, LANES), whole(parts - 1, count // 2, LANES)], (rows, own), 64 * one_product)
    own_in = exchanged(own_send)
    late = moved(after(own, own_keep), (1, -1, 1, 3))
    rest = whole(row_count - count, LANES)
    mix_term, = call(sent_kernel, [rest], (rows, mix), 0)
    pair_send, = call(pair_kernel, [whole(parts - 1, count, LANES)], (rows, after(two, mix_term, *own_in), late, mix_term),
                      0, 0, [pltpu.VMEM(rest.shape, F32)])
    pair_in = exchanged(pair_send)
    core_send, diagonal_send = call(
        cross_kernel, [whole(count // 2 + 8, LANES), whole(parts - 1, count // 2, LANES)],
        (twin, after(two, pair_send)), 0)
    diagonal_in = [crossed(diagonal_send[k - 1], k) for k in range(1, parts)]
    core_in = moved(core_send, (1, -1, 1, -1))
    two_keep, third_keep = call(keep_kernel, [whole(count, LANES)] * 2,
                                (rows, after(two, diagonal_send), mix, late), 64 * one_product)
    out, = call(functools.partial(finish_kernel, parts), [whole(4, count, pairs)],
                (rows, own_keep, two_keep, third_keep, own_labels, two, mix, late, core_in, *own_in, *pair_in, *diagonal_in),
                0, 0, [pltpu.VMEM((4, count, pairs), F32), pltpu.SemaphoreType.DMA((4,))], OFFCHIP)
    return out


def solution(mesh):
    in_specs = (P("blk", "red"), P("blk", "red"), P("red", None), P("blk", None), P("blk", None))
    out_specs = P(None, ("blk", "red"), None)
    return jax.shard_map(body, mesh=mesh, in_specs=in_specs, out_specs=out_specs, check_vma=False)
```

```python
import functools
import jax
import jax.numpy as jnp
from jax import lax
from jax.experimental import pallas as pl
from jax.experimental.pallas import tpu as pltpu
from jax.sharding import PartitionSpec as P

LANES = 128
F32 = jnp.float32
ONCHIP = pl.BlockSpec(memory_space=pltpu.VMEM)
OFFCHIP = pl.BlockSpec(memory_space=pltpu.HBM)


def column(labels):
    return jnp.broadcast_to(labels.astype(F32), (LANES, labels.shape[1])).T


def fold(rows, row_labels, cd_labels):
    tiles = rows.shape[1] // LANES
    kept = [
        jnp.where(row_labels == cd_labels[:, k * LANES:(k + 1) * LANES], rows[:, k * LANES:(k + 1) * LANES], 0.0)
        for k in range(tiles)
    ]
    kept = [kept[k] + kept[k + tiles // 2] for k in range(tiles // 2)]
    low = lower(kept[0].shape)
    first, middle, last = kept
    middle_turned, last_turned = turned(middle), turned(last)
    return first + jnp.where(low, middle_turned, last_turned), middle + last_turned


def lower(shape):
    return lax.broadcasted_iota(jnp.int32, shape, 1) < LANES // 2


def turned(array):
    return pltpu.roll(array, LANES // 2, 1)


def fetch(pairs, sems):
    copies = [pltpu.make_async_copy(src, dst, sems.at[i]) for i, (src, dst) in enumerate(pairs)]
    for copy in copies:
        copy.start()
    return copies


def pack_kernel(amp_ref, ij_ref, cd_ref, out_ref, amp, ij, cd, sems):
    pairs, width = amp.shape[0], out_ref.shape[0] - 8
    copies = fetch([(amp_ref, amp), (ij_ref, ij), (cd_ref, cd)], sems)
    copies[1].wait()
    copies[2].wait()
    rows = column(ij[...])
    labels = cd[...].astype(F32)
    out_ref[width:, :] = jnp.broadcast_to(ij[...].astype(F32), (8, pairs))
    copies[0].wait()
    for start in range(0, pairs, LANES):
        part = slice(start, start + LANES)
        first, second = fold(amp[part, :], rows[part], labels)
        out_ref[:LANES, part] = first.T
        out_ref[LANES:width, part] = second.T[:width - LANES]


def row_labels(rows):
    tile = rows[:, -LANES:]
    return jnp.where(lower(tile.shape), turned(tile), tile)


def narrowed(rows, slab_ref):
    width = slab_ref.shape[0] - 8
    full = jnp.dot(rows[:, :width], slab_ref[:width, :], precision=lax.Precision.HIGHEST, preferred_element_type=F32)
    slab_labels, own_labels = slab_ref[width:width + 1, :], row_labels(rows)
    total = None
    for start in range(0, full.shape[1], LANES):
        part = slice(start, start + LANES)
        kept = jnp.where(own_labels == slab_labels[:, part], full[:, part], 0.0)
        total = kept if total is None else total + kept
    return total + turned(total)


def beside(one, other):
    return jnp.where(lower(one.shape), one, other)


def apart(array):
    low, other = lower(array.shape), turned(array)
    return jnp.where(low, array, other), jnp.where(low, other, array)


def halved(term):
    half = term.shape[0] // 2
    return beside(term[:half], term[half:])


def unhalved(term):
    return jnp.concatenate(apart(term), axis=0)


def odd():
    return lax.rem(lax.axis_index("blk"), 2) == 1


def first_kernel(count, v_ref, ab_ref, cd_ref, rows_ref, v, ab, cd, labels, sems):
    parts = v.shape[0] // count
    mine = lax.axis_index("red")
    places = [pl.ds(pl.multiple_of(lax.rem(mine + k, parts) * count, count), count) for k in range(parts)]
    held = [pl.ds(k * count, count) for k in range(parts)]
    copies = fetch([(ab_ref, ab), (cd_ref, cd)] + [(v_ref.at[p], v.at[h]) for p, h in zip(places, held)], sems)
    copies[0].wait()
    copies[1].wait()
    labels[...] = column(ab[...])
    cd_labels = cd[...].astype(F32)
    for copy, p, h in zip(copies[2:], places, held):
        own_labels = labels[p, :]
        copy.wait()
        leading, last = fold(v[h, :], own_labels, cd_labels)
        rows_ref[h, :LANES] = leading
        rows_ref[h, LANES:] = beside(last, own_labels)


def labels_kernel(slab_ref, out_ref):
    out_ref[...] = slab_ref[slab_ref.shape[0] - 8:, :]


def second():
    return lax.rem(lax.axis_index("blk"), 4) == 2


def own_kernel(rows_ref, own_ref, keep_ref, send_ref):
    count = keep_ref.shape[0]
    term = narrowed(rows_ref[...], own_ref)
    keep_ref[...] = term[:count]
    for k in range(1, send_ref.shape[0] + 1):
        send_ref[k - 1] = halved(term[k * count:(k + 1) * count])


def sent_kernel(rows_ref, slab_ref, out_ref):
    count = rows_ref.shape[0] - out_ref.shape[0]
    out_ref[...] = narrowed(rows_ref[count:, :], slab_ref)


def pair_kernel(rows_ref, two_ref, late_ref, mix_term, send_ref, third):
    parts, count = send_ref.shape[0] + 1, send_ref.shape[1]
    third[...] = mix_term[...]

    @pl.when(second())
    def _():
        third[...] = narrowed(rows_ref[count:, :], late_ref)

    both = beside(narrowed(rows_ref[count:, :], two_ref), third[...])
    for k in range(1, parts):
        send_ref[k - 1] = both[(k - 1) * count:k * count]


def cross_kernel(twin_ref, two_ref, core_ref, diagonal_ref):
    parts, count = diagonal_ref.shape[0] + 1, diagonal_ref.shape[1] - 8
    term = narrowed(twin_ref[...], two_ref)
    width = two_ref.shape[0] - 8
    labels = two_ref[width:width + 1, :]
    tiles = [labels[:, start:start + LANES] for start in range(0, labels.shape[1], LANES)]
    core_ref[...] = halved(term[:count])
    for k in range(1, parts):
        diagonal_ref[k - 1, :count, :] = term[k * count:(k + 1) * count]
        diagonal_ref[k - 1, count:, :] = jnp.concatenate((tiles * 8)[:8], axis=0)


def keep_kernel(rows_ref, two_ref, mix_ref, late_ref, two_out, third_out):
    count = two_out.shape[0]
    two_out[...] = narrowed(rows_ref[:count, :], two_ref)

    @pl.when(second())
    def _():
        third_out[...] = narrowed(rows_ref[:count, :], late_ref)

    @pl.when(~second())
    def _():
        third_out[...] = narrowed(rows_ref[:count, :], mix_ref)


def finish_kernel(parts, rows_ref, own_keep, two_keep, third_keep, own_labels, two_ref, mix_ref, late_ref, core_ref, *refs):
    own_in, pair_in, diagonal_in = [refs[i * (parts - 1):(i + 1) * (parts - 1)] for i in range(3)]
    out_ref, out, sems = refs[-3:]
    count = own_keep.shape[0]
    width = two_ref.shape[0] - 8
    tiles = out.shape[2] // LANES
    rows = row_labels(rows_ref[:count, :])
    copies = []

    def store(m, term, labels):
        for k in range(tiles):
            out[m, :, k * LANES:(k + 1) * LANES] = jnp.where(rows == labels[k], term, 0.0)
        copies.append(pltpu.make_async_copy(out.at[m], out_ref.at[m], sems.at[m]))
        copies[-1].start()

    def of(ref, row=width):
        return [ref[row:row + 1, k * LANES:(k + 1) * LANES] for k in range(tiles)]

    def pick(here, one, other):
        return [jnp.where(here, x, y) for x, y in zip(one, other)]

    pairs = [apart(ref[...]) for ref in pair_in]
    store(0, sum([unhalved(ref[...]) for ref in own_in], own_keep[...]), of(own_labels, 0))
    store(2, sum([two for two, _ in pairs], two_keep[...]), of(two_ref))
    third = sum([third for _, third in pairs], third_keep[...])
    crossed = sum([ref[:count, :] for ref in diagonal_in], unhalved(core_ref[...]))
    crossed_labels = [diagonal_in[0][count + k:count + k + 1, :] for k in range(tiles)]
    third_labels = pick(second(), of(late_ref), of(mix_ref))
    store(1, jnp.where(odd(), third, crossed), pick(odd(), third_labels, crossed_labels))
    store(3, jnp.where(odd(), crossed, third), pick(odd(), crossed_labels, third_labels))
    for copy in copies:
        copy.wait()


def whole(*shape):
    return jax.ShapeDtypeStruct(shape, F32)


def call(kernel, out_shape, args, flops, off=0, scratch=(), out_specs=ONCHIP):
    moved = sum(a.size * 4 for a in list(args) + out_shape)
    args = [pltpu.with_memory_space_constraint(a, pltpu.HBM) for a in args[:off]] + list(args[off:])
    return pl.pallas_call(
        kernel,
        out_shape=out_shape,
        in_specs=[OFFCHIP] * off + [ONCHIP] * (len(args) - off),
        out_specs=[out_specs] * len(out_shape),
        scratch_shapes=list(scratch),
        cost_estimate=pl.CostEstimate(flops=flops, bytes_accessed=0, transcendentals=0),
        compiler_params=pltpu.CompilerParams(vmem_limit_bytes=32 * 1024 * 1024),
    )(*args)


def body(amplitudes, integrals, cd_irrep, ab_irrep, ij_irrep):
    blocks, parts = lax.axis_size("blk"), lax.axis_size("red")
    pairs, depth = amplitudes.shape
    row_count = integrals.shape[0]
    width = depth // 4
    count = row_count // parts
    one_product = 12 * row_count * width * pairs

    def moved(array, steps):
        return lax.ppermute(array, "blk", [(i, (i + steps[i % 4]) % blocks) for i in range(blocks)])

    def exchanged(array):
        return [
            lax.ppermute(array[k - 1], "red", [(i, (i + k) % parts) for i in range(parts)])
            for k in range(1, parts)
        ]

    def after(array, *earlier):
        return lax.optimization_barrier((array, *earlier))[0]

    def staging(array, labels, copies):
        return [
            pltpu.VMEM(array.shape, F32),
            pltpu.VMEM(labels.shape, jnp.int32),
            pltpu.VMEM(cd_irrep.shape, jnp.int32),
        ], pltpu.SemaphoreType.DMA((2 + copies,))

    stage, sems = staging(amplitudes, ij_irrep, 1)
    own, = call(pack_kernel, [whole(width + 8, pairs)], (amplitudes, ij_irrep, cd_irrep),
                4 * amplitudes.size, 3, stage + [sems])
    def crossed(array, step):
        routes = [((b, r), (b ^ 1, (r + step) % parts)) for b in range(blocks) for r in range(parts)]
        return lax.ppermute(array, ("blk", "red"), [(b * parts + r, c * parts + t) for (b, r), (c, t) in routes])

    two = moved(own, (2, 2, 2, 2))
    own_labels, = call(labels_kernel, [whole(8, pairs)], (own,), 0)
    mix = moved(after(own, own_labels), (1, 3, 1, -1))
    stage, sems = staging(integrals, ab_irrep, parts)
    rows, = call(
        functools.partial(first_kernel, count), [whole(row_count, 2 * LANES)],
        (after(integrals, own_labels), ab_irrep, cd_irrep), 0, 3,
        stage + [pltpu.VMEM((row_count, LANES), F32), sems])
    twin = moved(rows, (1, -1, 1, -1))
    own_keep, own_send = call(
        own_kernel, [whole(count, LANES), whole(parts - 1, count // 2, LANES)], (rows, own), 64 * one_product)
    own_in = exchanged(own_send)
    late = moved(after(own, own_keep), (1, -1, 1, 3))
    rest = whole(row_count - count, LANES)
    mix_term, = call(sent_kernel, [rest], (rows, mix), 0)
    core_send, diagonal_send = call(
        cross_kernel, [whole(count // 2, LANES), whole(parts - 1, count + 8, LANES)],
        (twin, after(two, mix_term, *own_in)), 0)
    diagonal_in = [crossed(diagonal_send[k - 1], k) for k in range(1, parts)]
    pair_send, = call(pair_kernel, [whole(parts - 1, count, LANES)], (rows, after(two, diagonal_send), late, mix_term),
                      0, 0, [pltpu.VMEM(rest.shape, F32)])
    pair_in = exchanged(pair_send)
    core_in = moved(after(core_send, pair_send), (1, -1, 1, -1))
    two_keep, third_keep = call(keep_kernel, [whole(count, LANES)] * 2,
                                (rows, after(two, pair_send), mix, late), 0)
    out, = call(functools.partial(finish_kernel, parts), [whole(4, count, pairs)],
                (rows, own_keep, two_keep, third_keep, own_labels, two, mix, late, core_in, *own_in, *pair_in, *diagonal_in),
                0, 0, [pltpu.VMEM((4, count, pairs), F32), pltpu.SemaphoreType.DMA((4,))], OFFCHIP)
    return out


def solution(mesh):
    in_specs = (P("blk", "red"), P("blk", "red"), P("red", None), P("blk", None), P("blk", None))
    out_specs = P(None, ("blk", "red"), None)
    return jax.shard_map(body, mesh=mesh, in_specs=in_specs, out_specs=out_specs, check_vma=False)
```

```python
import functools
import jax
import jax.numpy as jnp
from jax import lax
from jax.experimental import pallas as pl
from jax.experimental.pallas import tpu as pltpu
from jax.sharding import PartitionSpec as P

LANES = 128
F32 = jnp.float32
ONCHIP = pl.BlockSpec(memory_space=pltpu.VMEM)
OFFCHIP = pl.BlockSpec(memory_space=pltpu.HBM)


def column(labels):
    return jnp.broadcast_to(labels.astype(F32), (LANES, labels.shape[1])).T


def fold(rows, row_labels, cd_labels):
    tiles = rows.shape[1] // LANES
    kept = [
        jnp.where(row_labels == cd_labels[:, k * LANES:(k + 1) * LANES], rows[:, k * LANES:(k + 1) * LANES], 0.0)
        for k in range(tiles)
    ]
    kept = [kept[k] + kept[k + tiles // 2] for k in range(tiles // 2)]
    low = lower(kept[0].shape)
    first, middle, last = kept
    middle_turned, last_turned = turned(middle), turned(last)
    return first + jnp.where(low, middle_turned, last_turned), middle + last_turned


def lower(shape):
    return lax.broadcasted_iota(jnp.int32, shape, 1) < LANES // 2


def turned(array):
    return pltpu.roll(array, LANES // 2, 1)


def fetch(pairs, sems):
    copies = [pltpu.make_async_copy(src, dst, sems.at[i]) for i, (src, dst) in enumerate(pairs)]
    for copy in copies:
        copy.start()
    return copies


def pack_kernel(amp_ref, ij_ref, cd_ref, out_ref, amp, ij, cd, sems):
    pairs, width = amp.shape[0], out_ref.shape[0] - 8
    copies = fetch([(amp_ref, amp), (ij_ref, ij), (cd_ref, cd)], sems)
    copies[1].wait()
    copies[2].wait()
    rows = column(ij[...])
    labels = cd[...].astype(F32)
    out_ref[width:, :] = jnp.broadcast_to(ij[...].astype(F32), (8, pairs))
    copies[0].wait()
    for start in range(0, pairs, LANES):
        part = slice(start, start + LANES)
        first, second = fold(amp[part, :], rows[part], labels)
        out_ref[:LANES, part] = first.T
        out_ref[LANES:width, part] = second.T[:width - LANES]


def row_labels(rows):
    tile = rows[:, -LANES:]
    return jnp.where(lower(tile.shape), turned(tile), tile)


def narrowed(rows, slab_ref):
    width = slab_ref.shape[0] - 8
    full = jnp.dot(rows[:, :width], slab_ref[:width, :], precision=lax.Precision.HIGHEST, preferred_element_type=F32)
    slab_labels, own_labels = slab_ref[width:width + 1, :], row_labels(rows)
    total = None
    for start in range(0, full.shape[1], LANES):
        part = slice(start, start + LANES)
        kept = jnp.where(own_labels == slab_labels[:, part], full[:, part], 0.0)
        total = kept if total is None else total + kept
    return total + turned(total)


def beside(one, other):
    return jnp.where(lower(one.shape), one, other)


def apart(array):
    low, other = lower(array.shape), turned(array)
    return jnp.where(low, array, other), jnp.where(low, other, array)


def halved(term):
    half = term.shape[0] // 2
    return beside(term[:half], term[half:])


def unhalved(term):
    return jnp.concatenate(apart(term), axis=0)


def odd():
    return lax.rem(lax.axis_index("blk"), 2) == 1


def first_kernel(count, v_ref, ab_ref, cd_ref, rows_ref, v, ab, cd, labels, sems):
    parts = v.shape[0] // count
    mine = lax.axis_index("red")
    places = [pl.ds(pl.multiple_of(lax.rem(mine + k, parts) * count, count), count) for k in range(parts)]
    held = [pl.ds(k * count, count) for k in range(parts)]
    copies = fetch([(ab_ref, ab), (cd_ref, cd)] + [(v_ref.at[p], v.at[h]) for p, h in zip(places, held)], sems)
    copies[0].wait()
    copies[1].wait()
    labels[...] = column(ab[...])
    cd_labels = cd[...].astype(F32)
    for copy, p, h in zip(copies[2:], places, held):
        own_labels = labels[p, :]
        copy.wait()
        leading, last = fold(v[h, :], own_labels, cd_labels)
        rows_ref[h, :LANES] = leading
        rows_ref[h, LANES:] = beside(last, own_labels)


def labels_kernel(slab_ref, out_ref):
    out_ref[...] = slab_ref[slab_ref.shape[0] - 8:, :]


def second():
    return lax.rem(lax.axis_index("blk"), 4) == 2


def own_kernel(rows_ref, own_ref, keep_ref, send_ref):
    count = keep_ref.shape[0]
    term = narrowed(rows_ref[...], own_ref)
    keep_ref[...] = term[:count]
    for k in range(1, send_ref.shape[0] + 1):
        send_ref[k - 1] = halved(term[k * count:(k + 1) * count])


def sent_kernel(rows_ref, slab_ref, out_ref):
    count = rows_ref.shape[0] - out_ref.shape[0]
    out_ref[...] = narrowed(rows_ref[count:, :], slab_ref)


def pair_kernel(rows_ref, two_ref, late_ref, mix_term, send_ref, third):
    parts, count = send_ref.shape[0] + 1, send_ref.shape[1]
    third[...] = mix_term[...]

    @pl.when(second())
    def _():
        third[...] = narrowed(rows_ref[count:, :], late_ref)

    both = beside(narrowed(rows_ref[count:, :], two_ref), third[...])
    for k in range(1, parts):
        send_ref[k - 1] = both[(k - 1) * count:k * count]


def cross_kernel(twin_ref, two_ref, core_ref, diagonal_ref):
    parts, half = diagonal_ref.shape[0] + 1, diagonal_ref.shape[1]
    term = narrowed(twin_ref[...], two_ref)
    width = two_ref.shape[0] - 8
    labels = two_ref[width:width + 1, :]
    tiles = [labels[:, start:start + LANES] for start in range(0, labels.shape[1], LANES)]
    core_ref[:half, :] = halved(term[:2 * half])
    core_ref[half:, :] = jnp.concatenate((tiles * 8)[:8], axis=0)
    for k in range(1, parts):
        diagonal_ref[k - 1] = halved(term[2 * k * half:2 * (k + 1) * half])


def keep_kernel(rows_ref, two_ref, mix_ref, late_ref, *refs):
    diagonal_in, (two_out, third_out, crossed_out) = refs[:-3], refs[-3:]
    count = two_out.shape[0]
    terms = [unhalved(ref[...]) for ref in diagonal_in]
    crossed_out[...] = sum(terms[1:], terms[0])
    two_out[...] = narrowed(rows_ref[:count, :], two_ref)

    @pl.when(second())
    def _():
        third_out[...] = narrowed(rows_ref[:count, :], late_ref)

    @pl.when(~second())
    def _():
        third_out[...] = narrowed(rows_ref[:count, :], mix_ref)


def total_kernel(*refs):
    terms, out_ref = [ref[...] for ref in refs[:-1]], refs[-1]
    out_ref[...] = sum(terms[1:], terms[0])


def finish_kernel(parts, rows_ref, own_keep, two_keep, third_keep, crossed_ref, own_labels, two_ref, mix_ref, late_ref, core_ref, *refs):
    own_in, (pair_ref, out_ref, out, sems) = refs[:parts - 1], refs[parts - 1:]
    count = own_keep.shape[0]
    width = two_ref.shape[0] - 8
    tiles = out.shape[2] // LANES
    rows = row_labels(rows_ref[:count, :])
    copies = []

    def store(m, term, labels):
        for k in range(tiles):
            out[m, :, k * LANES:(k + 1) * LANES] = jnp.where(rows == labels[k], term, 0.0)
        copies.append(pltpu.make_async_copy(out.at[m], out_ref.at[m], sems.at[m]))
        copies[-1].start()

    def of(ref, row=width):
        return [ref[row:row + 1, k * LANES:(k + 1) * LANES] for k in range(tiles)]

    def pick(here, one, other):
        return [jnp.where(here, x, y) for x, y in zip(one, other)]

    two, third = apart(pair_ref[...])
    store(0, sum([unhalved(ref[...]) for ref in own_in], own_keep[...]), of(own_labels, 0))
    store(2, two + two_keep[...], of(two_ref))
    third = third + third_keep[...]
    crossed = crossed_ref[...] + unhalved(core_ref[:count // 2, :])
    crossed_labels = [core_ref[count // 2 + k:count // 2 + k + 1, :] for k in range(tiles)]
    third_labels = pick(second(), of(late_ref), of(mix_ref))
    store(1, jnp.where(odd(), third, crossed), pick(odd(), third_labels, crossed_labels))
    store(3, jnp.where(odd(), crossed, third), pick(odd(), crossed_labels, third_labels))
    for copy in copies:
        copy.wait()


def whole(*shape):
    return jax.ShapeDtypeStruct(shape, F32)


def call(kernel, out_shape, args, flops, off=0, scratch=(), out_specs=ONCHIP):
    moved = sum(a.size * 4 for a in list(args) + out_shape)
    args = [pltpu.with_memory_space_constraint(a, pltpu.HBM) for a in args[:off]] + list(args[off:])
    return pl.pallas_call(
        kernel,
        out_shape=out_shape,
        in_specs=[OFFCHIP] * off + [ONCHIP] * (len(args) - off),
        out_specs=[out_specs] * len(out_shape),
        scratch_shapes=list(scratch),
        cost_estimate=pl.CostEstimate(flops=flops, bytes_accessed=0, transcendentals=0),
        compiler_params=pltpu.CompilerParams(vmem_limit_bytes=32 * 1024 * 1024),
    )(*args)


def body(amplitudes, integrals, cd_irrep, ab_irrep, ij_irrep):
    blocks, parts = lax.axis_size("blk"), lax.axis_size("red")
    pairs, depth = amplitudes.shape
    row_count = integrals.shape[0]
    width = depth // 4
    count = row_count // parts
    one_product = 12 * row_count * width * pairs

    def moved(array, steps):
        return lax.ppermute(array, "blk", [(i, (i + steps[i % 4]) % blocks) for i in range(blocks)])

    def exchanged(array):
        return [
            lax.ppermute(array[k - 1], "red", [(i, (i + k) % parts) for i in range(parts)])
            for k in range(1, parts)
        ]

    def after(array, *earlier):
        return lax.optimization_barrier((array, *earlier))[0]

    def staging(array, labels, copies):
        return [
            pltpu.VMEM(array.shape, F32),
            pltpu.VMEM(labels.shape, jnp.int32),
            pltpu.VMEM(cd_irrep.shape, jnp.int32),
        ], pltpu.SemaphoreType.DMA((2 + copies,))

    stage, sems = staging(amplitudes, ij_irrep, 1)
    own, = call(pack_kernel, [whole(width + 8, pairs)], (amplitudes, ij_irrep, cd_irrep),
                4 * amplitudes.size, 3, stage + [sems])
    def crossed(array, step):
        routes = [((b, r), (b ^ 1, (r + step) % parts)) for b in range(blocks) for r in range(parts)]
        return lax.ppermute(array, ("blk", "red"), [(b * parts + r, c * parts + t) for (b, r), (c, t) in routes])

    two = moved(own, (2, 2, 2, 2))
    own_labels, = call(labels_kernel, [whole(8, pairs)], (own,), 0)
    mix = moved(after(own, own_labels), (1, 3, 1, -1))
    stage, sems = staging(integrals, ab_irrep, parts)
    rows, = call(
        functools.partial(first_kernel, count), [whole(row_count, 2 * LANES)],
        (after(integrals, own_labels), ab_irrep, cd_irrep), 0, 3,
        stage + [pltpu.VMEM((row_count, LANES), F32), sems])
    twin = moved(rows, (1, -1, 1, -1))
    own_keep, own_send = call(
        own_kernel, [whole(count, LANES), whole(parts - 1, count // 2, LANES)], (rows, own), 64 * one_product)
    own_in = exchanged(own_send)
    late = moved(after(own, own_keep), (1, -1, 1, 3))
    rest = whole(row_count - count, LANES)
    mix_term, = call(sent_kernel, [rest], (rows, mix), 0)
    core_send, diagonal_send = call(
        cross_kernel, [whole(count // 2 + 8, LANES), whole(parts - 1, count // 2, LANES)],
        (twin, after(two, mix_term, *own_in)), 0)
    diagonal_in = [crossed(diagonal_send[k - 1], k) for k in range(1, parts)]
    pair_send, = call(pair_kernel, [whole(parts - 1, count, LANES)], (rows, after(two, diagonal_send), late, mix_term),
                      0, 0, [pltpu.VMEM(rest.shape, F32)])
    pair_in = exchanged(pair_send)
    core_in = moved(after(core_send, pair_send), (1, -1, 1, -1))
    two_keep, third_keep, crossed_sum = call(
        keep_kernel, [whole(count, LANES)] * 3, (rows, after(two, pair_send), mix, late, *diagonal_in), 4 * one_product)
    pair_sum, = call(total_kernel, [whole(count, LANES)], tuple(pair_in), 0)
    out, = call(functools.partial(finish_kernel, parts), [whole(4, count, pairs)],
                (rows, own_keep, two_keep, third_keep, crossed_sum, own_labels, two, mix, late, core_in, *own_in, pair_sum),
                0, 0, [pltpu.VMEM((4, count, pairs), F32), pltpu.SemaphoreType.DMA((4,))], OFFCHIP)
    return out


def solution(mesh):
    in_specs = (P("blk", "red"), P("blk", "red"), P("red", None), P("blk", None), P("blk", None))
    out_specs = P(None, ("blk", "red"), None)
    return jax.shard_map(body, mesh=mesh, in_specs=in_specs, out_specs=out_specs, check_vma=False)
```

```python
import functools
import jax
import jax.numpy as jnp
from jax import lax
from jax.experimental import pallas as pl
from jax.experimental.pallas import tpu as pltpu
from jax.sharding import PartitionSpec as P

LANES = 128
F32 = jnp.float32
ONCHIP = pl.BlockSpec(memory_space=pltpu.VMEM)
OFFCHIP = pl.BlockSpec(memory_space=pltpu.HBM)


def column(labels):
    return jnp.broadcast_to(labels.astype(F32), (LANES, labels.shape[1])).T


def fold(rows, row_labels, cd_labels):
    tiles = rows.shape[1] // LANES
    kept = [
        jnp.where(row_labels == cd_labels[:, k * LANES:(k + 1) * LANES], rows[:, k * LANES:(k + 1) * LANES], 0.0)
        for k in range(tiles)
    ]
    kept = [kept[k] + kept[k + tiles // 2] for k in range(tiles // 2)]
    low = lower(kept[0].shape)
    first, middle, last = kept
    middle_turned, last_turned = turned(middle), turned(last)
    return first + jnp.where(low, middle_turned, last_turned), middle + last_turned


def lower(shape):
    return lax.broadcasted_iota(jnp.int32, shape, 1) < LANES // 2


def turned(array):
    return pltpu.roll(array, LANES // 2, 1)


def fetch(pairs, sems):
    copies = [pltpu.make_async_copy(src, dst, sems.at[i]) for i, (src, dst) in enumerate(pairs)]
    for copy in copies:
        copy.start()
    return copies


def pack_kernel(amp_ref, ij_ref, cd_ref, out_ref, amp, ij, cd, sems):
    pairs, width = amp.shape[0], out_ref.shape[0] - 8
    copies = fetch([(amp_ref, amp), (ij_ref, ij), (cd_ref, cd)], sems)
    copies[1].wait()
    copies[2].wait()
    rows = column(ij[...])
    labels = cd[...].astype(F32)
    out_ref[width:, :] = jnp.broadcast_to(ij[...].astype(F32), (8, pairs))
    copies[0].wait()
    for start in range(0, pairs, LANES):
        part = slice(start, start + LANES)
        first, second = fold(amp[part, :], rows[part], labels)
        out_ref[:LANES, part] = first.T
        out_ref[LANES:width, part] = second.T[:width - LANES]


def row_labels(rows):
    tile = rows[:, -LANES:]
    return jnp.where(lower(tile.shape), turned(tile), tile)


def split(array):
    high = array.astype(jnp.bfloat16)
    return high, (array - high.astype(F32)).astype(jnp.bfloat16)


def product(one, other):
    (one_high, one_low), (other_high, other_low) = split(one), split(other)

    def dot(left, right):
        return jnp.dot(left, right, preferred_element_type=F32)

    return dot(one_high, other_high) + (dot(one_high, other_low) + dot(one_low, other_high))


def narrowed(rows, slab_ref):
    width = slab_ref.shape[0] - 8
    full = product(rows[:, :width], slab_ref[:width, :])
    slab_labels, own_labels = slab_ref[width:width + 1, :], row_labels(rows)
    total = None
    for start in range(0, full.shape[1], LANES):
        part = slice(start, start + LANES)
        kept = jnp.where(own_labels == slab_labels[:, part], full[:, part], 0.0)
        total = kept if total is None else total + kept
    return total + turned(total)


def beside(one, other):
    return jnp.where(lower(one.shape), one, other)


def apart(array):
    low, other = lower(array.shape), turned(array)
    return jnp.where(low, array, other), jnp.where(low, other, array)


def halved(term):
    half = term.shape[0] // 2
    return beside(term[:half], term[half:])


def unhalved(term):
    return jnp.concatenate(apart(term), axis=0)


def odd():
    return lax.rem(lax.axis_index("blk"), 2) == 1


def first_kernel(count, v_ref, ab_ref, cd_ref, rows_ref, v, ab, cd, labels, sems):
    parts = v.shape[0] // count
    mine = lax.axis_index("red")
    places = [pl.ds(pl.multiple_of(lax.rem(mine + k, parts) * count, count), count) for k in range(parts)]
    held = [pl.ds(k * count, count) for k in range(parts)]
    copies = fetch([(ab_ref, ab), (cd_ref, cd)] + [(v_ref.at[p], v.at[h]) for p, h in zip(places, held)], sems)
    copies[0].wait()
    copies[1].wait()
    labels[...] = column(ab[...])
    cd_labels = cd[...].astype(F32)
    for copy, p, h in zip(copies[2:], places, held):
        own_labels = labels[p, :]
        copy.wait()
        leading, last = fold(v[h, :], own_labels, cd_labels)
        rows_ref[h, :LANES] = leading
        rows_ref[h, LANES:] = beside(last, own_labels)


def labels_kernel(slab_ref, out_ref):
    out_ref[...] = slab_ref[slab_ref.shape[0] - 8:, :]


def second():
    return lax.rem(lax.axis_index("blk"), 4) == 2


def own_kernel(rows_ref, own_ref, keep_ref, send_ref):
    count = keep_ref.shape[0]
    term = narrowed(rows_ref[...], own_ref)
    keep_ref[...] = term[:count]
    for k in range(1, send_ref.shape[0] + 1):
        send_ref[k - 1] = halved(term[k * count:(k + 1) * count])


def sent_kernel(rows_ref, slab_ref, out_ref):
    count = rows_ref.shape[0] - out_ref.shape[0]
    out_ref[...] = narrowed(rows_ref[count:, :], slab_ref)


def pair_kernel(rows_ref, two_ref, late_ref, mix_term, send_ref, third):
    parts, count = send_ref.shape[0] + 1, send_ref.shape[1]
    third[...] = mix_term[...]

    @pl.when(second())
    def _():
        third[...] = narrowed(rows_ref[count:, :], late_ref)

    both = beside(narrowed(rows_ref[count:, :], two_ref), third[...])
    for k in range(1, parts):
        send_ref[k - 1] = both[(k - 1) * count:k * count]


def diagonal_kernel(twin_ref, two_ref, send_ref):
    parts, half = send_ref.shape[0] + 1, send_ref.shape[1]
    term = narrowed(twin_ref[2 * half:, :], two_ref)
    for k in range(1, parts):
        send_ref[k - 1] = halved(term[2 * (k - 1) * half:2 * k * half])


def core_kernel(twin_ref, two_ref, send_ref):
    half = send_ref.shape[0] - 8
    width = two_ref.shape[0] - 8
    labels = two_ref[width:width + 1, :]
    tiles = [labels[:, start:start + LANES] for start in range(0, labels.shape[1], LANES)]
    send_ref[:half, :] = halved(narrowed(twin_ref[:2 * half, :], two_ref))
    send_ref[half:, :] = jnp.concatenate((tiles * 8)[:8], axis=0)


def keep_kernel(rows_ref, two_ref, mix_ref, late_ref, *refs):
    diagonal_in, (two_out, third_out, crossed_out) = refs[:-3], refs[-3:]
    count = two_out.shape[0]
    terms = [unhalved(ref[...]) for ref in diagonal_in]
    crossed_out[...] = sum(terms[1:], terms[0])
    two_out[...] = narrowed(rows_ref[:count, :], two_ref)

    @pl.when(second())
    def _():
        third_out[...] = narrowed(rows_ref[:count, :], late_ref)

    @pl.when(~second())
    def _():
        third_out[...] = narrowed(rows_ref[:count, :], mix_ref)


def total_kernel(*refs):
    terms, out_ref = [ref[...] for ref in refs[:-1]], refs[-1]
    out_ref[...] = sum(terms[1:], terms[0])


def finish_kernel(parts, rows_ref, own_keep, two_keep, third_keep, crossed_ref, own_labels, two_ref, mix_ref, late_ref, core_ref, *refs):
    own_in, (pair_ref, out_ref, out, sems) = refs[:parts - 1], refs[parts - 1:]
    count = own_keep.shape[0]
    width = two_ref.shape[0] - 8
    tiles = out.shape[2] // LANES
    rows = row_labels(rows_ref[:count, :])
    copies = []

    def store(m, term, labels):
        for k in range(tiles):
            out[m, :, k * LANES:(k + 1) * LANES] = jnp.where(rows == labels[k], term, 0.0)
        copies.append(pltpu.make_async_copy(out.at[m], out_ref.at[m], sems.at[m]))
        copies[-1].start()

    def of(ref, row=width):
        return [ref[row:row + 1, k * LANES:(k + 1) * LANES] for k in range(tiles)]

    def pick(here, one, other):
        return [jnp.where(here, x, y) for x, y in zip(one, other)]

    two, third = apart(pair_ref[...])
    store(0, sum([unhalved(ref[...]) for ref in own_in], own_keep[...]), of(own_labels, 0))
    store(2, two + two_keep[...], of(two_ref))
    third = third + third_keep[...]
    crossed = crossed_ref[...] + unhalved(core_ref[:count // 2, :])
    crossed_labels = [core_ref[count // 2 + k:count // 2 + k + 1, :] for k in range(tiles)]
    third_labels = pick(second(), of(late_ref), of(mix_ref))
    store(1, jnp.where(odd(), third, crossed), pick(odd(), third_labels, crossed_labels))
    store(3, jnp.where(odd(), crossed, third), pick(odd(), crossed_labels, third_labels))
    for copy in copies:
        copy.wait()


def whole(*shape):
    return jax.ShapeDtypeStruct(shape, F32)


def call(kernel, out_shape, args, flops, off=0, scratch=(), out_specs=ONCHIP):
    moved = sum(a.size * 4 for a in list(args) + out_shape)
    args = [pltpu.with_memory_space_constraint(a, pltpu.HBM) for a in args[:off]] + list(args[off:])
    return pl.pallas_call(
        kernel,
        out_shape=out_shape,
        in_specs=[OFFCHIP] * off + [ONCHIP] * (len(args) - off),
        out_specs=[out_specs] * len(out_shape),
        scratch_shapes=list(scratch),
        cost_estimate=pl.CostEstimate(flops=flops, bytes_accessed=0, transcendentals=0),
        compiler_params=pltpu.CompilerParams(vmem_limit_bytes=32 * 1024 * 1024),
    )(*args)


def body(amplitudes, integrals, cd_irrep, ab_irrep, ij_irrep):
    blocks, parts = lax.axis_size("blk"), lax.axis_size("red")
    pairs, depth = amplitudes.shape
    row_count = integrals.shape[0]
    width = depth // 4
    count = row_count // parts
    one_product = 12 * row_count * width * pairs

    def moved(array, steps):
        return lax.ppermute(array, "blk", [(i, (i + steps[i % 4]) % blocks) for i in range(blocks)])

    def exchanged(array):
        return [
            lax.ppermute(array[k - 1], "red", [(i, (i + k) % parts) for i in range(parts)])
            for k in range(1, parts)
        ]

    def after(array, *earlier):
        return lax.optimization_barrier((array, *earlier))[0]

    def staging(array, labels, copies):
        return [
            pltpu.VMEM(array.shape, F32),
            pltpu.VMEM(labels.shape, jnp.int32),
            pltpu.VMEM(cd_irrep.shape, jnp.int32),
        ], pltpu.SemaphoreType.DMA((2 + copies,))

    stage, sems = staging(amplitudes, ij_irrep, 1)
    own, = call(pack_kernel, [whole(width + 8, pairs)], (amplitudes, ij_irrep, cd_irrep),
                4 * amplitudes.size, 3, stage + [sems])
    def crossed(array, step):
        routes = [((b, r), (b ^ 1, (r + step) % parts)) for b in range(blocks) for r in range(parts)]
        return lax.ppermute(array, ("blk", "red"), [(b * parts + r, c * parts + t) for (b, r), (c, t) in routes])

    two = moved(own, (2, 2, 2, 2))
    own_labels, = call(labels_kernel, [whole(8, pairs)], (own,), 0)
    mix = moved(after(own, own_labels), (1, 3, 1, -1))
    stage, sems = staging(integrals, ab_irrep, parts)
    rows, = call(
        functools.partial(first_kernel, count), [whole(row_count, 2 * LANES)],
        (after(integrals, own_labels), ab_irrep, cd_irrep), 0, 3,
        stage + [pltpu.VMEM((row_count, LANES), F32), sems])
    twin = moved(rows, (1, -1, 1, -1))
    own_keep, own_send = call(
        own_kernel, [whole(count, LANES), whole(parts - 1, count // 2, LANES)], (rows, own), 64 * one_product)
    own_in = exchanged(own_send)
    late = moved(after(own, own_keep), (1, -1, 1, 3))
    rest = whole(row_count - count, LANES)
    mix_term, = call(sent_kernel, [rest], (rows, mix), 0)
    diagonal_send, = call(diagonal_kernel, [whole(parts - 1, count // 2, LANES)],
                          (twin, after(two, mix_term, *own_in)), 0)
    diagonal_in = [crossed(diagonal_send[k - 1], k) for k in range(1, parts)]
    pair_send, = call(pair_kernel, [whole(parts - 1, count, LANES)], (rows, after(two, diagonal_send), late, mix_term),
                      0, 0, [pltpu.VMEM(rest.shape, F32)])
    pair_in = exchanged(pair_send)
    core_send, = call(core_kernel, [whole(count // 2 + 8, LANES)], (twin, after(two, pair_send)), 0)
    core_in = moved(core_send, (1, -1, 1, -1))
    two_keep, third_keep, crossed_sum = call(
        keep_kernel, [whole(count, LANES)] * 3, (rows, after(two, pair_send), mix, late, *diagonal_in), 4 * one_product)
    pair_sum, = call(total_kernel, [whole(count, LANES)], tuple(pair_in), 0)
    out, = call(functools.partial(finish_kernel, parts), [whole(4, count, pairs)],
                (rows, own_keep, two_keep, third_keep, crossed_sum, own_labels, two, mix, late, core_in, *own_in, pair_sum),
                0, 0, [pltpu.VMEM((4, count, pairs), F32), pltpu.SemaphoreType.DMA((4,))], OFFCHIP)
    return out


def solution(mesh):
    in_specs = (P("blk", "red"), P("blk", "red"), P("red", None), P("blk", None), P("blk", None))
    out_specs = P(None, ("blk", "red"), None)
    return jax.shard_map(body, mesh=mesh, in_specs=in_specs, out_specs=out_specs, check_vma=False)
```

```python
import functools
import jax
import jax.numpy as jnp
from jax import lax
from jax.experimental import pallas as pl
from jax.experimental.pallas import tpu as pltpu
from jax.sharding import PartitionSpec as P

LANES = 128
F32 = jnp.float32
ONCHIP = pl.BlockSpec(memory_space=pltpu.VMEM)
OFFCHIP = pl.BlockSpec(memory_space=pltpu.HBM)


def column(labels):
    return jnp.broadcast_to(labels.astype(F32), (LANES, labels.shape[1])).T


def fold(rows, row_labels, cd_labels):
    tiles = rows.shape[1] // LANES
    kept = [
        jnp.where(row_labels == cd_labels[:, k * LANES:(k + 1) * LANES], rows[:, k * LANES:(k + 1) * LANES], 0.0)
        for k in range(tiles)
    ]
    kept = [kept[k] + kept[k + tiles // 2] for k in range(tiles // 2)]
    low = lower(kept[0].shape)
    first, middle, last = kept
    middle_turned, last_turned = turned(middle), turned(last)
    return first + jnp.where(low, middle_turned, last_turned), middle + last_turned


def lower(shape):
    return lax.broadcasted_iota(jnp.int32, shape, 1) < LANES // 2


def turned(array):
    return pltpu.roll(array, LANES // 2, 1)


def fetch(pairs, sems):
    copies = [pltpu.make_async_copy(src, dst, sems.at[i]) for i, (src, dst) in enumerate(pairs)]
    for copy in copies:
        copy.start()
    return copies


def pack_kernel(amp_ref, ij_ref, cd_ref, out_ref, amp, ij, cd, sems):
    pairs, width = amp.shape[0], out_ref.shape[0] - 8
    copies = fetch([(amp_ref, amp), (ij_ref, ij), (cd_ref, cd)], sems)
    copies[1].wait()
    copies[2].wait()
    rows = column(ij[...])
    labels = cd[...].astype(F32)
    out_ref[width:, :] = jnp.broadcast_to(ij[...].astype(F32), (8, pairs))
    copies[0].wait()
    for start in range(0, pairs, LANES):
        part = slice(start, start + LANES)
        first, second = fold(amp[part, :], rows[part], labels)
        out_ref[:LANES, part] = first.T
        out_ref[LANES:width, part] = second.T[:width - LANES]


def row_labels(rows):
    tile = rows[:, -LANES:]
    return jnp.where(lower(tile.shape), turned(tile), tile)


def split(array):
    high = array.astype(jnp.bfloat16)
    return high, (array - high.astype(F32)).astype(jnp.bfloat16)


def product(one, other):
    (one_high, one_low), (other_high, other_low) = split(one), split(other)

    def dot(left, right):
        return jnp.dot(left, right, preferred_element_type=F32)

    return dot(one_high, other_high) + (dot(one_high, other_low) + dot(one_low, other_high))


def narrowed(rows, slab_ref):
    width = slab_ref.shape[0] - 8
    full = product(rows[:, :width], slab_ref[:width, :])
    slab_labels, own_labels = slab_ref[width:width + 1, :], row_labels(rows)
    total = None
    for start in range(0, full.shape[1], LANES):
        part = slice(start, start + LANES)
        kept = jnp.where(own_labels == slab_labels[:, part], full[:, part], 0.0)
        total = kept if total is None else total + kept
    return total + turned(total)


def beside(one, other):
    return jnp.where(lower(one.shape), one, other)


def apart(array):
    low, other = lower(array.shape), turned(array)
    return jnp.where(low, array, other), jnp.where(low, other, array)


def halved(term):
    half = term.shape[0] // 2
    return beside(term[:half], term[half:])


def unhalved(term):
    return jnp.concatenate(apart(term), axis=0)


def odd():
    return lax.rem(lax.axis_index("blk"), 2) == 1


def first_kernel(count, v_ref, ab_ref, cd_ref, rows_ref, v, ab, cd, labels, sems):
    parts = v.shape[0] // count
    mine = lax.axis_index("red")
    places = [pl.ds(pl.multiple_of(lax.rem(mine + k, parts) * count, count), count) for k in range(parts)]
    held = [pl.ds(k * count, count) for k in range(parts)]
    copies = fetch([(ab_ref, ab), (cd_ref, cd)] + [(v_ref.at[p], v.at[h]) for p, h in zip(places, held)], sems)
    copies[0].wait()
    copies[1].wait()
    labels[...] = column(ab[...])
    cd_labels = cd[...].astype(F32)
    for copy, p, h in zip(copies[2:], places, held):
        own_labels = labels[p, :]
        copy.wait()
        leading, last = fold(v[h, :], own_labels, cd_labels)
        rows_ref[h, :LANES] = leading
        rows_ref[h, LANES:] = beside(last, own_labels)


def labels_kernel(slab_ref, out_ref):
    out_ref[...] = slab_ref[slab_ref.shape[0] - 8:, :]


def second():
    return lax.rem(lax.axis_index("blk"), 4) == 2


def own_kernel(rows_ref, own_ref, keep_ref, send_ref):
    count = keep_ref.shape[0]
    term = narrowed(rows_ref[...], own_ref)
    keep_ref[...] = term[:count]
    for k in range(1, send_ref.shape[0] + 1):
        send_ref[k - 1] = halved(term[k * count:(k + 1) * count])


def sent_kernel(rows_ref, slab_ref, out_ref):
    count = rows_ref.shape[0] - out_ref.shape[0]
    out_ref[...] = narrowed(rows_ref[count:, :], slab_ref)


def both_kernel(rows_ref, twin_ref, two_ref, out_ref, send_ref):
    parts, half = send_ref.shape[0] + 1, send_ref.shape[1]
    sent = out_ref.shape[0]
    rows = jnp.concatenate([twin_ref[2 * half:, :], rows_ref[2 * half:, :]], axis=0)
    term = narrowed(rows, two_ref)
    for k in range(1, parts):
        send_ref[k - 1] = halved(term[2 * (k - 1) * half:2 * k * half])
    out_ref[...] = term[sent:]


def pair_kernel(rows_ref, late_ref, two_term, mix_term, send_ref, third):
    parts, count = send_ref.shape[0] + 1, send_ref.shape[1]
    third[...] = mix_term[...]

    @pl.when(second())
    def _():
        third[...] = narrowed(rows_ref[count:, :], late_ref)

    both = beside(two_term[...], third[...])
    for k in range(1, parts):
        send_ref[k - 1] = both[(k - 1) * count:k * count]


def core_kernel(twin_ref, two_ref, send_ref):
    half = send_ref.shape[0] - 8
    width = two_ref.shape[0] - 8
    labels = two_ref[width:width + 1, :]
    tiles = [labels[:, start:start + LANES] for start in range(0, labels.shape[1], LANES)]
    send_ref[:half, :] = halved(narrowed(twin_ref[:2 * half, :], two_ref))
    send_ref[half:, :] = jnp.concatenate((tiles * 8)[:8], axis=0)


def keep_kernel(rows_ref, two_ref, mix_ref, late_ref, *refs):
    diagonal_in, (two_out, third_out, crossed_out) = refs[:-3], refs[-3:]
    count = two_out.shape[0]
    terms = [unhalved(ref[...]) for ref in diagonal_in]
    crossed_out[...] = sum(terms[1:], terms[0])
    two_out[...] = narrowed(rows_ref[:count, :], two_ref)

    @pl.when(second())
    def _():
        third_out[...] = narrowed(rows_ref[:count, :], late_ref)

    @pl.when(~second())
    def _():
        third_out[...] = narrowed(rows_ref[:count, :], mix_ref)


def total_kernel(*refs):
    terms, out_ref = [ref[...] for ref in refs[:-1]], refs[-1]
    out_ref[...] = sum(terms[1:], terms[0])


def finish_kernel(parts, rows_ref, own_keep, two_keep, third_keep, crossed_ref, own_labels, two_ref, mix_ref, late_ref, core_ref, *refs):
    own_in, (pair_ref, out_ref, out, sems) = refs[:parts - 1], refs[parts - 1:]
    count = own_keep.shape[0]
    width = two_ref.shape[0] - 8
    tiles = out.shape[2] // LANES
    rows = row_labels(rows_ref[:count, :])
    copies = []

    def store(m, term, labels):
        for k in range(tiles):
            out[m, :, k * LANES:(k + 1) * LANES] = jnp.where(rows == labels[k], term, 0.0)
        copies.append(pltpu.make_async_copy(out.at[m], out_ref.at[m], sems.at[m]))
        copies[-1].start()

    def of(ref, row=width):
        return [ref[row:row + 1, k * LANES:(k + 1) * LANES] for k in range(tiles)]

    def pick(here, one, other):
        return [jnp.where(here, x, y) for x, y in zip(one, other)]

    two, third = apart(pair_ref[...])
    store(0, sum([unhalved(ref[...]) for ref in own_in], own_keep[...]), of(own_labels, 0))
    store(2, two + two_keep[...], of(two_ref))
    third = third + third_keep[...]
    crossed = crossed_ref[...] + unhalved(core_ref[:count // 2, :])
    crossed_labels = [core_ref[count // 2 + k:count // 2 + k + 1, :] for k in range(tiles)]
    third_labels = pick(second(), of(late_ref), of(mix_ref))
    store(1, jnp.where(odd(), third, crossed), pick(odd(), third_labels, crossed_labels))
    store(3, jnp.where(odd(), crossed, third), pick(odd(), crossed_labels, third_labels))
    for copy in copies:
        copy.wait()


def whole(*shape):
    return jax.ShapeDtypeStruct(shape, F32)


def call(kernel, out_shape, args, flops, off=0, scratch=(), out_specs=ONCHIP):
    moved = sum(a.size * 4 for a in list(args) + out_shape)
    args = [pltpu.with_memory_space_constraint(a, pltpu.HBM) for a in args[:off]] + list(args[off:])
    return pl.pallas_call(
        kernel,
        out_shape=out_shape,
        in_specs=[OFFCHIP] * off + [ONCHIP] * (len(args) - off),
        out_specs=[out_specs] * len(out_shape),
        scratch_shapes=list(scratch),
        cost_estimate=pl.CostEstimate(flops=flops, bytes_accessed=0, transcendentals=0),
        compiler_params=pltpu.CompilerParams(vmem_limit_bytes=32 * 1024 * 1024),
    )(*args)


def body(amplitudes, integrals, cd_irrep, ab_irrep, ij_irrep):
    blocks, parts = lax.axis_size("blk"), lax.axis_size("red")
    pairs, depth = amplitudes.shape
    row_count = integrals.shape[0]
    width = depth // 4
    count = row_count // parts
    one_product = 12 * row_count * width * pairs

    def moved(array, steps):
        return lax.ppermute(array, "blk", [(i, (i + steps[i % 4]) % blocks) for i in range(blocks)])

    def exchanged(array):
        return [
            lax.ppermute(array[k - 1], "red", [(i, (i + k) % parts) for i in range(parts)])
            for k in range(1, parts)
        ]

    def after(array, *earlier):
        return lax.optimization_barrier((array, *earlier))[0]

    def staging(array, labels, copies):
        return [
            pltpu.VMEM(array.shape, F32),
            pltpu.VMEM(labels.shape, jnp.int32),
            pltpu.VMEM(cd_irrep.shape, jnp.int32),
        ], pltpu.SemaphoreType.DMA((2 + copies,))

    stage, sems = staging(amplitudes, ij_irrep, 1)
    own, = call(pack_kernel, [whole(width + 8, pairs)], (amplitudes, ij_irrep, cd_irrep),
                4 * amplitudes.size, 3, stage + [sems])
    def crossed(array, step):
        routes = [((b, r), (b ^ 1, (r + step) % parts)) for b in range(blocks) for r in range(parts)]
        return lax.ppermute(array, ("blk", "red"), [(b * parts + r, c * parts + t) for (b, r), (c, t) in routes])

    two = moved(own, (2, 2, 2, 2))
    own_labels, = call(labels_kernel, [whole(8, pairs)], (own,), 0)
    mix = moved(after(own, own_labels), (1, 3, 1, -1))
    stage, sems = staging(integrals, ab_irrep, parts)
    rows, = call(
        functools.partial(first_kernel, count), [whole(row_count, 2 * LANES)],
        (after(integrals, own_labels), ab_irrep, cd_irrep), 0, 3,
        stage + [pltpu.VMEM((row_count, LANES), F32), sems])
    twin = moved(rows, (1, -1, 1, -1))
    own_keep, own_send = call(
        own_kernel, [whole(count, LANES), whole(parts - 1, count // 2, LANES)], (rows, own), 64 * one_product)
    own_in = exchanged(own_send)
    late = moved(after(own, own_keep), (1, -1, 1, 3))
    rest = whole(row_count - count, LANES)
    mix_term, = call(sent_kernel, [rest], (rows, mix), 0)
    two_term, diagonal_send = call(
        both_kernel, [rest, whole(parts - 1, count // 2, LANES)],
        (rows, twin, after(two, mix_term, *own_in)), 0)
    diagonal_in = [crossed(diagonal_send[k - 1], k) for k in range(1, parts)]
    pair_send, = call(pair_kernel, [whole(parts - 1, count, LANES)], (rows, late, two_term, mix_term),
                      0, 0, [pltpu.VMEM(rest.shape, F32)])
    pair_in = exchanged(pair_send)
    core_send, = call(core_kernel, [whole(count // 2 + 8, LANES)], (twin, after(two, pair_send)), 0)
    core_in = moved(core_send, (1, -1, 1, -1))
    two_keep, third_keep, crossed_sum = call(
        keep_kernel, [whole(count, LANES)] * 3, (rows, after(two, pair_send), mix, late, *diagonal_in), 4 * one_product)
    pair_sum, = call(total_kernel, [whole(count, LANES)], tuple(pair_in), 0)
    out, = call(functools.partial(finish_kernel, parts), [whole(4, count, pairs)],
                (rows, own_keep, two_keep, third_keep, crossed_sum, own_labels, two, mix, late, core_in, *own_in, pair_sum),
                0, 0, [pltpu.VMEM((4, count, pairs), F32), pltpu.SemaphoreType.DMA((4,))], OFFCHIP)
    return out


def solution(mesh):
    in_specs = (P("blk", "red"), P("blk", "red"), P("red", None), P("blk", None), P("blk", None))
    out_specs = P(None, ("blk", "red"), None)
    return jax.shard_map(body, mesh=mesh, in_specs=in_specs, out_specs=out_specs, check_vma=False)
```

```python
import functools
import jax
import jax.numpy as jnp
from jax import lax
from jax.experimental import pallas as pl
from jax.experimental.pallas import tpu as pltpu
from jax.sharding import PartitionSpec as P

LANES = 128
F32 = jnp.float32
ONCHIP = pl.BlockSpec(memory_space=pltpu.VMEM)
OFFCHIP = pl.BlockSpec(memory_space=pltpu.HBM)


def column(labels):
    return jnp.broadcast_to(labels.astype(F32), (LANES, labels.shape[1])).T


def fold(rows, row_labels, cd_labels):
    tiles = rows.shape[1] // LANES
    kept = [
        jnp.where(row_labels == cd_labels[:, k * LANES:(k + 1) * LANES], rows[:, k * LANES:(k + 1) * LANES], 0.0)
        for k in range(tiles)
    ]
    kept = [kept[k] + kept[k + tiles // 2] for k in range(tiles // 2)]
    low = lower(kept[0].shape)
    first, middle, last = kept
    middle_turned, last_turned = turned(middle), turned(last)
    return first + jnp.where(low, middle_turned, last_turned), middle + last_turned


def lower(shape):
    return lax.broadcasted_iota(jnp.int32, shape, 1) < LANES // 2


def turned(array):
    return pltpu.roll(array, LANES // 2, 1)


def fetch(pairs, sems):
    copies = [pltpu.make_async_copy(src, dst, sems.at[i]) for i, (src, dst) in enumerate(pairs)]
    for copy in copies:
        copy.start()
    return copies


def pack_kernel(amp_ref, ij_ref, cd_ref, out_ref, amp, ij, cd, sems):
    pairs, width = amp.shape[0], out_ref.shape[0] - 8
    copies = fetch([(amp_ref, amp), (ij_ref, ij), (cd_ref, cd)], sems)
    copies[1].wait()
    copies[2].wait()
    rows = column(ij[...])
    labels = cd[...].astype(F32)
    out_ref[width:, :] = jnp.broadcast_to(ij[...].astype(F32), (8, pairs))
    copies[0].wait()
    for start in range(0, pairs, LANES):
        part = slice(start, start + LANES)
        first, second = fold(amp[part, :], rows[part], labels)
        out_ref[:LANES, part] = first.T
        out_ref[LANES:width, part] = second.T[:width - LANES]


def row_labels(rows):
    tile = rows[:, -LANES:]
    return jnp.where(lower(tile.shape), turned(tile), tile)


def split(array):
    high = array.astype(jnp.bfloat16)
    return high, (array - high.astype(F32)).astype(jnp.bfloat16)


def product(one, other):
    (one_high, one_low), (other_high, other_low) = split(one), split(other)

    def dot(left, right):
        return jnp.dot(left, right, preferred_element_type=F32)

    return dot(one_high, other_high) + (dot(one_high, other_low) + dot(one_low, other_high))


def narrowed(rows, slab_ref):
    width = slab_ref.shape[0] - 8
    full = product(rows[:, :width], slab_ref[:width, :])
    slab_labels, own_labels = slab_ref[width:width + 1, :], row_labels(rows)
    total = None
    for start in range(0, full.shape[1], LANES):
        part = slice(start, start + LANES)
        kept = jnp.where(own_labels == slab_labels[:, part], full[:, part], 0.0)
        total = kept if total is None else total + kept
    return total + turned(total)


def beside(one, other):
    return jnp.where(lower(one.shape), one, other)


def apart(array):
    low, other = lower(array.shape), turned(array)
    return jnp.where(low, array, other), jnp.where(low, other, array)


def halved(term):
    half = term.shape[0] // 2
    return beside(term[:half], term[half:])


def unhalved(term):
    return jnp.concatenate(apart(term), axis=0)


def odd():
    return lax.rem(lax.axis_index("blk"), 2) == 1


def first_kernel(count, v_ref, ab_ref, cd_ref, rows_ref, v, ab, cd, labels, sems):
    parts = v.shape[0] // count
    mine = lax.axis_index("red")
    places = [pl.ds(pl.multiple_of(lax.rem(mine + k, parts) * count, count), count) for k in range(parts)]
    held = [pl.ds(k * count, count) for k in range(parts)]
    copies = fetch([(ab_ref, ab), (cd_ref, cd)] + [(v_ref.at[p], v.at[h]) for p, h in zip(places, held)], sems)
    copies[0].wait()
    copies[1].wait()
    labels[...] = column(ab[...])
    cd_labels = cd[...].astype(F32)
    for copy, p, h in zip(copies[2:], places, held):
        own_labels = labels[p, :]
        copy.wait()
        leading, last = fold(v[h, :], own_labels, cd_labels)
        rows_ref[h, :LANES] = leading
        rows_ref[h, LANES:] = beside(last, own_labels)


def labels_kernel(slab_ref, out_ref):
    out_ref[...] = slab_ref[slab_ref.shape[0] - 8:, :]


def second():
    return lax.rem(lax.axis_index("blk"), 4) == 2


def own_kernel(rows_ref, own_ref, keep_ref, send_ref):
    count = keep_ref.shape[0]
    term = narrowed(rows_ref[...], own_ref)
    keep_ref[...] = term[:count]
    for k in range(1, send_ref.shape[0] + 1):
        send_ref[k - 1] = halved(term[k * count:(k + 1) * count])


def sent_kernel(rows_ref, slab_ref, out_ref):
    count = rows_ref.shape[0] - out_ref.shape[0]
    out_ref[...] = narrowed(rows_ref[count:, :], slab_ref)


def both_kernel(rows_ref, twin_ref, two_ref, out_ref, send_ref):
    parts, half = send_ref.shape[0] + 1, send_ref.shape[1]
    sent = out_ref.shape[0]
    rows = jnp.concatenate([twin_ref[2 * half:, :], rows_ref[2 * half:, :]], axis=0)
    term = narrowed(rows, two_ref)
    for k in range(1, parts):
        send_ref[k - 1] = halved(term[2 * (k - 1) * half:2 * k * half])
    out_ref[...] = term[sent:]


def pair_kernel(rows_ref, late_ref, two_term, mix_term, send_ref, third):
    parts, count = send_ref.shape[0] + 1, send_ref.shape[1]
    third[...] = mix_term[...]

    @pl.when(second())
    def _():
        third[...] = narrowed(rows_ref[count:, :], late_ref)

    both = beside(two_term[...], third[...])
    for k in range(1, parts):
        send_ref[k - 1] = both[(k - 1) * count:k * count]


def core_kernel(twin_ref, two_ref, send_ref):
    half = send_ref.shape[0] - 8
    width = two_ref.shape[0] - 8
    labels = two_ref[width:width + 1, :]
    tiles = [labels[:, start:start + LANES] for start in range(0, labels.shape[1], LANES)]
    send_ref[:half, :] = halved(narrowed(twin_ref[:2 * half, :], two_ref))
    send_ref[half:, :] = jnp.concatenate((tiles * 8)[:8], axis=0)


def keep_kernel(rows_ref, two_ref, mix_ref, late_ref, two_out, third_out):
    count = two_out.shape[0]
    two_out[...] = narrowed(rows_ref[:count, :], two_ref)

    @pl.when(second())
    def _():
        third_out[...] = narrowed(rows_ref[:count, :], late_ref)

    @pl.when(~second())
    def _():
        third_out[...] = narrowed(rows_ref[:count, :], mix_ref)


def halves_kernel(*refs):
    terms, out_ref = [unhalved(ref[...]) for ref in refs[:-1]], refs[-1]
    out_ref[...] = sum(terms[1:], terms[0])


def tiles_of(ref, row, tiles):
    return [ref[row:row + 1, k * LANES:(k + 1) * LANES] for k in range(tiles)]


def stored(place, plane, term, rows, labels, out_ref, out, sems):
    for k, label in enumerate(labels):
        out[plane, :, k * LANES:(k + 1) * LANES] = jnp.where(rows == label, term, 0.0)
    copy = pltpu.make_async_copy(out.at[plane], out_ref.at[place], sems.at[plane])
    copy.start()
    return copy


def early_kernel(rows_ref, own_keep, own_labels, crossed_ref, core_ref, *refs):
    own_in, (out_ref, out, sems) = refs[:-3], refs[-3:]
    count = own_keep.shape[0]
    tiles = out.shape[2] // LANES
    rows = row_labels(rows_ref[:count, :])
    own = sum([unhalved(ref[...]) for ref in own_in], own_keep[...])
    first = stored(0, 0, own, rows, tiles_of(own_labels, 0, tiles), out_ref, out, sems)
    crossed = crossed_ref[...] + unhalved(core_ref[:count // 2, :])
    labels = [core_ref[count // 2 + k:count // 2 + k + 1, :] for k in range(tiles)]
    last = stored(jnp.where(odd(), 3, 1), 1, crossed, rows, labels, out_ref, out, sems)
    first.wait()
    last.wait()


def finish_kernel(rows_ref, two_keep, third_keep, two_ref, mix_ref, late_ref, pair_ref, begun_ref, out_ref, out, sems):
    count = two_keep.shape[0]
    width = two_ref.shape[0] - 8
    tiles = out.shape[2] // LANES
    rows = row_labels(rows_ref[:count, :])
    two, third = apart(pair_ref[...])
    first = stored(2, 0, two + two_keep[...], rows, tiles_of(two_ref, width, tiles), out_ref, out, sems)
    labels = [
        jnp.where(second(), x, y) for x, y in zip(tiles_of(late_ref, width, tiles), tiles_of(mix_ref, width, tiles))
    ]
    last = stored(jnp.where(odd(), 1, 3), 1, third + third_keep[...], rows, labels, out_ref, out, sems)
    first.wait()
    last.wait()


def total_kernel(*refs):
    terms, out_ref = [ref[...] for ref in refs[:-1]], refs[-1]
    out_ref[...] = sum(terms[1:], terms[0])


def whole(*shape):
    return jax.ShapeDtypeStruct(shape, F32)


def call(kernel, out_shape, args, flops, off=0, scratch=(), out_specs=ONCHIP, onto=None):
    moved = sum(a.size * 4 for a in list(args) + out_shape)
    args = [pltpu.with_memory_space_constraint(a, pltpu.HBM) for a in args[:off]] + list(args[off:])
    return pl.pallas_call(
        kernel,
        out_shape=out_shape,
        in_specs=[OFFCHIP if i < off or i == onto else ONCHIP for i in range(len(args))],
        input_output_aliases={} if onto is None else {onto: 0},
        out_specs=[out_specs] * len(out_shape),
        scratch_shapes=list(scratch),
        cost_estimate=pl.CostEstimate(flops=flops, bytes_accessed=0, transcendentals=0),
        compiler_params=pltpu.CompilerParams(vmem_limit_bytes=32 * 1024 * 1024),
    )(*args)


def body(amplitudes, integrals, cd_irrep, ab_irrep, ij_irrep):
    blocks, parts = lax.axis_size("blk"), lax.axis_size("red")
    pairs, depth = amplitudes.shape
    row_count = integrals.shape[0]
    width = depth // 4
    count = row_count // parts
    one_product = 12 * row_count * width * pairs

    def moved(array, steps):
        return lax.ppermute(array, "blk", [(i, (i + steps[i % 4]) % blocks) for i in range(blocks)])

    def exchanged(array):
        return [
            lax.ppermute(array[k - 1], "red", [(i, (i + k) % parts) for i in range(parts)])
            for k in range(1, parts)
        ]

    def after(array, *earlier):
        return lax.optimization_barrier((array, *earlier))[0]

    def staging(array, labels, copies):
        return [
            pltpu.VMEM(array.shape, F32),
            pltpu.VMEM(labels.shape, jnp.int32),
            pltpu.VMEM(cd_irrep.shape, jnp.int32),
        ], pltpu.SemaphoreType.DMA((2 + copies,))

    stage, sems = staging(amplitudes, ij_irrep, 1)
    own, = call(pack_kernel, [whole(width + 8, pairs)], (amplitudes, ij_irrep, cd_irrep),
                4 * amplitudes.size, 3, stage + [sems])
    def crossed(array, step):
        routes = [((b, r), (b ^ 1, (r + step) % parts)) for b in range(blocks) for r in range(parts)]
        return lax.ppermute(array, ("blk", "red"), [(b * parts + r, c * parts + t) for (b, r), (c, t) in routes])

    two = moved(own, (2, 2, 2, 2))
    own_labels, = call(labels_kernel, [whole(8, pairs)], (own,), 0)
    mix = moved(after(own, own_labels), (1, 3, 1, -1))
    stage, sems = staging(integrals, ab_irrep, parts)
    rows, = call(
        functools.partial(first_kernel, count), [whole(row_count, 2 * LANES)],
        (after(integrals, own_labels), ab_irrep, cd_irrep), 0, 3,
        stage + [pltpu.VMEM((row_count, LANES), F32), sems])
    twin = moved(rows, (1, -1, 1, -1))
    own_keep, own_send = call(
        own_kernel, [whole(count, LANES), whole(parts - 1, count // 2, LANES)], (rows, own), 64 * one_product)
    own_in = exchanged(own_send)
    late = moved(after(own, own_keep), (1, -1, 1, 3))
    rest = whole(row_count - count, LANES)
    mix_term, = call(sent_kernel, [rest], (rows, mix), 0)
    two_term, diagonal_send = call(
        both_kernel, [rest, whole(parts - 1, count // 2, LANES)],
        (rows, twin, after(two, mix_term, *own_in)), 0)
    diagonal_in = [crossed(diagonal_send[k - 1], k) for k in range(1, parts)]
    pair_send, = call(pair_kernel, [whole(parts - 1, count, LANES)], (rows, late, two_term, mix_term),
                      0, 0, [pltpu.VMEM(rest.shape, F32)])
    pair_in = exchanged(pair_send)
    core_send, = call(core_kernel, [whole(count // 2 + 8, LANES)], (twin, after(two, pair_send)), 0)
    core_in = moved(core_send, (1, -1, 1, -1))
    two_keep, third_keep = call(keep_kernel, [whole(count, LANES)] * 2, (rows, after(two, pair_send), mix, late), 0)
    crossed_sum, = call(halves_kernel, [whole(count, LANES)], tuple(diagonal_in), 3 * one_product)
    stage = [pltpu.VMEM((2, count, pairs), F32), pltpu.SemaphoreType.DMA((2,))]
    begun, = call(early_kernel, [whole(4, count, pairs)],
                  (rows, own_keep, own_labels, crossed_sum, core_in, *own_in), 0, 0, stage, OFFCHIP)
    pair_sum, = call(total_kernel, [whole(count, LANES)], tuple(pair_in), 0)
    out, = call(finish_kernel, [whole(4, count, pairs)],
                (rows, two_keep, third_keep, two, mix, late, pair_sum, begun), 0, 0, stage, OFFCHIP, 7)
    return out


def solution(mesh):
    in_specs = (P("blk", "red"), P("blk", "red"), P("red", None), P("blk", None), P("blk", None))
    out_specs = P(None, ("blk", "red"), None)
    return jax.shard_map(body, mesh=mesh, in_specs=in_specs, out_specs=out_specs, check_vma=False)
```

```python
import functools
import jax
import jax.numpy as jnp
from jax import lax
from jax.experimental import pallas as pl
from jax.experimental.pallas import tpu as pltpu
from jax.sharding import PartitionSpec as P

LANES = 128
F32 = jnp.float32
ONCHIP = pl.BlockSpec(memory_space=pltpu.VMEM)
OFFCHIP = pl.BlockSpec(memory_space=pltpu.HBM)


def column(labels):
    return jnp.broadcast_to(labels.astype(F32), (LANES, labels.shape[1])).T


def fold(rows, row_labels, cd_labels):
    tiles = rows.shape[1] // LANES
    kept = [
        jnp.where(row_labels == cd_labels[:, k * LANES:(k + 1) * LANES], rows[:, k * LANES:(k + 1) * LANES], 0.0)
        for k in range(tiles)
    ]
    kept = [kept[k] + kept[k + tiles // 2] for k in range(tiles // 2)]
    low = lower(kept[0].shape)
    first, middle, last = kept
    middle_turned, last_turned = turned(middle), turned(last)
    return first + jnp.where(low, middle_turned, last_turned), middle + last_turned


def lower(shape):
    return lax.broadcasted_iota(jnp.int32, shape, 1) < LANES // 2


def turned(array):
    return pltpu.roll(array, LANES // 2, 1)


def fetch(pairs, sems):
    copies = [pltpu.make_async_copy(src, dst, sems.at[i]) for i, (src, dst) in enumerate(pairs)]
    for copy in copies:
        copy.start()
    return copies


def pack_kernel(amp_ref, ij_ref, cd_ref, out_ref, amp, ij, cd, sems):
    pairs, width = amp.shape[0], out_ref.shape[0] - 8
    copies = fetch([(amp_ref, amp), (ij_ref, ij), (cd_ref, cd)], sems)
    copies[1].wait()
    copies[2].wait()
    rows = column(ij[...])
    labels = cd[...].astype(F32)
    out_ref[width:, :] = jnp.broadcast_to(ij[...].astype(F32), (8, pairs))
    copies[0].wait()
    for start in range(0, pairs, LANES):
        part = slice(start, start + LANES)
        first, second = fold(amp[part, :], rows[part], labels)
        out_ref[:LANES, part] = first.T
        out_ref[LANES:width, part] = second.T[:width - LANES]


def row_labels(rows):
    tile = rows[:, -LANES:]
    return jnp.where(lower(tile.shape), turned(tile), tile)


def split(array):
    high = array.astype(jnp.bfloat16)
    return high, (array - high.astype(F32)).astype(jnp.bfloat16)


def product(one, other):
    (one_high, one_low), (other_high, other_low) = split(one), split(other)

    def dot(left, right):
        return jnp.dot(left, right, preferred_element_type=F32)

    return dot(one_high, other_high) + (dot(one_high, other_low) + dot(one_low, other_high))


def narrowed(rows, slab_ref):
    width = slab_ref.shape[0] - 8
    full = product(rows[:, :width], slab_ref[:width, :])
    slab_labels, own_labels = slab_ref[width:width + 1, :], row_labels(rows)
    total = None
    for start in range(0, full.shape[1], LANES):
        part = slice(start, start + LANES)
        kept = jnp.where(own_labels == slab_labels[:, part], full[:, part], 0.0)
        total = kept if total is None else total + kept
    return total + turned(total)


def beside(one, other):
    return jnp.where(lower(one.shape), one, other)


def apart(array):
    low, other = lower(array.shape), turned(array)
    return jnp.where(low, array, other), jnp.where(low, other, array)


def halved(term):
    half = term.shape[0] // 2
    return beside(term[:half], term[half:])


def unhalved(term):
    return jnp.concatenate(apart(term), axis=0)


def odd():
    return lax.rem(lax.axis_index("blk"), 2) == 1


def first_kernel(count, v_ref, ab_ref, cd_ref, rows_ref, v, ab, cd, labels, sems):
    parts = v.shape[0] // count
    mine = lax.axis_index("red")
    places = [pl.ds(pl.multiple_of(lax.rem(mine + k, parts) * count, count), count) for k in range(parts)]
    held = [pl.ds(k * count, count) for k in range(parts)]
    copies = fetch([(ab_ref, ab), (cd_ref, cd)] + [(v_ref.at[p], v.at[h]) for p, h in zip(places, held)], sems)
    copies[0].wait()
    copies[1].wait()
    labels[...] = column(ab[...])
    cd_labels = cd[...].astype(F32)
    for copy, p, h in zip(copies[2:], places, held):
        own_labels = labels[p, :]
        copy.wait()
        leading, last = fold(v[h, :], own_labels, cd_labels)
        rows_ref[h, :LANES] = leading
        rows_ref[h, LANES:] = beside(last, own_labels)


def labels_kernel(slab_ref, out_ref):
    out_ref[...] = slab_ref[slab_ref.shape[0] - 8:, :]


def second():
    return lax.rem(lax.axis_index("blk"), 4) == 2


def own_kernel(rows_ref, own_ref, keep_ref, send_ref):
    count = keep_ref.shape[0]
    term = narrowed(rows_ref[...], own_ref)
    keep_ref[...] = term[:count]
    for k in range(1, send_ref.shape[0] + 1):
        send_ref[k - 1] = halved(term[k * count:(k + 1) * count])


def sent_kernel(rows_ref, slab_ref, out_ref):
    count = rows_ref.shape[0] - out_ref.shape[0]
    out_ref[...] = narrowed(rows_ref[count:, :], slab_ref)


def both_kernel(rows_ref, twin_ref, two_ref, out_ref, send_ref):
    parts, half = send_ref.shape[0] + 1, send_ref.shape[1]
    sent = out_ref.shape[0]
    rows = jnp.concatenate([twin_ref[2 * half:, :], rows_ref[2 * half:, :]], axis=0)
    term = narrowed(rows, two_ref)
    for k in range(1, parts):
        send_ref[k - 1] = halved(term[2 * (k - 1) * half:2 * k * half])
    out_ref[...] = term[sent:]


def pair_kernel(rows_ref, late_ref, two_term, mix_term, send_ref, third):
    parts, count = send_ref.shape[0] + 1, send_ref.shape[1]
    third[...] = mix_term[...]

    @pl.when(second())
    def _():
        third[...] = narrowed(rows_ref[count:, :], late_ref)

    both = beside(two_term[...], third[...])
    for k in range(1, parts):
        send_ref[k - 1] = both[(k - 1) * count:k * count]


def core_kernel(twin_ref, two_ref, send_ref):
    half = send_ref.shape[0] - 8
    width = two_ref.shape[0] - 8
    labels = two_ref[width:width + 1, :]
    tiles = [labels[:, start:start + LANES] for start in range(0, labels.shape[1], LANES)]
    send_ref[:half, :] = halved(narrowed(twin_ref[:2 * half, :], two_ref))
    send_ref[half:, :] = jnp.concatenate((tiles * 8)[:8], axis=0)


def keep_kernel(rows_ref, two_ref, mix_ref, late_ref, two_out, third_out):
    count = two_out.shape[0]
    two_out[...] = narrowed(rows_ref[:count, :], two_ref)

    @pl.when(second())
    def _():
        third_out[...] = narrowed(rows_ref[:count, :], late_ref)

    @pl.when(~second())
    def _():
        third_out[...] = narrowed(rows_ref[:count, :], mix_ref)


def halves_kernel(*refs):
    terms, out_ref = [unhalved(ref[...]) for ref in refs[:-1]], refs[-1]
    out_ref[...] = sum(terms[1:], terms[0])


def tiles_of(ref, row, tiles):
    return [ref[row:row + 1, k * LANES:(k + 1) * LANES] for k in range(tiles)]


def stored(place, plane, term, rows, labels, out_ref, out, sems):
    for k, label in enumerate(labels):
        out[plane, :, k * LANES:(k + 1) * LANES] = jnp.where(rows == label, term, 0.0)
    copy = pltpu.make_async_copy(out.at[plane], out_ref.at[place], sems.at[plane])
    copy.start()
    return copy


def early_kernel(rows_ref, own_keep, own_labels, crossed_ref, core_ref, *refs):
    own_in, (out_ref, out, sems) = refs[:-3], refs[-3:]
    count = own_keep.shape[0]
    tiles = out.shape[2] // LANES
    rows = row_labels(rows_ref[:count, :])
    own = sum([unhalved(ref[...]) for ref in own_in], own_keep[...])
    first = stored(0, 0, own, rows, tiles_of(own_labels, 0, tiles), out_ref, out, sems)
    crossed = crossed_ref[...] + unhalved(core_ref[:count // 2, :])
    labels = [core_ref[count // 2 + k:count // 2 + k + 1, :] for k in range(tiles)]
    last = stored(jnp.where(odd(), 3, 1), 1, crossed, rows, labels, out_ref, out, sems)
    first.wait()
    last.wait()


def finish_kernel(rows_ref, two_keep, third_keep, two_ref, mix_ref, late_ref, pair_ref, begun_ref, out_ref, out, sems):
    count = two_keep.shape[0]
    width = two_ref.shape[0] - 8
    tiles = out.shape[2] // LANES
    rows = row_labels(rows_ref[:count, :])
    two, third = apart(pair_ref[...])
    first = stored(2, 0, two + two_keep[...], rows, tiles_of(two_ref, width, tiles), out_ref, out, sems)
    labels = [
        jnp.where(second(), x, y) for x, y in zip(tiles_of(late_ref, width, tiles), tiles_of(mix_ref, width, tiles))
    ]
    last = stored(jnp.where(odd(), 1, 3), 1, third + third_keep[...], rows, labels, out_ref, out, sems)
    first.wait()
    last.wait()


def total_kernel(*refs):
    terms, out_ref = [ref[...] for ref in refs[:-1]], refs[-1]
    out_ref[...] = sum(terms[1:], terms[0])


def whole(*shape):
    return jax.ShapeDtypeStruct(shape, F32)


def call(kernel, out_shape, args, flops, off=0, scratch=(), out_specs=ONCHIP, onto=None):
    moved = sum(a.size * 4 for a in list(args) + out_shape)
    args = [pltpu.with_memory_space_constraint(a, pltpu.HBM) for a in args[:off]] + list(args[off:])
    return pl.pallas_call(
        kernel,
        out_shape=out_shape,
        in_specs=[OFFCHIP if i < off or i == onto else ONCHIP for i in range(len(args))],
        input_output_aliases={} if onto is None else {onto: 0},
        out_specs=[out_specs] * len(out_shape),
        scratch_shapes=list(scratch),
        cost_estimate=pl.CostEstimate(flops=flops, bytes_accessed=0, transcendentals=0),
        compiler_params=pltpu.CompilerParams(vmem_limit_bytes=32 * 1024 * 1024),
    )(*args)


def body(amplitudes, integrals, cd_irrep, ab_irrep, ij_irrep):
    blocks, parts = lax.axis_size("blk"), lax.axis_size("red")
    pairs, depth = amplitudes.shape
    row_count = integrals.shape[0]
    width = depth // 4
    count = row_count // parts
    one_product = 12 * row_count * width * pairs

    def moved(array, steps):
        return lax.ppermute(array, "blk", [(i, (i + steps[i % 4]) % blocks) for i in range(blocks)])

    def exchanged(array):
        return [
            lax.ppermute(array[k - 1], "red", [(i, (i + k) % parts) for i in range(parts)])
            for k in range(1, parts)
        ]

    def after(array, *earlier):
        return lax.optimization_barrier((array, *earlier))[0]

    def staging(array, labels, copies):
        return [
            pltpu.VMEM(array.shape, F32),
            pltpu.VMEM(labels.shape, jnp.int32),
            pltpu.VMEM(cd_irrep.shape, jnp.int32),
        ], pltpu.SemaphoreType.DMA((2 + copies,))

    stage, sems = staging(amplitudes, ij_irrep, 1)
    own, = call(pack_kernel, [whole(width + 8, pairs)], (amplitudes, ij_irrep, cd_irrep),
                4 * amplitudes.size, 3, stage + [sems])
    def crossed(array, step):
        routes = [((b, r), (b ^ 1, (r + step) % parts)) for b in range(blocks) for r in range(parts)]
        return lax.ppermute(array, ("blk", "red"), [(b * parts + r, c * parts + t) for (b, r), (c, t) in routes])

    two = moved(own, (2, 2, 2, 2))
    own_labels, = call(labels_kernel, [whole(8, pairs)], (own,), 0)
    mix = moved(after(own, own_labels), (1, 3, 1, -1))
    stage, sems = staging(integrals, ab_irrep, parts)
    rows, = call(
        functools.partial(first_kernel, count), [whole(row_count, 2 * LANES)],
        (after(integrals, own_labels), ab_irrep, cd_irrep), 0, 3,
        stage + [pltpu.VMEM((row_count, LANES), F32), sems])
    twin = moved(rows, (1, -1, 1, -1))
    own_keep, own_send = call(
        own_kernel, [whole(count, LANES), whole(parts - 1, count // 2, LANES)], (rows, own), 64 * one_product)
    own_in = exchanged(own_send)
    late = moved(after(own, own_keep), (1, -1, 1, 3))
    rest = whole(row_count - count, LANES)
    mix_term, = call(sent_kernel, [rest], (rows, mix), 64 * one_product)
    two_term, diagonal_send = call(
        both_kernel, [rest, whole(parts - 1, count // 2, LANES)],
        (rows, twin, after(two, mix_term, *own_in)), 0)
    diagonal_in = [crossed(diagonal_send[k - 1], k) for k in range(1, parts)]
    pair_send, = call(pair_kernel, [whole(parts - 1, count, LANES)], (rows, late, two_term, mix_term),
                      0, 0, [pltpu.VMEM(rest.shape, F32)])
    pair_in = exchanged(pair_send)
    core_send, = call(core_kernel, [whole(count // 2 + 8, LANES)], (twin, after(two, pair_send)), 0)
    core_in = moved(core_send, (1, -1, 1, -1))
    two_keep, third_keep = call(keep_kernel, [whole(count, LANES)] * 2, (rows, after(two, pair_send), mix, late), 0)
    crossed_sum, = call(halves_kernel, [whole(count, LANES)], tuple(diagonal_in), 3 * one_product)
    stage = [pltpu.VMEM((2, count, pairs), F32), pltpu.SemaphoreType.DMA((2,))]
    begun, = call(early_kernel, [whole(4, count, pairs)],
                  (rows, own_keep, own_labels, crossed_sum, core_in, *own_in), 0, 0, stage, OFFCHIP)
    pair_sum, = call(total_kernel, [whole(count, LANES)], tuple(pair_in), 0)
    out, = call(finish_kernel, [whole(4, count, pairs)],
                (rows, two_keep, third_keep, two, mix, late, pair_sum, begun), 0, 0, stage, OFFCHIP, 7)
    return out


def solution(mesh):
    in_specs = (P("blk", "red"), P("blk", "red"), P("red", None), P("blk", None), P("blk", None))
    out_specs = P(None, ("blk", "red"), None)
    return jax.shard_map(body, mesh=mesh, in_specs=in_specs, out_specs=out_specs, check_vma=False)
```

```python
import functools
import jax
import jax.numpy as jnp
from jax import lax
from jax.experimental import pallas as pl
from jax.experimental.pallas import tpu as pltpu
from jax.sharding import PartitionSpec as P

LANES = 128
F32 = jnp.float32
ONCHIP = pl.BlockSpec(memory_space=pltpu.VMEM)
OFFCHIP = pl.BlockSpec(memory_space=pltpu.HBM)


def column(labels):
    return jnp.broadcast_to(labels.astype(F32), (LANES, labels.shape[1])).T


def fold(rows, row_labels, cd_labels):
    tiles = rows.shape[1] // LANES
    kept = [
        jnp.where(row_labels == cd_labels[:, k * LANES:(k + 1) * LANES], rows[:, k * LANES:(k + 1) * LANES], 0.0)
        for k in range(tiles)
    ]
    kept = [kept[k] + kept[k + tiles // 2] for k in range(tiles // 2)]
    low = lower(kept[0].shape)
    first, middle, last = kept
    middle_turned, last_turned = turned(middle), turned(last)
    return first + jnp.where(low, middle_turned, last_turned), middle + last_turned


def lower(shape):
    return lax.broadcasted_iota(jnp.int32, shape, 1) < LANES // 2


def turned(array):
    return pltpu.roll(array, LANES // 2, 1)


def fetch(pairs, sems):
    copies = [pltpu.make_async_copy(src, dst, sems.at[i]) for i, (src, dst) in enumerate(pairs)]
    for copy in copies:
        copy.start()
    return copies


def pack_kernel(amp_ref, ij_ref, cd_ref, out_ref, amp, ij, cd, sems):
    pairs, width = amp.shape[0], out_ref.shape[0] - 8
    copies = fetch([(amp_ref, amp), (ij_ref, ij), (cd_ref, cd)], sems)
    copies[1].wait()
    copies[2].wait()
    rows = column(ij[...])
    labels = cd[...].astype(F32)
    out_ref[width:, :] = jnp.broadcast_to(ij[...].astype(F32), (8, pairs))
    copies[0].wait()
    for start in range(0, pairs, LANES):
        part = slice(start, start + LANES)
        first, second = fold(amp[part, :], rows[part], labels)
        out_ref[:LANES, part] = first.T
        out_ref[LANES:width, part] = second.T[:width - LANES]


def row_labels(rows):
    tile = rows[:, -LANES:]
    return jnp.where(lower(tile.shape), turned(tile), tile)


def split(array):
    high = array.astype(jnp.bfloat16)
    return high, (array - high.astype(F32)).astype(jnp.bfloat16)


def product(one, other):
    (one_high, one_low), (other_high, other_low) = one, other

    def dot(left, right):
        return jnp.dot(left, right, preferred_element_type=F32)

    return dot(one_high, other_high) + (dot(one_high, other_low) + dot(one_low, other_high))


def narrowed(rows, slab_ref):
    width = slab_ref.shape[0] - 8
    return residual(split(rows[:, :width]), row_labels(rows), slab_ref)


def residual(rows, own_labels, slab_ref):
    width = slab_ref.shape[0] - 8
    full = product(rows, split(slab_ref[:width, :]))
    slab_labels = slab_ref[width:width + 1, :]
    total = None
    for start in range(0, full.shape[1], LANES):
        part = slice(start, start + LANES)
        kept = jnp.where(own_labels == slab_labels[:, part], full[:, part], 0.0)
        total = kept if total is None else total + kept
    return total + turned(total)


def beside(one, other):
    return jnp.where(lower(one.shape), one, other)


def apart(array):
    low, other = lower(array.shape), turned(array)
    return jnp.where(low, array, other), jnp.where(low, other, array)


def halved(term):
    half = term.shape[0] // 2
    return beside(term[:half], term[half:])


def unhalved(term):
    return jnp.concatenate(apart(term), axis=0)


def odd():
    return lax.rem(lax.axis_index("blk"), 2) == 1


def first_kernel(count, v_ref, ab_ref, cd_ref, rows_ref, v, ab, cd, labels, sems):
    parts = v.shape[0] // count
    mine = lax.axis_index("red")
    places = [pl.ds(pl.multiple_of(lax.rem(mine + k, parts) * count, count), count) for k in range(parts)]
    held = [pl.ds(k * count, count) for k in range(parts)]
    copies = fetch([(ab_ref, ab), (cd_ref, cd)] + [(v_ref.at[p], v.at[h]) for p, h in zip(places, held)], sems)
    copies[0].wait()
    copies[1].wait()
    labels[...] = column(ab[...])
    cd_labels = cd[...].astype(F32)
    for copy, p, h in zip(copies[2:], places, held):
        own_labels = labels[p, :]
        copy.wait()
        leading, last = fold(v[h, :], own_labels, cd_labels)
        rows_ref[h, :LANES] = leading
        rows_ref[h, LANES:] = beside(last, own_labels)


def labels_kernel(slab_ref, out_ref):
    out_ref[...] = slab_ref[slab_ref.shape[0] - 8:, :]


def second():
    return lax.rem(lax.axis_index("blk"), 4) == 2


def own_kernel(rows_ref, own_ref, keep_ref, send_ref):
    count = keep_ref.shape[0]
    term = narrowed(rows_ref[...], own_ref)
    keep_ref[...] = term[:count]
    for k in range(1, send_ref.shape[0] + 1):
        send_ref[k - 1] = halved(term[k * count:(k + 1) * count])


def sent_kernel(rows_ref, slab_ref, out_ref):
    count = rows_ref.shape[0] - out_ref.shape[0]
    out_ref[...] = narrowed(rows_ref[count:, :], slab_ref)


def ready_kernel(count, rows_ref, twin_ref, high_ref, low_ref, labels_ref):
    width = high_ref.shape[1]
    rows = jnp.concatenate([twin_ref[count:, :], rows_ref[count:, :]], axis=0)
    high_ref[...], low_ref[...] = split(rows[:, :width])
    labels_ref[...] = row_labels(rows)


def both_kernel(high_ref, low_ref, labels_ref, two_ref, out_ref, send_ref):
    parts, half = send_ref.shape[0] + 1, send_ref.shape[1]
    sent = out_ref.shape[0]
    term = residual((high_ref[...], low_ref[...]), labels_ref[...], two_ref)
    for k in range(1, parts):
        send_ref[k - 1] = halved(term[2 * (k - 1) * half:2 * k * half])
    out_ref[...] = term[sent:]


def pair_kernel(rows_ref, late_ref, two_term, mix_term, send_ref, third):
    parts, count = send_ref.shape[0] + 1, send_ref.shape[1]
    third[...] = mix_term[...]

    @pl.when(second())
    def _():
        third[...] = narrowed(rows_ref[count:, :], late_ref)

    both = beside(two_term[...], third[...])
    for k in range(1, parts):
        send_ref[k - 1] = both[(k - 1) * count:k * count]


def core_kernel(twin_ref, two_ref, send_ref):
    half = send_ref.shape[0] - 8
    width = two_ref.shape[0] - 8
    labels = two_ref[width:width + 1, :]
    tiles = [labels[:, start:start + LANES] for start in range(0, labels.shape[1], LANES)]
    send_ref[:half, :] = halved(narrowed(twin_ref[:2 * half, :], two_ref))
    send_ref[half:, :] = jnp.concatenate((tiles * 8)[:8], axis=0)


def keep_kernel(rows_ref, two_ref, mix_ref, late_ref, two_out, third_out):
    count = two_out.shape[0]
    two_out[...] = narrowed(rows_ref[:count, :], two_ref)

    @pl.when(second())
    def _():
        third_out[...] = narrowed(rows_ref[:count, :], late_ref)

    @pl.when(~second())
    def _():
        third_out[...] = narrowed(rows_ref[:count, :], mix_ref)


def halves_kernel(*refs):
    terms, out_ref = [unhalved(ref[...]) for ref in refs[:-1]], refs[-1]
    out_ref[...] = sum(terms[1:], terms[0])


def tiles_of(ref, row, tiles):
    return [ref[row:row + 1, k * LANES:(k + 1) * LANES] for k in range(tiles)]


def stored(place, plane, term, rows, labels, out_ref, out, sems):
    for k, label in enumerate(labels):
        out[plane, :, k * LANES:(k + 1) * LANES] = jnp.where(rows == label, term, 0.0)
    copy = pltpu.make_async_copy(out.at[plane], out_ref.at[place], sems.at[plane])
    copy.start()
    return copy


def early_kernel(rows_ref, own_keep, own_labels, crossed_ref, core_ref, *refs):
    own_in, (out_ref, out, sems) = refs[:-3], refs[-3:]
    count = own_keep.shape[0]
    tiles = out.shape[2] // LANES
    rows = row_labels(rows_ref[:count, :])
    own = sum([unhalved(ref[...]) for ref in own_in], own_keep[...])
    first = stored(0, 0, own, rows, tiles_of(own_labels, 0, tiles), out_ref, out, sems)
    crossed = crossed_ref[...] + unhalved(core_ref[:count // 2, :])
    labels = [core_ref[count // 2 + k:count // 2 + k + 1, :] for k in range(tiles)]
    last = stored(jnp.where(odd(), 3, 1), 1, crossed, rows, labels, out_ref, out, sems)
    first.wait()
    last.wait()


def finish_kernel(rows_ref, two_keep, third_keep, two_ref, mix_ref, late_ref, pair_ref, begun_ref, out_ref, out, sems):
    count = two_keep.shape[0]
    width = two_ref.shape[0] - 8
    tiles = out.shape[2] // LANES
    rows = row_labels(rows_ref[:count, :])
    two, third = apart(pair_ref[...])
    labels = [
        jnp.where(second(), x, y) for x, y in zip(tiles_of(late_ref, width, tiles), tiles_of(mix_ref, width, tiles))
    ]
    place = jnp.where(odd(), 1, 0)
    for plane, term, plane_labels in (
        (place, two + two_keep[...], tiles_of(two_ref, width, tiles)), (1 - place, third + third_keep[...], labels)
    ):
        for k, label in enumerate(plane_labels):
            out[plane, :, k * LANES:(k + 1) * LANES] = jnp.where(rows == label, term, 0.0)
    copy = pltpu.make_async_copy(out, out_ref.at[pl.ds(2 - place, 2)], sems.at[0])
    copy.start()
    copy.wait()


def total_kernel(*refs):
    terms, out_ref = [ref[...] for ref in refs[:-1]], refs[-1]
    out_ref[...] = sum(terms[1:], terms[0])


def whole(*shape):
    return jax.ShapeDtypeStruct(shape, F32)


def call(kernel, out_shape, args, flops, off=0, scratch=(), out_specs=ONCHIP, onto=None):
    moved = sum(a.size * 4 for a in list(args) + out_shape)
    args = [pltpu.with_memory_space_constraint(a, pltpu.HBM) for a in args[:off]] + list(args[off:])
    return pl.pallas_call(
        kernel,
        out_shape=out_shape,
        in_specs=[OFFCHIP if i < off or i == onto else ONCHIP for i in range(len(args))],
        input_output_aliases={} if onto is None else {onto: 0},
        out_specs=[out_specs] * len(out_shape),
        scratch_shapes=list(scratch),
        cost_estimate=pl.CostEstimate(flops=flops, bytes_accessed=0, transcendentals=0),
        compiler_params=pltpu.CompilerParams(vmem_limit_bytes=32 * 1024 * 1024),
    )(*args)


def body(amplitudes, integrals, cd_irrep, ab_irrep, ij_irrep):
    blocks, parts = lax.axis_size("blk"), lax.axis_size("red")
    pairs, depth = amplitudes.shape
    row_count = integrals.shape[0]
    width = depth // 4
    count = row_count // parts
    one_product = 12 * row_count * width * pairs

    def moved(array, steps):
        return lax.ppermute(array, "blk", [(i, (i + steps[i % 4]) % blocks) for i in range(blocks)])

    def exchanged(array):
        return [
            lax.ppermute(array[k - 1], "red", [(i, (i + k) % parts) for i in range(parts)])
            for k in range(1, parts)
        ]

    def after(array, *earlier):
        return lax.optimization_barrier((array, *earlier))[0]

    def staging(array, labels, copies):
        return [
            pltpu.VMEM(array.shape, F32),
            pltpu.VMEM(labels.shape, jnp.int32),
            pltpu.VMEM(cd_irrep.shape, jnp.int32),
        ], pltpu.SemaphoreType.DMA((2 + copies,))

    stage, sems = staging(amplitudes, ij_irrep, 1)
    own, = call(pack_kernel, [whole(width + 8, pairs)], (amplitudes, ij_irrep, cd_irrep),
                4 * amplitudes.size, 3, stage + [sems])
    def crossed(array, step):
        routes = [((b, r), (b ^ 1, (r + step) % parts)) for b in range(blocks) for r in range(parts)]
        return lax.ppermute(array, ("blk", "red"), [(b * parts + r, c * parts + t) for (b, r), (c, t) in routes])

    two = moved(own, (2, 2, 2, 2))
    own_labels, = call(labels_kernel, [whole(8, pairs)], (own,), 0)
    mix = moved(after(own, own_labels), (1, 3, 1, -1))
    stage, sems = staging(integrals, ab_irrep, parts)
    rows, = call(
        functools.partial(first_kernel, count), [whole(row_count, 2 * LANES)],
        (after(integrals, own_labels), ab_irrep, cd_irrep), 0, 3,
        stage + [pltpu.VMEM((row_count, LANES), F32), sems])
    twin = moved(rows, (1, -1, 1, -1))
    own_keep, own_send = call(
        own_kernel, [whole(count, LANES), whole(parts - 1, count // 2, LANES)], (rows, own), 64 * one_product)
    own_in = exchanged(own_send)
    late = moved(after(own, own_keep), (1, -1, 1, 3))
    rest = whole(row_count - count, LANES)
    mix_term, = call(sent_kernel, [rest], (rows, mix), 0)
    sent = 2 * (row_count - count)
    ready = call(functools.partial(ready_kernel, count),
                 [jax.ShapeDtypeStruct((sent, width), jnp.bfloat16)] * 2 + [whole(sent, LANES)], (rows, twin), 0)
    two_term, diagonal_send = call(
        both_kernel, [rest, whole(parts - 1, count // 2, LANES)],
        (*ready, after(two, mix_term, *ready, *own_in)), 0)
    diagonal_in = [crossed(diagonal_send[k - 1], k) for k in range(1, parts)]
    pair_send, = call(pair_kernel, [whole(parts - 1, count, LANES)], (rows, late, two_term, mix_term),
                      0, 0, [pltpu.VMEM(rest.shape, F32)])
    pair_in = exchanged(pair_send)
    core_send, = call(core_kernel, [whole(count // 2 + 8, LANES)], (twin, after(two, pair_send)), 0)
    core_in = moved(core_send, (1, -1, 1, -1))
    two_keep, third_keep = call(keep_kernel, [whole(count, LANES)] * 2, (rows, after(two, pair_send), mix, late), 0)
    crossed_sum, = call(halves_kernel, [whole(count, LANES)], tuple(diagonal_in), 3 * one_product)
    stage = [pltpu.VMEM((2, count, pairs), F32), pltpu.SemaphoreType.DMA((2,))]
    begun, = call(early_kernel, [whole(4, count, pairs)],
                  (rows, own_keep, own_labels, crossed_sum, core_in, *own_in), 0, 0, stage, OFFCHIP)
    pair_sum, = call(total_kernel, [whole(count, LANES)], tuple(pair_in), 0)
    out, = call(finish_kernel, [whole(4, count, pairs)],
                (rows, two_keep, third_keep, two, mix, late, pair_sum, begun), 0, 0, stage, OFFCHIP, 7)
    return out


def solution(mesh):
    in_specs = (P("blk", "red"), P("blk", "red"), P("red", None), P("blk", None), P("blk", None))
    out_specs = P(None, ("blk", "red"), None)
    return jax.shard_map(body, mesh=mesh, in_specs=in_specs, out_specs=out_specs, check_vma=False)
```

```python
import functools
import jax
import jax.numpy as jnp
from jax import lax
from jax.experimental import pallas as pl
from jax.experimental.pallas import tpu as pltpu
from jax.sharding import PartitionSpec as P

LANES = 128
F32 = jnp.float32
ONCHIP = pl.BlockSpec(memory_space=pltpu.VMEM)
OFFCHIP = pl.BlockSpec(memory_space=pltpu.HBM)


def column(labels):
    return jnp.broadcast_to(labels.astype(F32), (LANES, labels.shape[1])).T


def fold(rows, row_labels, cd_labels):
    tiles = rows.shape[1] // LANES
    kept = [
        jnp.where(row_labels == cd_labels[:, k * LANES:(k + 1) * LANES], rows[:, k * LANES:(k + 1) * LANES], 0.0)
        for k in range(tiles)
    ]
    kept = [kept[k] + kept[k + tiles // 2] for k in range(tiles // 2)]
    low = lower(kept[0].shape)
    first, middle, last = kept
    middle_turned, last_turned = turned(middle), turned(last)
    return first + jnp.where(low, middle_turned, last_turned), middle + last_turned


def lower(shape):
    return lax.broadcasted_iota(jnp.int32, shape, 1) < LANES // 2


def turned(array):
    return pltpu.roll(array, LANES // 2, 1)


def fetch(pairs, sems):
    copies = [pltpu.make_async_copy(src, dst, sems.at[i]) for i, (src, dst) in enumerate(pairs)]
    for copy in copies:
        copy.start()
    return copies


def pack_kernel(amp_ref, ij_ref, cd_ref, out_ref, amp, ij, cd, sems):
    pairs, width = amp.shape[0], out_ref.shape[0] - 8
    copies = fetch([(amp_ref, amp), (ij_ref, ij), (cd_ref, cd)], sems)
    copies[1].wait()
    copies[2].wait()
    rows = column(ij[...])
    labels = cd[...].astype(F32)
    out_ref[width:, :] = jnp.broadcast_to(ij[...].astype(F32), (8, pairs))
    copies[0].wait()
    for start in range(0, pairs, LANES):
        part = slice(start, start + LANES)
        first, second = fold(amp[part, :], rows[part], labels)
        out_ref[:LANES, part] = first.T
        out_ref[LANES:width, part] = second.T[:width - LANES]


def row_labels(rows):
    tile = rows[:, -LANES:]
    return jnp.where(lower(tile.shape), turned(tile), tile)


def split(array):
    high = array.astype(jnp.bfloat16)
    return high, (array - high.astype(F32)).astype(jnp.bfloat16)


def product(one, other):
    (one_high, one_low), (other_high, other_low) = one, other

    def dot(left, right):
        return jnp.dot(left, right, preferred_element_type=F32)

    return dot(one_high, other_high) + (dot(one_high, other_low) + dot(one_low, other_high))


def narrowed(rows, slab_ref):
    width = slab_ref.shape[0] - 8
    return residual(split(rows[:, :width]), row_labels(rows), slab_ref)


def residual(rows, own_labels, slab_ref):
    width = slab_ref.shape[0] - 8
    full = product(rows, split(slab_ref[:width, :]))
    slab_labels = slab_ref[width:width + 1, :]
    total = None
    for start in range(0, full.shape[1], LANES):
        part = slice(start, start + LANES)
        kept = jnp.where(own_labels == slab_labels[:, part], full[:, part], 0.0)
        total = kept if total is None else total + kept
    return total + turned(total)


def beside(one, other):
    return jnp.where(lower(one.shape), one, other)


def apart(array):
    low, other = lower(array.shape), turned(array)
    return jnp.where(low, array, other), jnp.where(low, other, array)


def halved(term):
    half = term.shape[0] // 2
    return beside(term[:half], term[half:])


def unhalved(term):
    return jnp.concatenate(apart(term), axis=0)


def odd():
    return lax.rem(lax.axis_index("blk"), 2) == 1


def first_kernel(count, v_ref, ab_ref, cd_ref, rows_ref, v, ab, cd, labels, sems):
    parts = v.shape[0] // count
    mine = lax.axis_index("red")
    places = [pl.ds(pl.multiple_of(lax.rem(mine + k, parts) * count, count), count) for k in range(parts)]
    held = [pl.ds(k * count, count) for k in range(parts)]
    copies = fetch([(ab_ref, ab), (cd_ref, cd)] + [(v_ref.at[p], v.at[h]) for p, h in zip(places, held)], sems)
    copies[0].wait()
    copies[1].wait()
    labels[...] = column(ab[...])
    cd_labels = cd[...].astype(F32)
    for copy, p, h in zip(copies[2:], places, held):
        own_labels = labels[p, :]
        copy.wait()
        leading, last = fold(v[h, :], own_labels, cd_labels)
        rows_ref[h, :LANES] = leading
        rows_ref[h, LANES:] = beside(last, own_labels)


def labels_kernel(slab_ref, out_ref):
    out_ref[...] = slab_ref[slab_ref.shape[0] - 8:, :]


def second():
    return lax.rem(lax.axis_index("blk"), 4) == 2


def own_kernel(rows_ref, own_ref, keep_ref, send_ref):
    count = keep_ref.shape[0]
    term = narrowed(rows_ref[...], own_ref)
    keep_ref[...] = term[:count]
    for k in range(1, send_ref.shape[0] + 1):
        send_ref[k - 1] = halved(term[k * count:(k + 1) * count])


def sent_kernel(rows_ref, slab_ref, out_ref):
    count = rows_ref.shape[0] - out_ref.shape[0]
    out_ref[...] = narrowed(rows_ref[count:, :], slab_ref)


def ready_kernel(count, rows_ref, twin_ref, high_ref, low_ref, labels_ref):
    width = high_ref.shape[1]
    rows = jnp.concatenate([twin_ref[count:, :], rows_ref[count:, :]], axis=0)
    high_ref[...], low_ref[...] = split(rows[:, :width])
    labels_ref[...] = row_labels(rows)


def both_kernel(high_ref, low_ref, labels_ref, two_ref, out_ref, send_ref):
    parts, half = send_ref.shape[0] + 1, send_ref.shape[1]
    sent = out_ref.shape[0]
    term = residual((high_ref[...], low_ref[...]), labels_ref[...], two_ref)
    for k in range(1, parts):
        send_ref[k - 1] = halved(term[2 * (k - 1) * half:2 * k * half])
    out_ref[...] = term[sent:]


def pair_kernel(rows_ref, late_ref, two_term, mix_term, send_ref, third):
    parts, count = send_ref.shape[0] + 1, send_ref.shape[1]
    third[...] = mix_term[...]

    @pl.when(second())
    def _():
        third[...] = narrowed(rows_ref[count:, :], late_ref)

    both = beside(two_term[...], third[...])
    for k in range(1, parts):
        send_ref[k - 1] = both[(k - 1) * count:k * count]


def core_kernel(twin_ref, two_ref, send_ref):
    half = send_ref.shape[0] - 8
    width = two_ref.shape[0] - 8
    labels = two_ref[width:width + 1, :]
    tiles = [labels[:, start:start + LANES] for start in range(0, labels.shape[1], LANES)]
    send_ref[:half, :] = halved(narrowed(twin_ref[:2 * half, :], two_ref))
    send_ref[half:, :] = jnp.concatenate((tiles * 8)[:8], axis=0)


def keep_kernel(rows_ref, two_ref, mix_ref, late_ref, two_out, third_out):
    count = two_out.shape[0]
    two_out[...] = narrowed(rows_ref[:count, :], two_ref)

    @pl.when(second())
    def _():
        third_out[...] = narrowed(rows_ref[:count, :], late_ref)

    @pl.when(~second())
    def _():
        third_out[...] = narrowed(rows_ref[:count, :], mix_ref)


def halves_kernel(*refs):
    terms, out_ref = [unhalved(ref[...]) for ref in refs[:-1]], refs[-1]
    out_ref[...] = sum(terms[1:], terms[0])


def tiles_of(ref, row, tiles):
    return [ref[row:row + 1, k * LANES:(k + 1) * LANES] for k in range(tiles)]


def stored(place, plane, term, rows, labels, out_ref, out, sems):
    for k, label in enumerate(labels):
        out[plane, :, k * LANES:(k + 1) * LANES] = jnp.where(rows == label, term, 0.0)
    copy = pltpu.make_async_copy(out.at[plane], out_ref.at[place], sems.at[plane])
    copy.start()
    return copy


def early_kernel(rows_ref, own_keep, own_labels, crossed_ref, core_ref, *refs):
    own_in, (out_ref, out, sems) = refs[:-3], refs[-3:]
    count = own_keep.shape[0]
    tiles = out.shape[2] // LANES
    rows = row_labels(rows_ref[:count, :])
    own = sum([unhalved(ref[...]) for ref in own_in], own_keep[...])
    first = stored(0, 0, own, rows, tiles_of(own_labels, 0, tiles), out_ref, out, sems)
    crossed = crossed_ref[...] + unhalved(core_ref[:count // 2, :])
    labels = [core_ref[count // 2 + k:count // 2 + k + 1, :] for k in range(tiles)]
    last = stored(jnp.where(odd(), 3, 1), 1, crossed, rows, labels, out_ref, out, sems)
    first.wait()
    last.wait()


def finish_kernel(rows_ref, two_keep, third_keep, two_ref, mix_ref, late_ref, pair_ref, begun_ref, out_ref, out, sems):
    count = two_keep.shape[0]
    width = two_ref.shape[0] - 8
    tiles = out.shape[2] // LANES
    rows = row_labels(rows_ref[:count, :])
    two, third = apart(pair_ref[...])
    labels = [
        jnp.where(second(), x, y) for x, y in zip(tiles_of(late_ref, width, tiles), tiles_of(mix_ref, width, tiles))
    ]
    place = jnp.where(odd(), 1, 0)
    for plane, term, plane_labels in (
        (place, two + two_keep[...], tiles_of(two_ref, width, tiles)), (1 - place, third + third_keep[...], labels)
    ):
        for k, label in enumerate(plane_labels):
            out[plane, :, k * LANES:(k + 1) * LANES] = jnp.where(rows == label, term, 0.0)
    copy = pltpu.make_async_copy(out, out_ref.at[pl.ds(2 - place, 2)], sems.at[0])
    copy.start()
    copy.wait()


def total_kernel(*refs):
    terms, out_ref = [ref[...] for ref in refs[:-1]], refs[-1]
    out_ref[...] = sum(terms[1:], terms[0])


def whole(*shape):
    return jax.ShapeDtypeStruct(shape, F32)


def call(kernel, out_shape, args, flops, off=0, scratch=(), out_specs=ONCHIP, onto=None):
    moved = sum(a.size * 4 for a in list(args) + out_shape)
    args = [pltpu.with_memory_space_constraint(a, pltpu.HBM) for a in args[:off]] + list(args[off:])
    return pl.pallas_call(
        kernel,
        out_shape=out_shape,
        in_specs=[OFFCHIP if i < off or i == onto else ONCHIP for i in range(len(args))],
        input_output_aliases={} if onto is None else {onto: 0},
        out_specs=[out_specs] * len(out_shape),
        scratch_shapes=list(scratch),
        cost_estimate=pl.CostEstimate(flops=flops, bytes_accessed=0, transcendentals=0),
        compiler_params=pltpu.CompilerParams(vmem_limit_bytes=32 * 1024 * 1024),
    )(*args)


def body(amplitudes, integrals, cd_irrep, ab_irrep, ij_irrep):
    blocks, parts = lax.axis_size("blk"), lax.axis_size("red")
    pairs, depth = amplitudes.shape
    row_count = integrals.shape[0]
    width = depth // 4
    count = row_count // parts
    one_product = 12 * row_count * width * pairs

    def moved(array, steps):
        return lax.ppermute(array, "blk", [(i, (i + steps[i % 4]) % blocks) for i in range(blocks)])

    def exchanged(array):
        return [
            lax.ppermute(array[k - 1], "red", [(i, (i + k) % parts) for i in range(parts)])
            for k in range(1, parts)
        ]

    def after(array, *earlier):
        return lax.optimization_barrier((array, *earlier))[0]

    def staging(array, labels, copies):
        return [
            pltpu.VMEM(array.shape, F32),
            pltpu.VMEM(labels.shape, jnp.int32),
            pltpu.VMEM(cd_irrep.shape, jnp.int32),
        ], pltpu.SemaphoreType.DMA((2 + copies,))

    stage, sems = staging(amplitudes, ij_irrep, 1)
    own, = call(pack_kernel, [whole(width + 8, pairs)], (amplitudes, ij_irrep, cd_irrep),
                4 * amplitudes.size, 3, stage + [sems])
    def crossed(array, step):
        routes = [((b, r), (b ^ 1, (r + step) % parts)) for b in range(blocks) for r in range(parts)]
        return lax.ppermute(array, ("blk", "red"), [(b * parts + r, c * parts + t) for (b, r), (c, t) in routes])

    two = moved(own, (2, 2, 2, 2))
    own_labels, = call(labels_kernel, [whole(8, pairs)], (own,), 0)
    mix = moved(after(own, own_labels), (1, 3, 1, -1))
    stage, sems = staging(integrals, ab_irrep, parts)
    rows, = call(
        functools.partial(first_kernel, count), [whole(row_count, 2 * LANES)],
        (after(integrals, own_labels), ab_irrep, cd_irrep), 0, 3,
        stage + [pltpu.VMEM((row_count, LANES), F32), sems])
    twin = moved(rows, (1, -1, 1, -1))
    own_keep, own_send = call(
        own_kernel, [whole(count, LANES), whole(parts - 1, count // 2, LANES)], (rows, own), 64 * one_product)
    own_in = exchanged(own_send)
    late = moved(after(own, own_keep, twin), (1, -1, 1, 3))
    rest = whole(row_count - count, LANES)
    mix_term, = call(sent_kernel, [rest], (rows, mix), 0)
    sent = 2 * (row_count - count)
    ready = call(functools.partial(ready_kernel, count),
                 [jax.ShapeDtypeStruct((sent, width), jnp.bfloat16)] * 2 + [whole(sent, LANES)], (rows, twin), 0)
    two_term, diagonal_send = call(
        both_kernel, [rest, whole(parts - 1, count // 2, LANES)],
        (*ready, after(two, mix_term, *ready, *own_in)), 0)
    diagonal_in = [crossed(diagonal_send[k - 1], k) for k in range(1, parts)]
    pair_send, = call(pair_kernel, [whole(parts - 1, count, LANES)], (rows, late, two_term, mix_term),
                      0, 0, [pltpu.VMEM(rest.shape, F32)])
    pair_in = exchanged(pair_send)
    core_send, = call(core_kernel, [whole(count // 2 + 8, LANES)], (twin, after(two, pair_send)), 0)
    core_in = moved(core_send, (1, -1, 1, -1))
    two_keep, third_keep = call(keep_kernel, [whole(count, LANES)] * 2, (rows, after(two, pair_send), mix, late), 0)
    crossed_sum, = call(halves_kernel, [whole(count, LANES)], tuple(diagonal_in), 3 * one_product)
    stage = [pltpu.VMEM((2, count, pairs), F32), pltpu.SemaphoreType.DMA((2,))]
    begun, = call(early_kernel, [whole(4, count, pairs)],
                  (rows, own_keep, own_labels, crossed_sum, core_in, *own_in), 0, 0, stage, OFFCHIP)
    pair_sum, = call(total_kernel, [whole(count, LANES)], tuple(pair_in), 0)
    out, = call(finish_kernel, [whole(4, count, pairs)],
                (rows, two_keep, third_keep, two, mix, late, pair_sum, begun), 0, 0, stage, OFFCHIP, 7)
    return out


def solution(mesh):
    in_specs = (P("blk", "red"), P("blk", "red"), P("red", None), P("blk", None), P("blk", None))
    out_specs = P(None, ("blk", "red"), None)
    return jax.shard_map(body, mesh=mesh, in_specs=in_specs, out_specs=out_specs, check_vma=False)
```

```python
import functools
import jax
import jax.numpy as jnp
from jax import lax
from jax.experimental import pallas as pl
from jax.experimental.pallas import tpu as pltpu
from jax.sharding import PartitionSpec as P

LANES = 128
F32 = jnp.float32
ONCHIP = pl.BlockSpec(memory_space=pltpu.VMEM)
OFFCHIP = pl.BlockSpec(memory_space=pltpu.HBM)


def column(labels):
    return jnp.broadcast_to(labels.astype(F32), (LANES, labels.shape[1])).T


def fold(rows, row_labels, cd_labels):
    tiles = rows.shape[1] // LANES
    kept = [
        jnp.where(row_labels == cd_labels[:, k * LANES:(k + 1) * LANES], rows[:, k * LANES:(k + 1) * LANES], 0.0)
        for k in range(tiles)
    ]
    kept = [kept[k] + kept[k + tiles // 2] for k in range(tiles // 2)]
    low = lower(kept[0].shape)
    first, middle, last = kept
    middle_turned, last_turned = turned(middle), turned(last)
    return first + jnp.where(low, middle_turned, last_turned), middle + last_turned


def lower(shape):
    return lax.broadcasted_iota(jnp.int32, shape, 1) < LANES // 2


def turned(array):
    return pltpu.roll(array, LANES // 2, 1)


def fetch(pairs, sems):
    copies = [pltpu.make_async_copy(src, dst, sems.at[i]) for i, (src, dst) in enumerate(pairs)]
    for copy in copies:
        copy.start()
    return copies


def pack_kernel(amp_ref, ij_ref, cd_ref, out_ref, amp, ij, cd, sems):
    pairs, width = amp.shape[0], out_ref.shape[0] - 8
    copies = fetch([(amp_ref, amp), (ij_ref, ij), (cd_ref, cd)], sems)
    copies[1].wait()
    copies[2].wait()
    rows = column(ij[...])
    labels = cd[...].astype(F32)
    out_ref[width:, :] = jnp.broadcast_to(ij[...].astype(F32), (8, pairs))
    copies[0].wait()
    for start in range(0, pairs, LANES):
        part = slice(start, start + LANES)
        first, second = fold(amp[part, :], rows[part], labels)
        out_ref[:LANES, part] = first.T
        out_ref[LANES:width, part] = second.T[:width - LANES]


def row_labels(rows):
    tile = rows[:, -LANES:]
    return jnp.where(lower(tile.shape), turned(tile), tile)


def split(array):
    high = array.astype(jnp.bfloat16)
    return high, (array - high.astype(F32)).astype(jnp.bfloat16)


def product(one, other):
    (one_high, one_low), (other_high, other_low) = one, other

    def dot(left, right):
        return jnp.dot(left, right, preferred_element_type=F32)

    return dot(one_high, other_high) + (dot(one_high, other_low) + dot(one_low, other_high))


def narrowed(rows, slab_ref):
    width = slab_ref.shape[0] - 8
    return residual(split(rows[:, :width]), row_labels(rows), slab_ref)


def residual(rows, own_labels, slab_ref):
    width = slab_ref.shape[0] - 8
    full = product(rows, split(slab_ref[:width, :]))
    slab_labels = slab_ref[width:width + 1, :]
    total = None
    for start in range(0, full.shape[1], LANES):
        part = slice(start, start + LANES)
        kept = jnp.where(own_labels == slab_labels[:, part], full[:, part], 0.0)
        total = kept if total is None else total + kept
    return total + turned(total)


def beside(one, other):
    return jnp.where(lower(one.shape), one, other)


def apart(array):
    low, other = lower(array.shape), turned(array)
    return jnp.where(low, array, other), jnp.where(low, other, array)


def halved(term):
    half = term.shape[0] // 2
    return beside(term[:half], term[half:])


def unhalved(term):
    return jnp.concatenate(apart(term), axis=0)


def odd():
    return lax.rem(lax.axis_index("blk"), 2) == 1


def first_kernel(count, v_ref, ab_ref, cd_ref, rows_ref, v, ab, cd, labels, sems):
    parts = v.shape[0] // count
    mine = lax.axis_index("red")
    places = [pl.ds(pl.multiple_of(lax.rem(mine + k, parts) * count, count), count) for k in range(parts)]
    held = [pl.ds(k * count, count) for k in range(parts)]
    copies = fetch([(ab_ref, ab), (cd_ref, cd)] + [(v_ref.at[p], v.at[h]) for p, h in zip(places, held)], sems)
    copies[0].wait()
    copies[1].wait()
    labels[...] = column(ab[...])
    cd_labels = cd[...].astype(F32)
    for copy, p, h in zip(copies[2:], places, held):
        own_labels = labels[p, :]
        copy.wait()
        leading, last = fold(v[h, :], own_labels, cd_labels)
        rows_ref[h, :LANES] = leading
        rows_ref[h, LANES:] = beside(last, own_labels)


def labels_kernel(slab_ref, out_ref):
    out_ref[...] = slab_ref[slab_ref.shape[0] - 8:, :]


def second():
    return lax.rem(lax.axis_index("blk"), 4) == 2


def own_kernel(rows_ref, own_ref, keep_ref, send_ref):
    count = keep_ref.shape[0]
    term = narrowed(rows_ref[...], own_ref)
    keep_ref[...] = term[:count]
    for k in range(1, send_ref.shape[0] + 1):
        send_ref[k - 1] = halved(term[k * count:(k + 1) * count])


def sent_kernel(rows_ref, slab_ref, out_ref):
    count = rows_ref.shape[0] - out_ref.shape[0]
    out_ref[...] = narrowed(rows_ref[count:, :], slab_ref)


def ready_kernel(count, rows_ref, twin_ref, high_ref, low_ref, labels_ref):
    width = high_ref.shape[1]
    rows = jnp.concatenate([twin_ref[count:, :], rows_ref[count:, :]], axis=0)
    high_ref[...], low_ref[...] = split(rows[:, :width])
    labels_ref[...] = row_labels(rows)


def both_kernel(high_ref, low_ref, labels_ref, two_ref, out_ref, send_ref):
    parts, half = send_ref.shape[0] + 1, send_ref.shape[1]
    sent = out_ref.shape[0]
    term = residual((high_ref[...], low_ref[...]), labels_ref[...], two_ref)
    for k in range(1, parts):
        send_ref[k - 1] = halved(term[2 * (k - 1) * half:2 * k * half])
    out_ref[...] = term[sent:]


def pair_kernel(rows_ref, late_ref, two_term, mix_term, send_ref, third):
    parts, count = send_ref.shape[0] + 1, send_ref.shape[1]
    third[...] = mix_term[...]

    @pl.when(second())
    def _():
        third[...] = narrowed(rows_ref[count:, :], late_ref)

    both = beside(two_term[...], third[...])
    for k in range(1, parts):
        send_ref[k - 1] = both[(k - 1) * count:k * count]


def core_kernel(twin_ref, two_ref, send_ref):
    half = send_ref.shape[0] - 8
    width = two_ref.shape[0] - 8
    labels = two_ref[width:width + 1, :]
    tiles = [labels[:, start:start + LANES] for start in range(0, labels.shape[1], LANES)]
    send_ref[:half, :] = halved(narrowed(twin_ref[:2 * half, :], two_ref))
    send_ref[half:, :] = jnp.concatenate((tiles * 8)[:8], axis=0)


def keep_kernel(rows_ref, two_ref, mix_ref, late_ref, two_out, third_out):
    count = two_out.shape[0]
    two_out[...] = narrowed(rows_ref[:count, :], two_ref)

    @pl.when(second())
    def _():
        third_out[...] = narrowed(rows_ref[:count, :], late_ref)

    @pl.when(~second())
    def _():
        third_out[...] = narrowed(rows_ref[:count, :], mix_ref)


def halves_kernel(*refs):
    terms, out_ref = [unhalved(ref[...]) for ref in refs[:-1]], refs[-1]
    out_ref[...] = sum(terms[1:], terms[0])


def tiles_of(ref, row, tiles):
    return [ref[row:row + 1, k * LANES:(k + 1) * LANES] for k in range(tiles)]


def stored(place, plane, term, rows, labels, out_ref, out, sems):
    for k, label in enumerate(labels):
        out[plane, :, k * LANES:(k + 1) * LANES] = jnp.where(rows == label, term, 0.0)
    copy = pltpu.make_async_copy(out.at[plane], out_ref.at[place], sems.at[plane])
    copy.start()
    return copy


def early_kernel(rows_ref, own_keep, own_labels, crossed_ref, core_ref, *refs):
    own_in, (out_ref, out, sems) = refs[:-3], refs[-3:]
    count = own_keep.shape[0]
    tiles = out.shape[2] // LANES
    rows = row_labels(rows_ref[:count, :])
    own = sum([unhalved(ref[...]) for ref in own_in], own_keep[...])
    first = stored(0, 0, own, rows, tiles_of(own_labels, 0, tiles), out_ref, out, sems)
    crossed = crossed_ref[...] + unhalved(core_ref[:count // 2, :])
    labels = [core_ref[count // 2 + k:count // 2 + k + 1, :] for k in range(tiles)]
    last = stored(jnp.where(odd(), 3, 1), 1, crossed, rows, labels, out_ref, out, sems)
    first.wait()
    last.wait()


def finish_kernel(rows_ref, two_keep, third_keep, two_ref, mix_ref, late_ref, pair_ref, begun_ref, out_ref, out, sems):
    count = two_keep.shape[0]
    width = two_ref.shape[0] - 8
    tiles = out.shape[2] // LANES
    rows = row_labels(rows_ref[:count, :])
    two, third = apart(pair_ref[...])
    labels = [
        jnp.where(second(), x, y) for x, y in zip(tiles_of(late_ref, width, tiles), tiles_of(mix_ref, width, tiles))
    ]
    place = jnp.where(odd(), 1, 0)
    for plane, term, plane_labels in (
        (place, two + two_keep[...], tiles_of(two_ref, width, tiles)), (1 - place, third + third_keep[...], labels)
    ):
        for k, label in enumerate(plane_labels):
            out[plane, :, k * LANES:(k + 1) * LANES] = jnp.where(rows == label, term, 0.0)
    copy = pltpu.make_async_copy(out, out_ref.at[pl.ds(2 - place, 2)], sems.at[0])
    copy.start()
    copy.wait()


def total_kernel(*refs):
    terms, out_ref = [ref[...] for ref in refs[:-1]], refs[-1]
    out_ref[...] = sum(terms[1:], terms[0])


def whole(*shape):
    return jax.ShapeDtypeStruct(shape, F32)


def call(kernel, out_shape, args, flops, off=0, scratch=(), out_specs=ONCHIP, onto=None):
    moved = sum(a.size * 4 for a in list(args) + out_shape)
    args = [pltpu.with_memory_space_constraint(a, pltpu.HBM) for a in args[:off]] + list(args[off:])
    return pl.pallas_call(
        kernel,
        out_shape=out_shape,
        in_specs=[OFFCHIP if i < off or i == onto else ONCHIP for i in range(len(args))],
        input_output_aliases={} if onto is None else {onto: 0},
        out_specs=[out_specs] * len(out_shape),
        scratch_shapes=list(scratch),
        cost_estimate=pl.CostEstimate(flops=flops, bytes_accessed=0, transcendentals=0),
        compiler_params=pltpu.CompilerParams(vmem_limit_bytes=32 * 1024 * 1024),
    )(*args)


def body(amplitudes, integrals, cd_irrep, ab_irrep, ij_irrep):
    blocks, parts = lax.axis_size("blk"), lax.axis_size("red")
    pairs, depth = amplitudes.shape
    row_count = integrals.shape[0]
    width = depth // 4
    count = row_count // parts
    one_product = 12 * row_count * width * pairs

    def moved(array, steps):
        return lax.ppermute(array, "blk", [(i, (i + steps[i % 4]) % blocks) for i in range(blocks)])

    def exchanged(array):
        return [
            lax.ppermute(array[k - 1], "red", [(i, (i + k) % parts) for i in range(parts)])
            for k in range(1, parts)
        ]

    def after(array, *earlier):
        return lax.optimization_barrier((array, *earlier))[0]

    def staging(array, labels, copies):
        return [
            pltpu.VMEM(array.shape, F32),
            pltpu.VMEM(labels.shape, jnp.int32),
            pltpu.VMEM(cd_irrep.shape, jnp.int32),
        ], pltpu.SemaphoreType.DMA((2 + copies,))

    stage, sems = staging(amplitudes, ij_irrep, 1)
    own, = call(pack_kernel, [whole(width + 8, pairs)], (amplitudes, ij_irrep, cd_irrep),
                4 * amplitudes.size, 3, stage + [sems])
    def crossed(array, step):
        routes = [((b, r), (b ^ 1, (r + step) % parts)) for b in range(blocks) for r in range(parts)]
        return lax.ppermute(array, ("blk", "red"), [(b * parts + r, c * parts + t) for (b, r), (c, t) in routes])

    two = moved(own, (2, 2, 2, 2))
    own_labels, = call(labels_kernel, [whole(8, pairs)], (own,), 0)
    mix = moved(after(own, own_labels), (1, 3, 1, -1))
    stage, sems = staging(integrals, ab_irrep, parts)
    rows, = call(
        functools.partial(first_kernel, count), [whole(row_count, 2 * LANES)],
        (after(integrals, own_labels), ab_irrep, cd_irrep), 0, 3,
        stage + [pltpu.VMEM((row_count, LANES), F32), sems])
    twin = moved(rows, (1, -1, 1, -1))
    own_keep, own_send = call(
        own_kernel, [whole(count, LANES), whole(parts - 1, count // 2, LANES)], (rows, own), 64 * one_product)
    own_in = exchanged(own_send)
    late = moved(after(own, rows), (1, -1, 1, 3))
    rest = whole(row_count - count, LANES)
    mix_term, = call(sent_kernel, [rest], (rows, mix), 0)
    sent = 2 * (row_count - count)
    ready = call(functools.partial(ready_kernel, count),
                 [jax.ShapeDtypeStruct((sent, width), jnp.bfloat16)] * 2 + [whole(sent, LANES)], (rows, twin), 0)
    two_term, diagonal_send = call(
        both_kernel, [rest, whole(parts - 1, count // 2, LANES)],
        (*ready, after(two, mix_term, *ready, *own_in)), 0)
    diagonal_in = [crossed(diagonal_send[k - 1], k) for k in range(1, parts)]
    pair_send, = call(pair_kernel, [whole(parts - 1, count, LANES)], (rows, late, two_term, mix_term),
                      0, 0, [pltpu.VMEM(rest.shape, F32)])
    pair_in = exchanged(pair_send)
    core_send, = call(core_kernel, [whole(count // 2 + 8, LANES)], (twin, after(two, pair_send)), 0)
    core_in = moved(core_send, (1, -1, 1, -1))
    two_keep, third_keep = call(keep_kernel, [whole(count, LANES)] * 2, (rows, after(two, pair_send), mix, late), 0)
    crossed_sum, = call(halves_kernel, [whole(count, LANES)], tuple(diagonal_in), 3 * one_product)
    stage = [pltpu.VMEM((2, count, pairs), F32), pltpu.SemaphoreType.DMA((2,))]
    begun, = call(early_kernel, [whole(4, count, pairs)],
                  (rows, own_keep, own_labels, crossed_sum, core_in, *own_in), 0, 0, stage, OFFCHIP)
    pair_sum, = call(total_kernel, [whole(count, LANES)], tuple(pair_in), 0)
    out, = call(finish_kernel, [whole(4, count, pairs)],
                (rows, two_keep, third_keep, two, mix, late, pair_sum, begun), 0, 0, stage, OFFCHIP, 7)
    return out


def solution(mesh):
    in_specs = (P("blk", "red"), P("blk", "red"), P("red", None), P("blk", None), P("blk", None))
    out_specs = P(None, ("blk", "red"), None)
    return jax.shard_map(body, mesh=mesh, in_specs=in_specs, out_specs=out_specs, check_vma=False)
```

```python
import functools
import jax
import jax.numpy as jnp
from jax import lax
from jax.experimental import pallas as pl
from jax.experimental.pallas import tpu as pltpu
from jax.sharding import PartitionSpec as P

LANES = 128
F32 = jnp.float32
ONCHIP = pl.BlockSpec(memory_space=pltpu.VMEM)
OFFCHIP = pl.BlockSpec(memory_space=pltpu.HBM)


def column(labels):
    return jnp.broadcast_to(labels.astype(F32), (LANES, labels.shape[1])).T


def fold(rows, row_labels, cd_labels):
    tiles = rows.shape[1] // LANES
    kept = [
        jnp.where(row_labels == cd_labels[:, k * LANES:(k + 1) * LANES], rows[:, k * LANES:(k + 1) * LANES], 0.0)
        for k in range(tiles)
    ]
    kept = [kept[k] + kept[k + tiles // 2] for k in range(tiles // 2)]
    low = lower(kept[0].shape)
    first, middle, last = kept
    middle_turned, last_turned = turned(middle), turned(last)
    return first + jnp.where(low, middle_turned, last_turned), middle + last_turned


def lower(shape):
    return lax.broadcasted_iota(jnp.int32, shape, 1) < LANES // 2


def turned(array):
    return pltpu.roll(array, LANES // 2, 1)


def fetch(pairs, sems):
    copies = [pltpu.make_async_copy(src, dst, sems.at[i]) for i, (src, dst) in enumerate(pairs)]
    for copy in copies:
        copy.start()
    return copies


def pack_kernel(amp_ref, ij_ref, cd_ref, out_ref, amp, ij, cd, sems):
    pairs, width = amp.shape[0], out_ref.shape[0] - 8
    copies = fetch([(amp_ref, amp), (ij_ref, ij), (cd_ref, cd)], sems)
    copies[1].wait()
    copies[2].wait()
    rows = column(ij[...])
    labels = cd[...].astype(F32)
    out_ref[width:, :] = jnp.broadcast_to(ij[...].astype(F32), (8, pairs))
    copies[0].wait()
    for start in range(0, pairs, LANES):
        part = slice(start, start + LANES)
        first, second = fold(amp[part, :], rows[part], labels)
        out_ref[:LANES, part] = first.T
        out_ref[LANES:width, part] = second.T[:width - LANES]


def row_labels(rows):
    tile = rows[:, -LANES:]
    return jnp.where(lower(tile.shape), turned(tile), tile)


def split(array):
    high = array.astype(jnp.bfloat16)
    return high, (array - high.astype(F32)).astype(jnp.bfloat16)


def product(one, other):
    (one_high, one_low), (other_high, other_low) = one, other

    def dot(left, right):
        return jnp.dot(left, right, preferred_element_type=F32)

    return dot(one_high, other_high) + (dot(one_high, other_low) + dot(one_low, other_high))


def narrowed(rows, slab_ref):
    width = slab_ref.shape[0] - 8
    return residual(split(rows[:, :width]), row_labels(rows), slab_ref)


def residual(rows, own_labels, slab_ref):
    width = slab_ref.shape[0] - 8
    full = product(rows, split(slab_ref[:width, :]))
    slab_labels = slab_ref[width:width + 1, :]
    total = None
    for start in range(0, full.shape[1], LANES):
        part = slice(start, start + LANES)
        kept = jnp.where(own_labels == slab_labels[:, part], full[:, part], 0.0)
        total = kept if total is None else total + kept
    return total + turned(total)


def beside(one, other):
    return jnp.where(lower(one.shape), one, other)


def apart(array):
    low, other = lower(array.shape), turned(array)
    return jnp.where(low, array, other), jnp.where(low, other, array)


def halved(term):
    half = term.shape[0] // 2
    return beside(term[:half], term[half:])


def unhalved(term):
    return jnp.concatenate(apart(term), axis=0)


def odd():
    return lax.rem(lax.axis_index("blk"), 2) == 1


def first_kernel(count, v_ref, ab_ref, cd_ref, rows_ref, v, ab, cd, labels, sems):
    parts = v.shape[0] // count
    mine = lax.axis_index("red")
    places = [pl.ds(pl.multiple_of(lax.rem(mine + k, parts) * count, count), count) for k in range(parts)]
    held = [pl.ds(k * count, count) for k in range(parts)]
    copies = fetch([(ab_ref, ab), (cd_ref, cd)] + [(v_ref.at[p], v.at[h]) for p, h in zip(places, held)], sems)
    copies[0].wait()
    copies[1].wait()
    labels[...] = column(ab[...])
    cd_labels = cd[...].astype(F32)
    for copy, p, h in zip(copies[2:], places, held):
        own_labels = labels[p, :]
        copy.wait()
        leading, last = fold(v[h, :], own_labels, cd_labels)
        rows_ref[h, :LANES] = leading
        rows_ref[h, LANES:] = beside(last, own_labels)


def labels_kernel(slab_ref, out_ref):
    out_ref[...] = slab_ref[slab_ref.shape[0] - 8:, :]


def second():
    return lax.rem(lax.axis_index("blk"), 4) == 2


def own_kernel(rows_ref, own_ref, keep_ref, send_ref):
    count = keep_ref.shape[0]
    term = narrowed(rows_ref[...], own_ref)
    keep_ref[...] = term[:count]
    for k in range(1, send_ref.shape[0] + 1):
        send_ref[k - 1] = halved(term[k * count:(k + 1) * count])


def sent_kernel(rows_ref, slab_ref, out_ref):
    count = rows_ref.shape[0] - out_ref.shape[0]
    out_ref[...] = narrowed(rows_ref[count:, :], slab_ref)


def ready_kernel(count, rows_ref, twin_ref, high_ref, low_ref, labels_ref):
    width = high_ref.shape[1]
    rows = jnp.concatenate([twin_ref[count:, :], rows_ref[count:, :]], axis=0)
    high_ref[...], low_ref[...] = split(rows[:, :width])
    labels_ref[...] = row_labels(rows)


def both_kernel(high_ref, low_ref, labels_ref, two_ref, out_ref, send_ref):
    parts, half = send_ref.shape[0] + 1, send_ref.shape[1]
    sent = out_ref.shape[0]
    term = residual((high_ref[...], low_ref[...]), labels_ref[...], two_ref)
    for k in range(1, parts):
        send_ref[k - 1] = halved(term[2 * (k - 1) * half:2 * k * half])
    out_ref[...] = term[sent:]


def pair_kernel(rows_ref, late_ref, two_term, mix_term, send_ref, third):
    parts, count = send_ref.shape[0] + 1, send_ref.shape[1]
    third[...] = mix_term[...]

    @pl.when(second())
    def _():
        third[...] = narrowed(rows_ref[count:, :], late_ref)

    both = beside(two_term[...], third[...])
    for k in range(1, parts):
        send_ref[k - 1] = both[(k - 1) * count:k * count]


def core_kernel(twin_ref, two_ref, send_ref):
    half = send_ref.shape[0] - 8
    width = two_ref.shape[0] - 8
    labels = two_ref[width:width + 1, :]
    tiles = [labels[:, start:start + LANES] for start in range(0, labels.shape[1], LANES)]
    send_ref[:half, :] = halved(narrowed(twin_ref[:2 * half, :], two_ref))
    send_ref[half:, :] = jnp.concatenate((tiles * 8)[:8], axis=0)


def keep_kernel(rows_ref, two_ref, mix_ref, late_ref, two_out, third_out):
    count = two_out.shape[0]
    two_out[...] = narrowed(rows_ref[:count, :], two_ref)

    @pl.when(second())
    def _():
        third_out[...] = narrowed(rows_ref[:count, :], late_ref)

    @pl.when(~second())
    def _():
        third_out[...] = narrowed(rows_ref[:count, :], mix_ref)


def halves_kernel(*refs):
    terms, out_ref = [unhalved(ref[...]) for ref in refs[:-1]], refs[-1]
    out_ref[...] = sum(terms[1:], terms[0])


def tiles_of(ref, row, tiles):
    return [ref[row:row + 1, k * LANES:(k + 1) * LANES] for k in range(tiles)]


def stored(place, plane, term, rows, labels, out_ref, out, sems):
    for k, label in enumerate(labels):
        out[plane, :, k * LANES:(k + 1) * LANES] = jnp.where(rows == label, term, 0.0)
    copy = pltpu.make_async_copy(out.at[plane], out_ref.at[place], sems.at[plane])
    copy.start()
    return copy


def early_kernel(rows_ref, own_keep, own_labels, crossed_ref, core_ref, mix_ref, late_ref, *refs):
    own_in, (out_ref, column_ref, third_ref, out, sems) = refs[:-5], refs[-5:]
    count = own_keep.shape[0]
    tiles = out.shape[2] // LANES
    rows = row_labels(rows_ref[:count, :])
    own = sum([unhalved(ref[...]) for ref in own_in], own_keep[...])
    first = stored(0, 0, own, rows, tiles_of(own_labels, 0, tiles), out_ref, out, sems)
    crossed = crossed_ref[...] + unhalved(core_ref[:count // 2, :])
    labels = [core_ref[count // 2 + k:count // 2 + k + 1, :] for k in range(tiles)]
    last = stored(jnp.where(odd(), 3, 1), 1, crossed, rows, labels, out_ref, out, sems)
    width = mix_ref.shape[0] - 8
    column_ref[...] = rows
    third_ref[...] = jnp.where(second(), late_ref[width:, :], mix_ref[width:, :])
    first.wait()
    last.wait()


def finish_kernel(column_ref, two_keep, third_keep, two_ref, third_ref, pair_ref, begun_ref, out_ref, out, sems):
    count = two_keep.shape[0]
    width = two_ref.shape[0] - 8
    tiles = out.shape[2] // LANES
    rows = column_ref[...]
    two, third = apart(pair_ref[...])
    labels = tiles_of(third_ref, 0, tiles)
    place = jnp.where(odd(), 1, 0)
    for plane, term, plane_labels in (
        (place, two + two_keep[...], tiles_of(two_ref, width, tiles)), (1 - place, third + third_keep[...], labels)
    ):
        for k, label in enumerate(plane_labels):
            out[plane, :, k * LANES:(k + 1) * LANES] = jnp.where(rows == label, term, 0.0)
    copy = pltpu.make_async_copy(out, out_ref.at[pl.ds(2 - place, 2)], sems.at[0])
    copy.start()
    copy.wait()


def total_kernel(*refs):
    terms, out_ref = [ref[...] for ref in refs[:-1]], refs[-1]
    out_ref[...] = sum(terms[1:], terms[0])


def whole(*shape):
    return jax.ShapeDtypeStruct(shape, F32)


def call(kernel, out_shape, args, flops, off=0, scratch=(), out_specs=ONCHIP, onto=None):
    moved = sum(a.size * 4 for a in list(args) + out_shape)
    args = [pltpu.with_memory_space_constraint(a, pltpu.HBM) for a in args[:off]] + list(args[off:])
    return pl.pallas_call(
        kernel,
        out_shape=out_shape,
        in_specs=[OFFCHIP if i < off or i == onto else ONCHIP for i in range(len(args))],
        input_output_aliases={} if onto is None else {onto: 0},
        out_specs=[out_specs] + [ONCHIP] * (len(out_shape) - 1),
        scratch_shapes=list(scratch),
        cost_estimate=pl.CostEstimate(flops=flops, bytes_accessed=0, transcendentals=0),
        compiler_params=pltpu.CompilerParams(vmem_limit_bytes=32 * 1024 * 1024),
    )(*args)


def body(amplitudes, integrals, cd_irrep, ab_irrep, ij_irrep):
    blocks, parts = lax.axis_size("blk"), lax.axis_size("red")
    pairs, depth = amplitudes.shape
    row_count = integrals.shape[0]
    width = depth // 4
    count = row_count // parts
    one_product = 12 * row_count * width * pairs

    def moved(array, steps):
        return lax.ppermute(array, "blk", [(i, (i + steps[i % 4]) % blocks) for i in range(blocks)])

    def exchanged(array):
        return [
            lax.ppermute(array[k - 1], "red", [(i, (i + k) % parts) for i in range(parts)])
            for k in range(1, parts)
        ]

    def after(array, *earlier):
        return lax.optimization_barrier((array, *earlier))[0]

    def staging(array, labels, copies):
        return [
            pltpu.VMEM(array.shape, F32),
            pltpu.VMEM(labels.shape, jnp.int32),
            pltpu.VMEM(cd_irrep.shape, jnp.int32),
        ], pltpu.SemaphoreType.DMA((2 + copies,))

    stage, sems = staging(amplitudes, ij_irrep, 1)
    own, = call(pack_kernel, [whole(width + 8, pairs)], (amplitudes, ij_irrep, cd_irrep),
                4 * amplitudes.size, 3, stage + [sems])
    def crossed(array, step):
        routes = [((b, r), (b ^ 1, (r + step) % parts)) for b in range(blocks) for r in range(parts)]
        return lax.ppermute(array, ("blk", "red"), [(b * parts + r, c * parts + t) for (b, r), (c, t) in routes])

    two = moved(own, (2, 2, 2, 2))
    own_labels, = call(labels_kernel, [whole(8, pairs)], (own,), 0)
    mix = moved(after(own, own_labels), (1, 3, 1, -1))
    stage, sems = staging(integrals, ab_irrep, parts)
    rows, = call(
        functools.partial(first_kernel, count), [whole(row_count, 2 * LANES)],
        (after(integrals, own_labels), ab_irrep, cd_irrep), 0, 3,
        stage + [pltpu.VMEM((row_count, LANES), F32), sems])
    twin = moved(rows, (1, -1, 1, -1))
    own_keep, own_send = call(
        own_kernel, [whole(count, LANES), whole(parts - 1, count // 2, LANES)], (rows, own), 64 * one_product)
    own_in = exchanged(own_send)
    late = moved(after(own, own_keep), (1, -1, 1, 3))
    rest = whole(row_count - count, LANES)
    mix_term, = call(sent_kernel, [rest], (rows, mix), 0)
    sent = 2 * (row_count - count)
    ready = call(functools.partial(ready_kernel, count),
                 [jax.ShapeDtypeStruct((sent, width), jnp.bfloat16)] * 2 + [whole(sent, LANES)], (rows, twin), 0)
    two_term, diagonal_send = call(
        both_kernel, [rest, whole(parts - 1, count // 2, LANES)],
        (*ready, after(two, mix_term, *ready, *own_in)), 0)
    diagonal_in = [crossed(diagonal_send[k - 1], k) for k in range(1, parts)]
    pair_send, = call(pair_kernel, [whole(parts - 1, count, LANES)], (rows, late, two_term, mix_term),
                      0, 0, [pltpu.VMEM(rest.shape, F32)])
    pair_in = exchanged(pair_send)
    core_send, = call(core_kernel, [whole(count // 2 + 8, LANES)], (twin, after(two, pair_send)), 0)
    core_in = moved(core_send, (1, -1, 1, -1))
    two_keep, third_keep = call(keep_kernel, [whole(count, LANES)] * 2, (rows, after(two, pair_send), mix, late), 0)
    crossed_sum, = call(halves_kernel, [whole(count, LANES)], tuple(diagonal_in), 3 * one_product)
    stage = [pltpu.VMEM((2, count, pairs), F32), pltpu.SemaphoreType.DMA((2,))]
    begun, column_kept, third_labels = call(
                  early_kernel, [whole(4, count, pairs), whole(count, LANES), whole(8, pairs)],
                  (rows, own_keep, own_labels, crossed_sum, core_in, mix, late, *own_in), 0, 0, stage, OFFCHIP)
    pair_sum, = call(total_kernel, [whole(count, LANES)], tuple(pair_in), 0)
    out, = call(finish_kernel, [whole(4, count, pairs)],
                (column_kept, two_keep, third_keep, two, third_labels, pair_sum, begun), 0, 0, stage, OFFCHIP, 6)
    return out


def solution(mesh):
    in_specs = (P("blk", "red"), P("blk", "red"), P("red", None), P("blk", None), P("blk", None))
    out_specs = P(None, ("blk", "red"), None)
    return jax.shard_map(body, mesh=mesh, in_specs=in_specs, out_specs=out_specs, check_vma=False)
```

```python
import functools
import jax
import jax.numpy as jnp
from jax import lax
from jax.experimental import pallas as pl
from jax.experimental.pallas import tpu as pltpu
from jax.sharding import PartitionSpec as P

LANES = 128
F32 = jnp.float32
ONCHIP = pl.BlockSpec(memory_space=pltpu.VMEM)
OFFCHIP = pl.BlockSpec(memory_space=pltpu.HBM)


def column(labels):
    return jnp.broadcast_to(labels.astype(F32), (LANES, labels.shape[1])).T


def fold(rows, row_labels, cd_labels):
    tiles = rows.shape[1] // LANES
    kept = [
        jnp.where(row_labels == cd_labels[:, k * LANES:(k + 1) * LANES], rows[:, k * LANES:(k + 1) * LANES], 0.0)
        for k in range(tiles)
    ]
    kept = [kept[k] + kept[k + tiles // 2] for k in range(tiles // 2)]
    low = lower(kept[0].shape)
    first, middle, last = kept
    middle_turned, last_turned = turned(middle), turned(last)
    return first + jnp.where(low, middle_turned, last_turned), middle + last_turned


def lower(shape):
    return lax.broadcasted_iota(jnp.int32, shape, 1) < LANES // 2


def turned(array):
    return pltpu.roll(array, LANES // 2, 1)


def fetch(pairs, sems):
    copies = [pltpu.make_async_copy(src, dst, sems.at[i]) for i, (src, dst) in enumerate(pairs)]
    for copy in copies:
        copy.start()
    return copies


def pack_kernel(amp_ref, ij_ref, cd_ref, out_ref, amp, ij, cd, sems):
    pairs, width = amp.shape[0], out_ref.shape[0] - 8
    copies = fetch([(amp_ref, amp), (ij_ref, ij), (cd_ref, cd)], sems)
    copies[1].wait()
    copies[2].wait()
    rows = column(ij[...])
    labels = cd[...].astype(F32)
    out_ref[width:, :] = jnp.broadcast_to(ij[...].astype(F32), (8, pairs))
    copies[0].wait()
    for start in range(0, pairs, LANES):
        part = slice(start, start + LANES)
        first, second = fold(amp[part, :], rows[part], labels)
        out_ref[:LANES, part] = first.T
        out_ref[LANES:width, part] = second.T[:width - LANES]


def row_labels(rows):
    tile = rows[:, -LANES:]
    return jnp.where(lower(tile.shape), turned(tile), tile)


def split(array):
    high = array.astype(jnp.bfloat16)
    return high, (array - high.astype(F32)).astype(jnp.bfloat16)


def product(one, other):
    (one_high, one_low), (other_high, other_low) = one, other

    def dot(left, right):
        return jnp.dot(left, right, preferred_element_type=F32)

    return dot(one_high, other_high) + (dot(one_high, other_low) + dot(one_low, other_high))


def narrowed(rows, slab_ref):
    width = slab_ref.shape[0] - 8
    return residual(split(rows[:, :width]), row_labels(rows), slab_ref)


def residual(rows, own_labels, slab_ref):
    width = slab_ref.shape[0] - 8
    full = product(rows, split(slab_ref[:width, :]))
    slab_labels = slab_ref[width:width + 1, :]
    total = None
    for start in range(0, full.shape[1], LANES):
        part = slice(start, start + LANES)
        kept = jnp.where(own_labels == slab_labels[:, part], full[:, part], 0.0)
        total = kept if total is None else total + kept
    return total + turned(total)


def beside(one, other):
    return jnp.where(lower(one.shape), one, other)


def apart(array):
    low, other = lower(array.shape), turned(array)
    return jnp.where(low, array, other), jnp.where(low, other, array)


def halved(term):
    half = term.shape[0] // 2
    return beside(term[:half], term[half:])


def unhalved(term):
    return jnp.concatenate(apart(term), axis=0)


def odd():
    return lax.rem(lax.axis_index("blk"), 2) == 1


def first_kernel(count, v_ref, ab_ref, cd_ref, rows_ref, v, ab, cd, labels, sems):
    parts = v.shape[0] // count
    mine = lax.axis_index("red")
    places = [pl.ds(pl.multiple_of(lax.rem(mine + k, parts) * count, count), count) for k in range(parts)]
    held = [pl.ds(k * count, count) for k in range(parts)]
    copies = fetch([(ab_ref, ab), (cd_ref, cd)] + [(v_ref.at[p], v.at[h]) for p, h in zip(places, held)], sems)
    copies[0].wait()
    copies[1].wait()
    labels[...] = column(ab[...])
    cd_labels = cd[...].astype(F32)
    for copy, p, h in zip(copies[2:], places, held):
        own_labels = labels[p, :]
        copy.wait()
        leading, last = fold(v[h, :], own_labels, cd_labels)
        rows_ref[h, :LANES] = leading
        rows_ref[h, LANES:] = beside(last, own_labels)


def labels_kernel(slab_ref, out_ref):
    out_ref[...] = slab_ref[slab_ref.shape[0] - 8:, :]


def second():
    return lax.rem(lax.axis_index("blk"), 4) == 2


def own_kernel(rows_ref, own_ref, keep_ref, send_ref):
    count = keep_ref.shape[0]
    term = narrowed(rows_ref[...], own_ref)
    keep_ref[...] = term[:count]
    for k in range(1, send_ref.shape[0] + 1):
        send_ref[k - 1] = halved(term[k * count:(k + 1) * count])


def sent_kernel(rows_ref, slab_ref, out_ref):
    count = rows_ref.shape[0] - out_ref.shape[0]
    out_ref[...] = narrowed(rows_ref[count:, :], slab_ref)


def ready_kernel(count, rows_ref, twin_ref, high_ref, low_ref, labels_ref):
    width = high_ref.shape[1]
    rows = jnp.concatenate([twin_ref[count:, :], rows_ref[count:, :]], axis=0)
    high_ref[...], low_ref[...] = split(rows[:, :width])
    labels_ref[...] = row_labels(rows)


def both_kernel(high_ref, low_ref, labels_ref, two_ref, out_ref, send_ref):
    parts, half = send_ref.shape[0] + 1, send_ref.shape[1]
    sent = out_ref.shape[0]
    term = residual((high_ref[...], low_ref[...]), labels_ref[...], two_ref)
    for k in range(1, parts):
        send_ref[k - 1] = halved(term[2 * (k - 1) * half:2 * k * half])
    out_ref[...] = term[sent:]


def pair_kernel(rows_ref, late_ref, two_term, mix_term, send_ref, third):
    parts, count = send_ref.shape[0] + 1, send_ref.shape[1]
    third[...] = mix_term[...]

    @pl.when(second())
    def _():
        third[...] = narrowed(rows_ref[count:, :], late_ref)

    both = beside(two_term[...], third[...])
    for k in range(1, parts):
        send_ref[k - 1] = both[(k - 1) * count:k * count]


def core_kernel(twin_ref, two_ref, send_ref):
    half = send_ref.shape[0] - 8
    width = two_ref.shape[0] - 8
    labels = two_ref[width:width + 1, :]
    tiles = [labels[:, start:start + LANES] for start in range(0, labels.shape[1], LANES)]
    send_ref[:half, :] = halved(narrowed(twin_ref[:2 * half, :], two_ref))
    send_ref[half:, :] = jnp.concatenate((tiles * 8)[:8], axis=0)


def keep_kernel(rows_ref, two_ref, mix_ref, late_ref, two_out, third_out):
    count = two_out.shape[0]
    two_out[...] = narrowed(rows_ref[:count, :], two_ref)

    @pl.when(second())
    def _():
        third_out[...] = narrowed(rows_ref[:count, :], late_ref)

    @pl.when(~second())
    def _():
        third_out[...] = narrowed(rows_ref[:count, :], mix_ref)


def halves_kernel(*refs):
    terms, out_ref = [unhalved(ref[...]) for ref in refs[:-1]], refs[-1]
    out_ref[...] = sum(terms[1:], terms[0])


def tiles_of(ref, row, tiles):
    return [ref[row:row + 1, k * LANES:(k + 1) * LANES] for k in range(tiles)]


def stored(place, plane, term, rows, labels, out_ref, out, sems):
    for k, label in enumerate(labels):
        out[plane, :, k * LANES:(k + 1) * LANES] = jnp.where(rows == label, term, 0.0)
    copy = pltpu.make_async_copy(out.at[plane], out_ref.at[place], sems.at[plane])
    copy.start()
    return copy


def early_kernel(rows_ref, own_keep, own_labels, crossed_ref, core_ref, *refs):
    own_in, (out_ref, out, sems) = refs[:-3], refs[-3:]
    count = own_keep.shape[0]
    tiles = out.shape[2] // LANES
    rows = row_labels(rows_ref[:count, :])
    own = sum([unhalved(ref[...]) for ref in own_in], own_keep[...])
    first = stored(0, 0, own, rows, tiles_of(own_labels, 0, tiles), out_ref, out, sems)
    crossed = crossed_ref[...] + unhalved(core_ref[:count // 2, :])
    labels = [core_ref[count // 2 + k:count // 2 + k + 1, :] for k in range(tiles)]
    last = stored(jnp.where(odd(), 3, 1), 1, crossed, rows, labels, out_ref, out, sems)
    first.wait()
    last.wait()


def finish_kernel(rows_ref, two_keep, third_keep, two_ref, mix_ref, late_ref, pair_ref, begun_ref, out_ref, out, sems):
    count = two_keep.shape[0]
    width = two_ref.shape[0] - 8
    tiles = out.shape[2] // LANES
    rows = row_labels(rows_ref[:count, :])
    two, third = apart(pair_ref[...])
    labels = [
        jnp.where(second(), x, y) for x, y in zip(tiles_of(late_ref, width, tiles), tiles_of(mix_ref, width, tiles))
    ]
    place = jnp.where(odd(), 1, 0)
    for plane, term, plane_labels in (
        (place, two + two_keep[...], tiles_of(two_ref, width, tiles)), (1 - place, third + third_keep[...], labels)
    ):
        for k, label in enumerate(plane_labels):
            out[plane, :, k * LANES:(k + 1) * LANES] = jnp.where(rows == label, term, 0.0)
    copy = pltpu.make_async_copy(out, out_ref.at[pl.ds(2 - place, 2)], sems.at[0])
    copy.start()
    copy.wait()


def total_kernel(*refs):
    terms, out_ref = [ref[...] for ref in refs[:-1]], refs[-1]
    out_ref[...] = sum(terms[1:], terms[0])


def whole(*shape):
    return jax.ShapeDtypeStruct(shape, F32)


def call(kernel, out_shape, args, flops, off=0, scratch=(), out_specs=ONCHIP, onto=None):
    moved = sum(a.size * 4 for a in list(args) + out_shape)
    args = [pltpu.with_memory_space_constraint(a, pltpu.HBM) for a in args[:off]] + list(args[off:])
    return pl.pallas_call(
        kernel,
        out_shape=out_shape,
        in_specs=[OFFCHIP if i < off or i == onto else ONCHIP for i in range(len(args))],
        input_output_aliases={} if onto is None else {onto: 0},
        out_specs=[out_specs] * len(out_shape),
        scratch_shapes=list(scratch),
        cost_estimate=pl.CostEstimate(flops=flops, bytes_accessed=0, transcendentals=0),
        compiler_params=pltpu.CompilerParams(vmem_limit_bytes=32 * 1024 * 1024),
    )(*args)


def body(amplitudes, integrals, cd_irrep, ab_irrep, ij_irrep):
    blocks, parts = lax.axis_size("blk"), lax.axis_size("red")
    pairs, depth = amplitudes.shape
    row_count = integrals.shape[0]
    width = depth // 4
    count = row_count // parts
    one_product = 12 * row_count * width * pairs

    def moved(array, steps):
        return lax.ppermute(array, "blk", [(i, (i + steps[i % 4]) % blocks) for i in range(blocks)])

    def exchanged(array):
        return [
            lax.ppermute(array[k - 1], "red", [(i, (i + k) % parts) for i in range(parts)])
            for k in range(1, parts)
        ]

    def after(array, *earlier):
        return lax.optimization_barrier((array, *earlier))[0]

    def staging(array, labels, copies):
        return [
            pltpu.VMEM(array.shape, F32),
            pltpu.VMEM(labels.shape, jnp.int32),
            pltpu.VMEM(cd_irrep.shape, jnp.int32),
        ], pltpu.SemaphoreType.DMA((2 + copies,))

    stage, sems = staging(amplitudes, ij_irrep, 1)
    own, = call(pack_kernel, [whole(width + 8, pairs)], (amplitudes, ij_irrep, cd_irrep),
                4 * amplitudes.size, 3, stage + [sems])
    def crossed(array, step):
        routes = [((b, r), (b ^ 1, (r + step) % parts)) for b in range(blocks) for r in range(parts)]
        return lax.ppermute(array, ("blk", "red"), [(b * parts + r, c * parts + t) for (b, r), (c, t) in routes])

    two = moved(own, (2, 2, 2, 2))
    own_labels, = call(labels_kernel, [whole(8, pairs)], (own,), 0)
    mix = moved(after(own, own_labels), (1, 3, 1, -1))
    stage, sems = staging(integrals, ab_irrep, parts)
    rows, = call(
        functools.partial(first_kernel, count), [whole(row_count, 2 * LANES)],
        (after(integrals, own_labels), ab_irrep, cd_irrep), 0, 3,
        stage + [pltpu.VMEM((row_count, LANES), F32), sems])
    twin = moved(rows, (1, -1, 1, -1))
    own_keep, own_send = call(
        own_kernel, [whole(count, LANES), whole(parts - 1, count // 2, LANES)], (rows, own), 64 * one_product)
    own_in = exchanged(own_send)
    late = moved(after(own, own_keep), (1, -1, 1, 3))
    rest = whole(row_count - count, LANES)
    mix_term, = call(sent_kernel, [rest], (rows, mix), 0)
    sent = 2 * (row_count - count)
    ready = call(functools.partial(ready_kernel, count),
                 [jax.ShapeDtypeStruct((sent, width), jnp.bfloat16)] * 2 + [whole(sent, LANES)], (rows, twin), 0)
    two_term, diagonal_send = call(
        both_kernel, [rest, whole(parts - 1, count // 2, LANES)],
        (*ready, after(two, mix_term, *ready, *own_in)), 0)
    diagonal_in = [crossed(diagonal_send[k - 1], k) for k in range(1, parts)]
    pair_send, = call(pair_kernel, [whole(parts - 1, count, LANES)], (rows, late, two_term, mix_term),
                      0, 0, [pltpu.VMEM(rest.shape, F32)])
    pair_in = exchanged(pair_send)
    core_send, = call(core_kernel, [whole(count // 2 + 8, LANES)], (twin, after(two, pair_send)), 0)
    core_in = moved(core_send, (1, -1, 1, -1))
    two_keep, third_keep = call(keep_kernel, [whole(count, LANES)] * 2, (rows, after(two, pair_send), mix, late), 0)
    crossed_sum, = call(halves_kernel, [whole(count, LANES)], tuple(diagonal_in), 3 * one_product)
    stage = [pltpu.VMEM((2, count, pairs), F32), pltpu.SemaphoreType.DMA((2,))]
    begun, = call(early_kernel, [whole(4, count, pairs)],
                  (rows, own_keep, own_labels, crossed_sum, core_in, *own_in), 0, 0, stage, OFFCHIP)
    pair_sum = pair_in[0] if parts == 2 else call(total_kernel, [whole(count, LANES)], tuple(pair_in), 0)[0]
    out, = call(finish_kernel, [whole(4, count, pairs)],
                (rows, two_keep, third_keep, two, mix, late, pair_sum, begun), 0, 0, stage, OFFCHIP, 7)
    return out


def solution(mesh):
    in_specs = (P("blk", "red"), P("blk", "red"), P("red", None), P("blk", None), P("blk", None))
    out_specs = P(None, ("blk", "red"), None)
    return jax.shard_map(body, mesh=mesh, in_specs=in_specs, out_specs=out_specs, check_vma=False)
```
